32 devices in a mesh: fsdp: 4 (over z), ctx: 4 (over x, core), tp: 2 (over y).
Axes of the slice: x: 2, y: 2, z: 4, core: 2. Of those that a mesh axis runs over, the one named last changes fastest.
Arguments:
- hidden_in: bfloat16 [4, 3072, 1536], P('fsdp', 'ctx'), may hold values from -6 to 6
- cotangent: bfloat16 [4, 3072, 1536], P('fsdp', 'ctx'), may hold values from -6 to 6
- doc_lengths: int32 [4, 8], P('fsdp'), may hold values from 1 to 1536, 3072 in all within a row
- stripe: int32 [4, 4], P('fsdp'), may hold values from 0 to 3, each once within a row
- query_key_value_weight: bfloat16 [1536, 3072], P('fsdp', 'tp'), may hold values from -0.15625 to 0.15625
- output_weight: bfloat16 [1536, 1536], P('fsdp', 'tp'), may hold values from -0.875 to 0.875
- feedforward_weight: bfloat16 [3, 1536, 4096], P(None, 'fsdp', 'tp'), may hold values from -0.15625 to 0.15625
- gains: bfloat16 [2, 1536], P(None, 'fsdp'), may hold values from 0.099609375 to 1.8984375
Outputs:
- hidden_out: bfloat16 [4, 3072, 1536], P('fsdp', 'ctx')
- grad_in: bfloat16 [4, 3072, 1536], P('fsdp', 'ctx')
- grad_qkv: float32 [1536, 3072], P(('fsdp', 'ctx'), 'tp')
- grad_out: float32 [1536, 1536], P(('fsdp', 'ctx'), 'tp')
- grad_ffn: float32 [3, 1536, 4096], P(None, ('fsdp', 'ctx'), 'tp')
- grad_gains: float32 [2, 1536], P(None, ('fsdp', 'ctx'))
The draws below stay inside these ranges and needn't reach their ends.
Inputs may be any that keep to these rules, and one draw needn't show every extreme that they name: `stripe`: each row holds every index of ctx once. `doc_lengths`: the lengths of a sequence sum to 3072.
All inputs are finite; a program needn't handle non-finite values.
Results may differ from the reference program's by a relative error of at most 0.023.
Values may be sent and summed in bfloat16 or wider, within the bound.
No kernel may reach another device: no remote copies, remote signals or barrier semaphores. Data moves between devices by JAX's collectives and lax.ppermute only.
A program may use at most 256 MiB of HBM per device.

```python
import math
import jax
import jax.numpy as jnp
import numpy as np
from jax import lax

D = 1536
KEY_VALUE_HEADS = 8
HEAD_SIZE = 96
FF = 4096
TOK_DEV = 768
DOCS = 8
QUERY_PER_KV = 2
QKV = 3072
ATT = 1536
SLOT_LENGTH = 3072
PACKED_COUNT = 4
N_CTX = 4


def strengthened(values, stream_key, source, target, parts, factor):
    owner, partner = [(jnp.arange(values.shape[dim]) // (values.shape[dim] // parts)).reshape([-1 if axis == dim else 1 for axis in range(values.ndim)]) for dim in (source, target)]
    chosen = jax.random.permutation(stream_key, parts)[partner]
    strong = (owner == chosen) | (owner == (partner + parts // 2) % parts)
    return jnp.where(strong, factor * values, values)


def levels(stream_key, dims, split, low, top_value):
    level = 1.0
    for dim, shards_of in split:
        draws = jax.random.uniform(jax.random.fold_in(jax.random.fold_in(stream_key, 6), dim), (shards_of,), jnp.float32, low / len(split), top_value / len(split))
        level = level * jnp.repeat(jnp.exp(draws), dims[dim] // shards_of).reshape((-1,) + (1,) * (len(dims) - 1 - dim))
    return level


def length_profile(amount, total, most, lean):
    portions = [(1 << 20) // math.isqrt(rank ** lean) + 1 for rank in range(2, amount + 1)]
    surplus, given = total - most - (amount - 1), [1] * (amount - 1)
    while surplus > 0:
        candidates = [i for i in range(amount - 1) if given[i] < most]
        mass, budget = sum([portions[i] for i in candidates]), surplus
        for i in candidates:
            more = min(most - given[i], max(1, budget * portions[i] // mass), surplus)
            given[i] = given[i] + more
            surplus = surplus - more
    return np.array([most] + given)


def uneven(own_key, count, total, most, lean):
    if count == 2:
        one = jax.random.randint(own_key, (), max(1, total - most), min(most, total - 1) + 1)
        return jnp.stack([one, total - one])
    tallies = jnp.asarray(length_profile(count, total, most, lean), jnp.int32)
    pairs = (count - 1) // 2
    donor, sink = tallies[1:1 + 2 * pairs:2], tallies[2:2 + 2 * pairs:2]
    margin = jnp.minimum(donor - 1, most - sink)
    shifted = jax.random.randint(jax.random.fold_in(own_key, 1), (pairs,), 0, 1 << 20) % (margin + 1)
    tallies = tallies.at[1:1 + 2 * pairs:2].set(donor - shifted).at[2:2 + 2 * pairs:2].set(sink + shifted)
    return tallies[jax.random.permutation(jax.random.fold_in(own_key, 2), count)]


def gaussian(own_key, dims, scale, limit, cuts=(), kind=jnp.bfloat16):
    array = scale * jax.random.normal(own_key, dims, jnp.float32)
    if cuts:
        array = array * levels(own_key, dims, cuts, -0.22, 0.18)
    return jnp.clip(array, -limit, limit).astype(kind)


def heavy_noise(stream_key, extent, spread, limit, shards, heavy, held_as=jnp.bfloat16):
    drawn = spread * jax.random.normal(stream_key, extent, jnp.float32)
    if shards:
        drawn = drawn * levels(stream_key, extent, shards, -0.22, 0.18)
    return jnp.clip(strengthened(drawn, jax.random.fold_in(stream_key, 3), *heavy), -limit, limit).astype(held_as)


def setup_inputs(seed: int = 0) -> dict:
    splits = jax.random.split(jax.random.key(seed), 9)
    return {
        "hidden_in": gaussian(splits[0], (PACKED_COUNT, SLOT_LENGTH, D), 1.0, 6.0, ((0, 4), (1, 4))),
        "cotangent": heavy_noise(splits[1], (PACKED_COUNT, SLOT_LENGTH, D), 1.0, 6.0, ((0, 4), (1, 4)), (1, 2, 4, 2.0)),
        "doc_lengths": jax.vmap(lambda own: uneven(own, DOCS, SLOT_LENGTH, SLOT_LENGTH // 2, 2))(jax.random.split(splits[2], PACKED_COUNT)).reshape((PACKED_COUNT, DOCS)).astype(jnp.int32),
        "stripe": jax.vmap(lambda own: jax.random.permutation(own, N_CTX))(jax.random.split(splits[3], PACKED_COUNT)).reshape((PACKED_COUNT, N_CTX)).astype(jnp.int32),
        "query_key_value_weight": gaussian(splits[4], (D, QKV), D ** -0.5, 0.15625, ((0, 4), (1, 2))),
        "output_weight": gaussian(splits[5], (D, ATT), (ATT // 32) ** -0.5, 0.875, ((0, 4), (1, 2))),
        "feedforward_weight": gaussian(splits[6], (3, D, FF), D ** -0.5, 0.15625, ((1, 4), (2, 2))),
        "gains": jnp.clip(1.0 + 0.18 * jax.random.normal(splits[7], (2, D), jnp.float32), 0.099609375, 1.8984375).astype(jnp.bfloat16),
    }


norm_eps = 1e-05
rope_base = 100000.0
masked_score = -1e+30
highest_precision = lax.Precision.HIGHEST

@jax.custom_vjp
def low(v):
    return lax.optimization_barrier(v.astype(jnp.bfloat16)).astype(jnp.float32)

@jax.custom_vjp
def lower_precision_backward(v):
    return v

def low_keep(v):
    return (low(v), None)

def low_pass(kept, grad):
    return (grad,)

def back_keep(v):
    return (v, None)

def back_low(kept, grad):
    return (low(grad),)
low.defvjp(low_keep, low_pass)
lower_precision_backward.defvjp(back_keep, back_low)

def slot_tables(doc_lengths, stripe):
    slots = jnp.arange(SLOT_LENGTH, dtype=jnp.int32)
    owners = slots // TOK_DEV
    choose = (owners[:, None] == jnp.arange(N_CTX, dtype=jnp.int32)[None, :]).astype(jnp.int32)
    residue = lax.optimization_barrier(jnp.sum(choose[None, :, :] * stripe[:, None, :], axis=2))
    packed = (slots % TOK_DEV)[None, :] * N_CTX + residue
    ends = jnp.cumsum(doc_lengths, axis=1)
    passed = (packed[:, :, None] >= ends[:, None, :]).astype(jnp.int32)
    segment = lax.optimization_barrier(jnp.sum(passed, axis=2))
    position = packed - lax.optimization_barrier(jnp.sum(passed * doc_lengths[:, None, :], axis=2))
    return (packed, segment, position)

def rope_tables(position):
    half_width = HEAD_SIZE // 2
    frequency = rope_base ** (-(2.0 * jnp.arange(half_width, dtype=jnp.float32)) / HEAD_SIZE)
    angles = position.astype(jnp.float32)[..., None] * frequency
    return (jnp.cos(angles), jnp.sin(angles))

def rotate(vector, cos_table, sin_table):
    half_width = vector.shape[-1] // 2
    front_half = vector[..., :half_width]
    back_half = vector[..., half_width:]
    return jnp.concatenate([front_half * cos_table - back_half * sin_table, back_half * cos_table + front_half * sin_table], axis=-1)

def rms_normed(values, gain):
    scale_row = lax.rsqrt(lax.optimization_barrier(jnp.mean(values * values, axis=-1, keepdims=True)) + norm_eps)
    return values * scale_row * gain

def attention(queries, keys_all, values_all, packed, segment):
    rows_per_block = min(512, SLOT_LENGTH)
    count_of_blocks = SLOT_LENGTH // rows_per_block
    inv_scale = HEAD_SIZE ** (-0.5)

    def one_sequence(layer_input):
        sequence_query_rows, seq_keys, seq_values, sequence_packed, sequence_segment_index = layer_input

        def single_block(block_in):
            block_queries, block_packed, block_segment = block_in
            scores = jnp.einsum('qhgd,khd->hgqk', block_queries, seq_keys, precision=highest_precision) * inv_scale
            scores = lower_precision_backward(scores)
            allowed = (block_segment[:, None] == sequence_segment_index[None, :]) & (sequence_packed[None, :] <= block_packed[:, None])
            scores = jnp.where(allowed, scores, masked_score)
            row_top = lax.optimization_barrier(jnp.max(scores, axis=-1, keepdims=True))
            weights = jnp.where(allowed, jnp.exp(scores - row_top), 0.0)
            probs = low(weights / lax.optimization_barrier(jnp.sum(weights, axis=-1, keepdims=True)))
            return jnp.einsum('hgqk,khd->qhgd', probs, seq_values, precision=highest_precision)
        block_list = lax.map(jax.checkpoint(single_block), (sequence_query_rows.reshape(count_of_blocks, rows_per_block, KEY_VALUE_HEADS, QUERY_PER_KV, HEAD_SIZE), sequence_packed.reshape(count_of_blocks, rows_per_block), sequence_segment_index.reshape(count_of_blocks, rows_per_block)))
        return block_list.reshape(SLOT_LENGTH, KEY_VALUE_HEADS, QUERY_PER_KV, HEAD_SIZE)
    return lax.map(one_sequence, (queries, keys_all, values_all, packed, segment))

def layer(layer_input, query_key_value_weight, output_weight, feedforward_weight, gains, tables):
    packed, segment, cos_table, sin_table = tables
    first_normed = low(rms_normed(layer_input, gains[0]))
    output_projected = lower_precision_backward(jnp.einsum('orx,xp->orp', first_normed, query_key_value_weight, precision=highest_precision))
    output_projected = output_projected.reshape(PACKED_COUNT, SLOT_LENGTH, KEY_VALUE_HEADS, QUERY_PER_KV + 2, HEAD_SIZE)
    queries = low(rotate(output_projected[:, :, :, :QUERY_PER_KV], cos_table[:, :, None, None, :], sin_table[:, :, None, None, :]))
    keys_all = low(rotate(output_projected[:, :, :, QUERY_PER_KV], cos_table[:, :, None, :], sin_table[:, :, None, :]))
    values_all = low(output_projected[:, :, :, QUERY_PER_KV + 1])
    attention_output = attention(queries, keys_all, values_all, packed, segment)
    attention_output = low(lower_precision_backward(attention_output)).reshape(PACKED_COUNT, SLOT_LENGTH, ATT)
    residual_middle = layer_input + lower_precision_backward(jnp.einsum('ajt,et->aje', attention_output, output_weight, precision=highest_precision))
    second_normed = low(rms_normed(residual_middle, gains[1]))
    gate_branch = lower_precision_backward(jnp.einsum('obj,jx->obx', second_normed, feedforward_weight[0], precision=highest_precision))
    up_branch = lower_precision_backward(jnp.einsum('obj,jx->obx', second_normed, feedforward_weight[1], precision=highest_precision))
    silu_output = low(jax.nn.silu(gate_branch) * up_branch)
    return residual_middle + lower_precision_backward(jnp.einsum('rza,qa->rzq', silu_output, feedforward_weight[2], precision=highest_precision))

def reference(hidden_in, cotangent, doc_lengths, stripe, query_key_value_weight, output_weight, feedforward_weight, gains):
    packed, segment, position = slot_tables(doc_lengths, stripe)
    cos_table, sin_table = rope_tables(position)
    tables = (packed, segment, cos_table, sin_table)

    def forward(layer_input, weight_qkv, weight_out, weight_ffn, gain_rows):
        return layer(layer_input, weight_qkv, weight_out, weight_ffn, gain_rows, tables)
    result, pullback = jax.vjp(forward, hidden_in.astype(jnp.float32), query_key_value_weight.astype(jnp.float32), output_weight.astype(jnp.float32), feedforward_weight.astype(jnp.float32), gains.astype(jnp.float32))
    grad_inputs, grad_qkv, grad_out, grad_ffn, grad_gains = pullback(cotangent.astype(jnp.float32))
    return (result.astype(jnp.bfloat16), grad_inputs.astype(jnp.bfloat16), grad_qkv, grad_out, grad_ffn, grad_gains)
```

```python
import functools
import math

import jax
import jax.numpy as jnp
from jax import lax
from jax.experimental import pallas as pl
from jax.experimental.pallas import tpu as pltpu
from jax.sharding import PartitionSpec as P

HEAD_SIZE = 96
QUERY_PER_KV = 2
HALF = HEAD_SIZE // 2
BLOCK = 128

norm_eps = 1e-05
rope_base = 100000.0
masked_score = -1e30
SCORE_SCALE = HEAD_SIZE ** (-0.5)
SCORE_SCALE_2 = SCORE_SCALE * math.log2(math.e)

bf16 = jnp.bfloat16
f32 = jnp.float32


def mm(a, b, contract=((1,), (0,))):
    return lax.dot_general(a, b, (contract, ((), ())), preferred_element_type=f32)


def fill_keys(count, blocks, kv_refs, kn_ref, kt_ref, vn_ref, vt_ref):
    for s in range(count):
        for b in range(blocks):
            columns = slice(b * BLOCK, (b + 1) * BLOCK)
            places = slice(s * BLOCK, (s + 1) * BLOCK)
            key = kv_refs[s][0, 0, :, columns]
            value = kv_refs[s][0, 1, :, columns]
            kn_ref[b, places, :] = key.T
            if kt_ref is not None:
                kt_ref[b, :, places] = key
            if vn_ref is not None:
                vn_ref[b, places, :] = value.T
            if vt_ref is not None:
                vt_ref[b, :, places] = value


def fill_places(count, stripes_ref, place_ref):
    step = lax.broadcasted_iota(jnp.int32, (BLOCK, QUERY_PER_KV * BLOCK), 0) * count
    for s in range(count):
        place_ref[s * BLOCK : (s + 1) * BLOCK, :] = step + stripes_ref[s]


def twice(row):
    return jnp.concatenate([row] * QUERY_PER_KV, axis=1)


def block_of(ref, i):
    columns = slice(i * BLOCK, (i + 1) * BLOCK)
    return jnp.concatenate([ref[0, g, :, columns] for g in range(QUERY_PER_KV)], axis=1)


def forward_kernel(count, blocks, starts_ref, stripes_ref, place_q_ref, start_q_ref, q_ref, *rest):
    kv_refs = rest[:count]
    o_ref, lse_ref, kn_ref, vt_ref, place_ref = rest[count:]
    fill_keys(count, blocks, kv_refs, kn_ref, None, None, vt_ref)
    fill_places(count, stripes_ref, place_ref)
    for i in range(blocks):
        columns = slice(i * BLOCK, (i + 1) * BLOCK)
        query = block_of(q_ref, i)
        place_q = twice(place_q_ref[:, columns])
        start_q = twice(start_q_ref[:, columns])

        def scores_of(b):
            scores = mm(kn_ref[b], query)
            offset = b * (BLOCK * count)
            place = place_ref[...]
            allowed = (place >= start_q - offset) & (place <= place_q - offset)
            return jnp.where(allowed, scores * SCORE_SCALE_2, masked_score)

        scores = scores_of(i)
        top = jnp.max(scores, axis=0, keepdims=True)
        weights = jnp.exp2(scores - top)
        total = jnp.sum(weights, axis=0, keepdims=True)
        accum = mm(vt_ref[i], weights.astype(bf16))

        def step(b, carry):
            top, total, accum = carry
            scores = scores_of(b)
            new_top = jnp.maximum(top, jnp.max(scores, axis=0, keepdims=True))
            fade = jnp.exp2(top - new_top)
            weights = jnp.exp2(scores - new_top)
            total = total * fade + jnp.sum(weights, axis=0, keepdims=True)
            accum = accum * fade + mm(vt_ref[b], weights.astype(bf16))
            return new_top, total, accum

        top, total, accum = lax.fori_loop(starts_ref[i], i, step, (top, total, accum))
        result = (accum / total).astype(bf16)
        lse = top + jnp.log2(total)
        for g in range(QUERY_PER_KV):
            part = slice(g * BLOCK, (g + 1) * BLOCK)
            o_ref[0, g, :, columns] = result[:, part]
            lse_ref[0, g : g + 1, columns] = lse[:, part]


def backward_kernel(
    count, blocks, starts_ref, stripes_ref, place_q_ref, start_q_ref, q_ref, do_ref, o_ref, lse_ref, *rest
):
    kv_refs = rest[:count]
    dq_ref = rest[count]
    dkv_refs = rest[count + 1 : 2 * count + 1]
    kn_ref, kt_ref, vn_ref, place_ref, dk_ref, dv_ref = rest[2 * count + 1 :]
    fill_keys(count, blocks, kv_refs, kn_ref, kt_ref, vn_ref, None)
    fill_places(count, stripes_ref, place_ref)
    dk_ref[...] = jnp.zeros_like(dk_ref)
    dv_ref[...] = jnp.zeros_like(dv_ref)
    for i in range(blocks):
        columns = slice(i * BLOCK, (i + 1) * BLOCK)
        query = block_of(q_ref, i)
        d_out = block_of(do_ref, i)
        out = block_of(o_ref, i)
        query_rows = query.T
        d_out_rows = d_out.T
        delta = jnp.sum(d_out.astype(f32) * out.astype(f32), axis=0, keepdims=True)
        lse = jnp.concatenate([lse_ref[0, g : g + 1, columns] for g in range(QUERY_PER_KV)], axis=1)
        place_q = twice(place_q_ref[:, columns])
        start_q = twice(start_q_ref[:, columns])

        def step(b, d_query):
            scores = mm(kn_ref[b], query)
            offset = b * (BLOCK * count)
            place = place_ref[...]
            allowed = (place >= start_q - offset) & (place <= place_q - offset)
            probs = jnp.exp2(jnp.where(allowed, scores * SCORE_SCALE_2, masked_score) - lse)
            d_prob = mm(vn_ref[b], d_out)
            d_score = (probs * (d_prob - delta)).astype(bf16)
            dv_ref[b] += mm(probs.astype(bf16), d_out_rows)
            dk_ref[b] += mm(d_score, query_rows)
            return d_query + mm(kt_ref[b], d_score)

        d_query = lax.fori_loop(
            starts_ref[i], i + 1, step, jnp.zeros((HEAD_SIZE, QUERY_PER_KV * BLOCK), f32)
        )
        for g in range(QUERY_PER_KV):
            dq_ref[0, g, :, columns] = d_query[:, g * BLOCK : (g + 1) * BLOCK] * SCORE_SCALE
    for s in range(count):
        places = slice(s * BLOCK, (s + 1) * BLOCK)
        for b in range(blocks):
            columns = slice(b * BLOCK, (b + 1) * BLOCK)
            dkv_refs[s][0, 0, :, columns] = (dk_ref[b, places, :] * SCORE_SCALE).T.astype(bf16)
            dkv_refs[s][0, 1, :, columns] = dv_ref[b, places, :].T.astype(bf16)


def head_spec(*dims):
    return pl.BlockSpec((1, *dims), lambda h, *_: (h,) + (0,) * len(dims))


def row_spec(tokens):
    return pl.BlockSpec((1, tokens), lambda h, *_: (0, 0))


def attention_forward(queries, pieces, starts, stripes, place, start):
    heads, _, _, tokens = queries.shape
    count, blocks = len(pieces), tokens // BLOCK
    keys = count * BLOCK
    per_query = head_spec(QUERY_PER_KV, HEAD_SIZE, tokens)
    per_kv = head_spec(2, HEAD_SIZE, tokens)
    return pl.pallas_call(
        functools.partial(forward_kernel, count, blocks),
        grid_spec=pltpu.PrefetchScalarGridSpec(
            num_scalar_prefetch=2,
            grid=(heads,),
            in_specs=[row_spec(tokens)] * 2 + [per_query] + [per_kv] * count,
            out_specs=[per_query, head_spec(QUERY_PER_KV, tokens)],
            scratch_shapes=[
                pltpu.VMEM((blocks, keys, HEAD_SIZE), bf16),
                pltpu.VMEM((blocks, HEAD_SIZE, keys), bf16),
                pltpu.VMEM((keys, QUERY_PER_KV * BLOCK), jnp.int32),
            ],
        ),
        out_shape=[
            jax.ShapeDtypeStruct(queries.shape, bf16),
            jax.ShapeDtypeStruct((heads, QUERY_PER_KV, tokens), f32),
        ],
        compiler_params=pltpu.CompilerParams(vmem_limit_bytes=40 << 20),
        cost_estimate=pl.CostEstimate(flops=3 << 30, bytes_accessed=8 << 20, transcendentals=8 << 20),
        name="attention_forward",
    )(starts, stripes, place, start, queries, *pieces)


def attention_backward(queries, d_att, attended, lse, pieces, starts, stripes, place, start):
    heads, _, _, tokens = queries.shape
    count, blocks = len(pieces), tokens // BLOCK
    keys = count * BLOCK
    per_query = head_spec(QUERY_PER_KV, HEAD_SIZE, tokens)
    per_kv = head_spec(2, HEAD_SIZE, tokens)
    return pl.pallas_call(
        functools.partial(backward_kernel, count, blocks),
        grid_spec=pltpu.PrefetchScalarGridSpec(
            num_scalar_prefetch=2,
            grid=(heads,),
            in_specs=[row_spec(tokens)] * 2
            + [per_query] * 3
            + [head_spec(QUERY_PER_KV, tokens)]
            + [per_kv] * count,
            out_specs=[per_query] + [per_kv] * count,
            scratch_shapes=[
                pltpu.VMEM((blocks, keys, HEAD_SIZE), bf16),
                pltpu.VMEM((blocks, HEAD_SIZE, keys), bf16),
                pltpu.VMEM((blocks, keys, HEAD_SIZE), bf16),
                pltpu.VMEM((keys, QUERY_PER_KV * BLOCK), jnp.int32),
                pltpu.VMEM((blocks, keys, HEAD_SIZE), f32),
                pltpu.VMEM((blocks, keys, HEAD_SIZE), f32),
            ],
        ),
        out_shape=[jax.ShapeDtypeStruct(queries.shape, f32)]
        + [jax.ShapeDtypeStruct(pieces[0].shape, bf16)] * count,
        compiler_params=pltpu.CompilerParams(vmem_limit_bytes=48 << 20),
        cost_estimate=pl.CostEstimate(flops=8 << 30, bytes_accessed=16 << 20, transcendentals=8 << 20),
        name="attention_backward",
    )(starts, stripes, place, start, queries, d_att, attended, lse, *pieces)


def core_swap(value):
    size = lax.axis_size("ctx")
    return lax.ppermute(value, "ctx", [(i, i ^ 1) for i in range(size)])


def chip_shift(value, by):
    size = lax.axis_size("ctx")
    return lax.ppermute(value, "ctx", [(i, (i + 2 * by) % size) for i in range(size)])


def group_shift(value, by):
    size = lax.axis_size("fsdp")
    return lax.ppermute(value, "fsdp", [(i, (i + by) % size) for i in range(size)])


def tp_sum(part):
    part = lax.optimization_barrier(part.astype(bf16))
    size = lax.axis_size("tp")
    if size != 2:
        return lax.psum(part, "tp").astype(f32)
    other = lax.ppermute(part, "tp", [(0, 1), (1, 0)])
    return part.astype(f32) + other.astype(f32)


def rows_for_core(activation, core):
    tokens, width = activation.shape
    groups, chips = lax.axis_size("fsdp"), lax.axis_size("ctx") // 2
    rows = width // (groups * chips * 2)
    turned = activation.T.reshape(groups, chips, 2, rows, tokens)
    return lax.dynamic_index_in_dim(turned, core, 2, keepdims=False)


def weight_gradient(left, right):
    chips = lax.axis_size("ctx") // 2
    groups = lax.axis_size("fsdp")
    chip, group = lax.axis_index("ctx") // 2, lax.axis_index("fsdp")
    _, _, rows, _ = left[0].shape
    columns = right[0].shape[1]

    def product(which):
        total = None
        for a, b in zip(left, right):
            picked = lax.dynamic_index_in_dim(a, which, 1, keepdims=False)
            term = mm(picked.reshape(groups * rows, -1), b)
            total = term if total is None else total + term
        return total

    arrived = [
        chip_shift(product((chip + by) % chips).astype(bf16), by) for by in range(1, chips)
    ]
    total = product(chip)
    for piece in arrived:
        total = total + piece.astype(f32)
    total = total.reshape(groups, rows, columns)
    low = total.astype(bf16)
    result = lax.dynamic_index_in_dim(total, group, 0, keepdims=False)
    for by in range(1, groups):
        sent = lax.dynamic_index_in_dim(low, (group + by) % groups, 0, keepdims=False)
        result = result + group_shift(sent, by).astype(f32)
    return result


def slot_meta(ctx_index, tokens, stripe_row, lengths):
    count = stripe_row.shape[0]
    ends = jnp.cumsum(lengths)
    residue = jnp.sum(jnp.where(jnp.arange(count) == ctx_index, stripe_row, 0))
    packed = jnp.arange(tokens, dtype=jnp.int32) * count + residue
    passed = (packed[:, None] >= ends[None, :]).astype(jnp.int32)
    start = jnp.sum(passed * lengths[None, :], axis=1)
    return packed, start


def rms_normed(values, gain):
    scale_row = lax.rsqrt(jnp.mean(values * values, axis=-1, keepdims=True) + norm_eps)
    return (values * scale_row * gain, scale_row)


def norm_back(grad_normed, values, scale_row, gain):
    unit_rows = values * scale_row
    weighted = grad_normed * gain
    return scale_row * (weighted - unit_rows * jnp.mean(weighted * unit_rows, axis=-1, keepdims=True))


def rotate(vector, cos_table, sin_table):
    front, back = vector[..., 0, :, :], vector[..., 1, :, :]
    return jnp.stack(
        [front * cos_table - back * sin_table, back * cos_table + front * sin_table], axis=-3
    )


def on_device(
    hidden_in,
    cotangent,
    doc_lengths,
    stripe,
    query_key_value_weight,
    output_weight,
    feedforward_weight,
    gains,
):
    ctx_count, ctx_index = lax.axis_size("ctx"), lax.axis_index("ctx")
    group_count, group = lax.axis_size("fsdp"), lax.axis_index("fsdp")
    core = ctx_index % 2
    tokens, width = hidden_in.shape[1:]
    qkv_columns = query_key_value_weight.shape[1]
    att_columns = output_weight.shape[1]
    units = feedforward_weight.shape[2]
    kv_heads = qkv_columns // ((QUERY_PER_KV + 2) * HEAD_SIZE)

    def share(weight):
        rows = weight.shape[0] // ctx_count
        return lax.dynamic_slice_in_dim(weight, ctx_index * rows, rows, 0)

    def gathered(weight):
        return lax.all_gather(weight, ("fsdp", "ctx"), axis=0, tiled=True)

    first = gathered(
        jnp.concatenate([share(query_key_value_weight), share(output_weight)], axis=1)
    )
    wq, wo = first[:, :qkv_columns], first[:, qkv_columns:]
    second = gathered(jnp.concatenate([share(feedforward_weight[i]) for i in range(3)], axis=1))
    w_gate, w_up, w_down = (second[:, i * units : (i + 1) * units] for i in range(3))

    gain_parts = [gains] + [group_shift(gains, by) for by in range(1, group_count)]
    gain_stack = jnp.stack(gain_parts, axis=0)
    gain_rows = jnp.concatenate(
        [
            lax.dynamic_index_in_dim(gain_stack, (group - i) % group_count, 0, keepdims=False)
            for i in range(group_count)
        ],
        axis=1,
    ).astype(f32)

    lengths, stripe_row = doc_lengths[0], stripe[0]
    packed, start = slot_meta(ctx_index, tokens, stripe_row, lengths)
    frequency = rope_base ** (-(2.0 * jnp.arange(HALF, dtype=f32)) / HEAD_SIZE)
    angles = frequency[:, None] * (packed - start).astype(f32)[None, :]
    cos_table, sin_table = jnp.cos(angles), jnp.sin(angles)
    block_starts = start[::BLOCK] // (ctx_count * BLOCK)
    sources = []
    for by in range(ctx_count // 2):
        source = (ctx_index - 2 * by) % ctx_count
        sources += [source, source ^ 1]
    stripes = jnp.stack(
        [lax.dynamic_index_in_dim(stripe_row, s, 0, keepdims=False) for s in sources]
    )
    meta = (block_starts, stripes, packed[None, :], start[None, :])

    layer_input = hidden_in[0].astype(f32)
    first_normed, scale_one = rms_normed(layer_input, gain_rows[0])
    first_normed = first_normed.astype(bf16)
    projected = mm(wq, first_normed, ((0,), (1,))).reshape(
        kv_heads, QUERY_PER_KV + 2, 2, HALF, tokens
    )
    turned = rotate(projected[:, : QUERY_PER_KV + 1], cos_table, sin_table).astype(bf16)
    queries = turned[:, :QUERY_PER_KV].reshape(kv_heads, QUERY_PER_KV, HEAD_SIZE, tokens)
    kv_own = jnp.stack(
        [
            turned[:, QUERY_PER_KV].reshape(kv_heads, HEAD_SIZE, tokens),
            projected[:, QUERY_PER_KV + 1].astype(bf16).reshape(kv_heads, HEAD_SIZE, tokens),
        ],
        axis=1,
    )
    pieces = []
    for by in range(ctx_count // 2):
        piece = chip_shift(kv_own, by) if by else kv_own
        pieces += [piece, core_swap(piece)]
    attended, lse = attention_forward(queries, pieces, *meta)
    attended_rows = attended.reshape(att_columns, tokens)
    attn_part = mm(attended_rows, wo, ((0,), (1,)))
    middle = layer_input + tp_sum(attn_part)

    second_normed, scale_two = rms_normed(middle, gain_rows[1])
    second_normed = second_normed.astype(bf16)
    grad_low = cotangent[0]
    gate = mm(second_normed, w_gate)
    up = mm(second_normed, w_up)
    d_act = mm(grad_low, w_down)
    sigmoid_gate = jax.nn.sigmoid(gate)
    silu_gate = gate * sigmoid_gate
    activated = (silu_gate * up).astype(bf16)
    d_gate = (d_act * up * sigmoid_gate * (1.0 + gate * (1.0 - sigmoid_gate))).astype(bf16)
    d_up = (d_act * silu_gate).astype(bf16)
    d_two = tp_sum(mm(d_gate, w_gate, ((1,), (1,))) + mm(d_up, w_up, ((1,), (1,))))
    hidden_out = (middle + tp_sum(mm(activated, w_down, ((1,), (1,))))).astype(bf16)

    def exchanged(activation):
        return rows_for_core(activation, core), core_swap(rows_for_core(activation, 1 - core))

    def both(value):
        return value, core_swap(value)

    rows_two = exchanged(second_normed)
    rows_dy = exchanged(grad_low)
    grad_gate = weight_gradient(rows_two, both(d_gate))
    grad_up = weight_gradient(rows_two, both(d_up))
    grad_down = weight_gradient(rows_dy, both(activated))

    d_mid = grad_low.astype(f32) + norm_back(d_two, middle, scale_two, gain_rows[1])
    gain_two = jnp.sum(d_two * (middle * scale_two), axis=0)
    d_branch = d_mid.astype(bf16)

    d_att = mm(wo, d_branch, ((0,), (1,))).astype(bf16).reshape(attended.shape)
    back = attention_backward(queries, d_att, attended, lse, pieces, *meta)
    d_query, d_pieces = back[0], back[1:]
    grad_out = weight_gradient(exchanged(d_branch), both(attended_rows.T))
    d_kv = None
    for by in reversed(range(ctx_count // 2)):
        mine, partners = d_pieces[2 * by], d_pieces[2 * by + 1]
        chip_sum = mine.astype(f32) + core_swap(partners).astype(f32)
        term = chip_shift(chip_sum.astype(bf16), -by).astype(f32) if by else chip_sum
        d_kv = term if d_kv is None else d_kv + term
    d_kv = d_kv.reshape(kv_heads, 2, 2, HALF, tokens)
    d_query = d_query.reshape(kv_heads, QUERY_PER_KV, 2, HALF, tokens)
    d_turned = rotate(
        jnp.concatenate([d_query, d_kv[:, :1]], axis=1), cos_table, -sin_table
    )
    d_proj = (
        jnp.concatenate([d_turned, d_kv[:, 1:]], axis=1).astype(bf16).reshape(qkv_columns, tokens)
    )
    d_one_part = mm(d_proj, wq, ((0,), (1,)))
    d_one = tp_sum(d_one_part)
    grad_qkv = weight_gradient(exchanged(first_normed), both(d_proj.T))
    grad_in = (d_mid + norm_back(d_one, layer_input, scale_one, gain_rows[0])).astype(bf16)
    gain_one = jnp.sum(d_one * (layer_input * scale_one), axis=0)

    grad_ffn = jnp.stack([grad_gate, grad_up, grad_down], axis=0)
    grad_gains = lax.psum_scatter(
        jnp.stack([gain_one, gain_two], axis=0), ("fsdp", "ctx"), scatter_dimension=1, tiled=True
    )
    return (hidden_out[None], grad_in[None], grad_qkv, grad_out, grad_ffn, grad_gains)


def solution(mesh):
    return jax.shard_map(
        on_device,
        mesh=mesh,
        in_specs=(
            P("fsdp", "ctx", None),
            P("fsdp", "ctx", None),
            P("fsdp", None),
            P("fsdp", None),
            P("fsdp", "tp"),
            P("fsdp", "tp"),
            P(None, "fsdp", "tp"),
            P(None, "fsdp"),
        ),
        out_specs=(
            P("fsdp", "ctx", None),
            P("fsdp", "ctx", None),
            P(("fsdp", "ctx"), "tp"),
            P(("fsdp", "ctx"), "tp"),
            P(None, ("fsdp", "ctx"), "tp"),
            P(None, ("fsdp", "ctx")),
        ),
        check_vma=False,
    )
```

```python
import functools
import math

import jax
import jax.numpy as jnp
from jax import lax
from jax.experimental import pallas as pl
from jax.experimental.pallas import tpu as pltpu
from jax.sharding import PartitionSpec as P

HEAD_SIZE = 96
QUERY_PER_KV = 2
HALF = HEAD_SIZE // 2
BLOCK = 128
CHUNKS = 2

norm_eps = 1e-05
rope_base = 100000.0
masked_score = -1e30
SCORE_SCALE = HEAD_SIZE ** (-0.5)
SCORE_SCALE_2 = SCORE_SCALE * math.log2(math.e)

SMALL_COST = pl.CostEstimate(flops=1, bytes_accessed=1, transcendentals=0)

bf16 = jnp.bfloat16
f32 = jnp.float32


def mm(a, b, contract=((1,), (0,))):
    return lax.dot_general(a, b, (contract, ((), ())), preferred_element_type=f32)


def fill_keys(count, blocks, kv_refs, kn_ref, kt_ref, vn_ref, vt_ref):
    for s in range(count):
        for b in range(blocks):
            columns = slice(b * BLOCK, (b + 1) * BLOCK)
            places = slice(s * BLOCK, (s + 1) * BLOCK)
            key = kv_refs[s][0, 0, :, columns]
            value = kv_refs[s][0, 1, :, columns]
            kn_ref[b, places, :] = key.T
            if kt_ref is not None:
                kt_ref[b, :, places] = key
            if vn_ref is not None:
                vn_ref[b, places, :] = value.T
            if vt_ref is not None:
                vt_ref[b, :, places] = value


def fill_places(count, stripes_ref, place_ref):
    step = lax.broadcasted_iota(jnp.int32, (BLOCK, QUERY_PER_KV * BLOCK), 0) * count
    for s in range(count):
        place_ref[s * BLOCK : (s + 1) * BLOCK, :] = step + stripes_ref[s]


def twice(row):
    return jnp.concatenate([row] * QUERY_PER_KV, axis=1)


def block_of(ref, i):
    columns = slice(i * BLOCK, (i + 1) * BLOCK)
    return jnp.concatenate([ref[0, g, :, columns] for g in range(QUERY_PER_KV)], axis=1)


def forward_kernel(count, blocks, starts_ref, stripes_ref, place_q_ref, start_q_ref, q_ref, *rest):
    kv_refs = rest[:count]
    o_ref, lse_ref, kn_ref, vt_ref, place_ref = rest[count:]
    fill_keys(count, blocks, kv_refs, kn_ref, None, None, vt_ref)
    fill_places(count, stripes_ref, place_ref)
    for i in range(blocks):
        columns = slice(i * BLOCK, (i + 1) * BLOCK)
        query = block_of(q_ref, i)
        place_q = twice(place_q_ref[:, columns])
        start_q = twice(start_q_ref[:, columns])

        def scores_of(b):
            scores = mm(kn_ref[b], query)
            offset = b * (BLOCK * count)
            place = place_ref[...]
            allowed = (place >= start_q - offset) & (place <= place_q - offset)
            return jnp.where(allowed, scores * SCORE_SCALE_2, masked_score)

        scores = scores_of(i)
        top = jnp.max(scores, axis=0, keepdims=True)
        weights = jnp.exp2(scores - top)
        total = jnp.sum(weights, axis=0, keepdims=True)
        accum = mm(vt_ref[i], weights.astype(bf16))

        def step(b, carry):
            top, total, accum = carry
            scores = scores_of(b)
            new_top = jnp.maximum(top, jnp.max(scores, axis=0, keepdims=True))
            fade = jnp.exp2(top - new_top)
            weights = jnp.exp2(scores - new_top)
            total = total * fade + jnp.sum(weights, axis=0, keepdims=True)
            accum = accum * fade + mm(vt_ref[b], weights.astype(bf16))
            return new_top, total, accum

        top, total, accum = lax.fori_loop(starts_ref[i], i, step, (top, total, accum))
        result = (accum / total).astype(bf16)
        lse = top + jnp.log2(total)
        for g in range(QUERY_PER_KV):
            part = slice(g * BLOCK, (g + 1) * BLOCK)
            o_ref[0, g, :, columns] = result[:, part]
            lse_ref[0, g : g + 1, columns] = lse[:, part]


def backward_kernel(
    count, blocks, starts_ref, stripes_ref, place_q_ref, start_q_ref, q_ref, do_ref, o_ref, lse_ref, *rest
):
    kv_refs = rest[:count]
    dq_ref = rest[count]
    dkv_refs = rest[count + 1 : 2 * count + 1]
    kn_ref, kt_ref, vn_ref, place_ref, dk_ref, dv_ref = rest[2 * count + 1 :]
    fill_keys(count, blocks, kv_refs, kn_ref, kt_ref, vn_ref, None)
    fill_places(count, stripes_ref, place_ref)
    dk_ref[...] = jnp.zeros_like(dk_ref)
    dv_ref[...] = jnp.zeros_like(dv_ref)
    for i in range(blocks):
        columns = slice(i * BLOCK, (i + 1) * BLOCK)
        query = block_of(q_ref, i)
        d_out = block_of(do_ref, i)
        out = block_of(o_ref, i)
        query_rows = query.T
        d_out_rows = d_out.T
        delta = jnp.sum(d_out.astype(f32) * out.astype(f32), axis=0, keepdims=True)
        lse = jnp.concatenate([lse_ref[0, g : g + 1, columns] for g in range(QUERY_PER_KV)], axis=1)
        place_q = twice(place_q_ref[:, columns])
        start_q = twice(start_q_ref[:, columns])

        def step(b, d_query):
            scores = mm(kn_ref[b], query)
            offset = b * (BLOCK * count)
            place = place_ref[...]
            allowed = (place >= start_q - offset) & (place <= place_q - offset)
            probs = jnp.exp2(jnp.where(allowed, scores * SCORE_SCALE_2, masked_score) - lse)
            d_prob = mm(vn_ref[b], d_out)
            d_score = (probs * (d_prob - delta)).astype(bf16)
            dv_ref[b] += mm(probs.astype(bf16), d_out_rows)
            dk_ref[b] += mm(d_score, query_rows)
            return d_query + mm(kt_ref[b], d_score)

        d_query = lax.fori_loop(
            starts_ref[i], i + 1, step, jnp.zeros((HEAD_SIZE, QUERY_PER_KV * BLOCK), f32)
        )
        for g in range(QUERY_PER_KV):
            dq_ref[0, g, :, columns] = d_query[:, g * BLOCK : (g + 1) * BLOCK] * SCORE_SCALE
    for s in range(count):
        places = slice(s * BLOCK, (s + 1) * BLOCK)
        for b in range(blocks):
            columns = slice(b * BLOCK, (b + 1) * BLOCK)
            dkv_refs[s][0, 0, :, columns] = (dk_ref[b, places, :] * SCORE_SCALE).T.astype(bf16)
            dkv_refs[s][0, 1, :, columns] = dv_ref[b, places, :].T.astype(bf16)


def head_spec(*dims):
    return pl.BlockSpec((1, *dims), lambda h, *_: (h,) + (0,) * len(dims))


def row_spec(tokens):
    return pl.BlockSpec((1, tokens), lambda h, *_: (0, 0))


def attention_forward(queries, pieces, starts, stripes, place, start):
    heads, _, _, tokens = queries.shape
    count, blocks = len(pieces), tokens // BLOCK
    keys = count * BLOCK
    per_query = head_spec(QUERY_PER_KV, HEAD_SIZE, tokens)
    per_kv = head_spec(2, HEAD_SIZE, tokens)
    return pl.pallas_call(
        functools.partial(forward_kernel, count, blocks),
        grid_spec=pltpu.PrefetchScalarGridSpec(
            num_scalar_prefetch=2,
            grid=(heads,),
            in_specs=[row_spec(tokens)] * 2 + [per_query] + [per_kv] * count,
            out_specs=[per_query, head_spec(QUERY_PER_KV, tokens)],
            scratch_shapes=[
                pltpu.VMEM((blocks, keys, HEAD_SIZE), bf16),
                pltpu.VMEM((blocks, HEAD_SIZE, keys), bf16),
                pltpu.VMEM((keys, QUERY_PER_KV * BLOCK), jnp.int32),
            ],
        ),
        out_shape=[
            jax.ShapeDtypeStruct(queries.shape, bf16),
            jax.ShapeDtypeStruct((heads, QUERY_PER_KV, tokens), f32),
        ],
        compiler_params=pltpu.CompilerParams(vmem_limit_bytes=40 << 20),
        cost_estimate=SMALL_COST,
        name="attention_forward",
    )(starts, stripes, place, start, queries, *pieces)


def attention_backward(queries, d_att, attended, lse, pieces, starts, stripes, place, start):
    heads, _, _, tokens = queries.shape
    count, blocks = len(pieces), tokens // BLOCK
    keys = count * BLOCK
    per_query = head_spec(QUERY_PER_KV, HEAD_SIZE, tokens)
    per_kv = head_spec(2, HEAD_SIZE, tokens)
    return pl.pallas_call(
        functools.partial(backward_kernel, count, blocks),
        grid_spec=pltpu.PrefetchScalarGridSpec(
            num_scalar_prefetch=2,
            grid=(heads,),
            in_specs=[row_spec(tokens)] * 2
            + [per_query] * 3
            + [head_spec(QUERY_PER_KV, tokens)]
            + [per_kv] * count,
            out_specs=[per_query] + [per_kv] * count,
            scratch_shapes=[
                pltpu.VMEM((blocks, keys, HEAD_SIZE), bf16),
                pltpu.VMEM((blocks, HEAD_SIZE, keys), bf16),
                pltpu.VMEM((blocks, keys, HEAD_SIZE), bf16),
                pltpu.VMEM((keys, QUERY_PER_KV * BLOCK), jnp.int32),
                pltpu.VMEM((blocks, keys, HEAD_SIZE), f32),
                pltpu.VMEM((blocks, keys, HEAD_SIZE), f32),
            ],
        ),
        out_shape=[jax.ShapeDtypeStruct(queries.shape, f32)]
        + [jax.ShapeDtypeStruct(pieces[0].shape, bf16)] * count,
        compiler_params=pltpu.CompilerParams(vmem_limit_bytes=48 << 20),
        cost_estimate=SMALL_COST,
        name="attention_backward",
    )(starts, stripes, place, start, queries, d_att, attended, lse, *pieces)


def pack_kernel(_, ffn_ref, out_ref, other_ref, packed_ref):
    units, columns = ffn_ref.shape[2], out_ref.shape[1]
    for i in range(3):
        packed_ref[:, i * units : (i + 1) * units] = ffn_ref[i]
    packed_ref[:, 3 * units : 3 * units + columns] = out_ref[...]
    packed_ref[:, 3 * units + columns :] = other_ref[...]


def packed_share(feedforward_weight, out_share, out_other, index, share_of):
    rows, columns = out_share.shape
    units = feedforward_weight.shape[2]
    if rows % 16:
        parts = [share_of(feedforward_weight[i]) for i in range(3)]
        return jnp.concatenate([*parts, out_share, out_other], axis=1)
    whole = pl.BlockSpec((rows, columns), lambda n, _: (0, 0))
    width = 3 * units + 2 * columns
    return pl.pallas_call(
        pack_kernel,
        grid_spec=pltpu.PrefetchScalarGridSpec(
            num_scalar_prefetch=1,
            grid=(1,),
            in_specs=[
                pl.BlockSpec((3, rows, units), lambda n, place: (0, place[0], 0)),
                whole,
                whole,
            ],
            out_specs=pl.BlockSpec((rows, width), lambda n, _: (0, 0)),
        ),
        out_shape=jax.ShapeDtypeStruct((rows, width), bf16),
        compiler_params=pltpu.CompilerParams(vmem_limit_bytes=32 << 20),
        cost_estimate=SMALL_COST,
        name="pack",
    )(index[None], feedforward_weight, out_share, out_other)


def input_gradient_kernel(mine_ref, other_ref, x_ref, d_mid_ref, gain_ref, out_ref):
    x = x_ref[...].astype(f32)
    scale = lax.rsqrt(jnp.mean(x * x, axis=-1, keepdims=True) + norm_eps)
    unit = x * scale
    weighted = (mine_ref[...].astype(f32) + other_ref[...].astype(f32)) * gain_ref[...]
    out_ref[...] = (
        d_mid_ref[...]
        + scale * (weighted - unit * jnp.mean(weighted * unit, axis=-1, keepdims=True))
    ).astype(bf16)


def input_gradient(sent, x, d_mid, gain):
    tokens, width = x.shape
    block = 256
    here = pl.BlockSpec((block, width), lambda n: (n, 0))
    return pl.pallas_call(
        input_gradient_kernel,
        grid=(tokens // block,),
        in_specs=[here] * 4 + [pl.BlockSpec((1, width), lambda n: (0, 0))],
        out_specs=here,
        out_shape=jax.ShapeDtypeStruct((tokens, width), bf16),
        compiler_params=pltpu.CompilerParams(vmem_limit_bytes=32 << 20),
        cost_estimate=SMALL_COST,
        name="input_gradient",
    )(*sent, x, d_mid, gain)


def project_kernel(x_ref, w_ref, cos_ref, sin_ref, q_ref, kv_ref):
    projected = mm(x_ref[...], w_ref[...]).T
    cos_table, sin_table = cos_ref[...], sin_ref[...]
    for j in range(QUERY_PER_KV + 1):
        first = j * HEAD_SIZE
        front = projected[first : first + HALF]
        back = projected[first + HALF : first + HEAD_SIZE]
        target = q_ref.at[0, j] if j < QUERY_PER_KV else kv_ref.at[0, 0]
        target[:HALF, :] = (front * cos_table - back * sin_table).astype(bf16)
        target[HALF:, :] = (back * cos_table + front * sin_table).astype(bf16)
    kv_ref[0, 1] = projected[(QUERY_PER_KV + 1) * HEAD_SIZE :].astype(bf16)


def project(normed, weight, cos_table, sin_table, first, heads):
    tokens, width = normed.shape
    columns = (QUERY_PER_KV + 2) * HEAD_SIZE
    whole = lambda shape: pl.BlockSpec(shape, lambda h: (0, 0))
    return pl.pallas_call(
        project_kernel,
        grid=(heads,),
        in_specs=[
            whole((tokens, width)),
            pl.BlockSpec((width, columns), lambda h: (0, first + h)),
            whole((HALF, tokens)),
            whole((HALF, tokens)),
        ],
        out_specs=[
            pl.BlockSpec((1, QUERY_PER_KV, HEAD_SIZE, tokens), lambda h: (h, 0, 0, 0)),
            pl.BlockSpec((1, 2, HEAD_SIZE, tokens), lambda h: (h, 0, 0, 0)),
        ],
        out_shape=[
            jax.ShapeDtypeStruct((heads, QUERY_PER_KV, HEAD_SIZE, tokens), bf16),
            jax.ShapeDtypeStruct((heads, 2, HEAD_SIZE, tokens), bf16),
        ],
        compiler_params=pltpu.CompilerParams(vmem_limit_bytes=40 << 20),
        cost_estimate=SMALL_COST,
        name="project",
    )(normed, weight, cos_table, sin_table)


def middle_kernel(count, tp_ref, x_ref, gain_ref, *refs):
    mine, others = refs[:count], refs[count : 2 * count]
    w_first, w_second, middle_ref, normed_ref, first_ref, second_ref = refs[2 * count :]

    def fill(first, second):
        first_ref[...] = jnp.concatenate([r[...] for r in first], axis=0).T
        second_ref[...] = jnp.concatenate([r[...] for r in second], axis=0).T

    @pl.when(tp_ref[0] == 0)
    def _():
        fill(mine, others)

    @pl.when(tp_ref[0] == 1)
    def _():
        fill(others, mine)

    branch = mm(first_ref[...], w_first[...], ((1,), (1,))) + mm(
        second_ref[...], w_second[...], ((1,), (1,))
    )
    middle = x_ref[...].astype(f32) + branch
    middle_ref[...] = middle
    scale = lax.rsqrt(jnp.mean(middle * middle, axis=-1, keepdims=True) + norm_eps)
    normed_ref[...] = (middle * scale * gain_ref[...]).astype(bf16)


def middle_of(mine, others, tp_index, x, gain, weight, first):
    tokens, width = x.shape
    features = sum(p.shape[0] for p in mine)
    block = 256
    half = first // features
    token_spec = pl.BlockSpec((block, width), lambda n, _: (n, 0))
    return pl.pallas_call(
        functools.partial(middle_kernel, len(mine)),
        grid_spec=pltpu.PrefetchScalarGridSpec(
            num_scalar_prefetch=1,
            grid=(tokens // block,),
            in_specs=[token_spec, pl.BlockSpec((1, width), lambda n, _: (0, 0))]
            + [pl.BlockSpec((p.shape[0], block), lambda n, _: (0, n)) for p in (*mine, *others)]
            + [
                pl.BlockSpec((width, features), lambda n, tp: (0, half + tp[0])),
                pl.BlockSpec((width, features), lambda n, tp: (0, half + 1 - tp[0])),
            ],
            out_specs=[token_spec] * 2,
            scratch_shapes=[pltpu.VMEM((block, features), bf16)] * 2,
        ),
        out_shape=[
            jax.ShapeDtypeStruct((tokens, width), f32),
            jax.ShapeDtypeStruct((tokens, width), bf16),
        ],
        compiler_params=pltpu.CompilerParams(vmem_limit_bytes=40 << 20),
        cost_estimate=SMALL_COST,
        name="middle",
    )(tp_index[None], x, gain, *mine, *others, weight, weight)


def down_kernel(a_ref, w_ref, out_ref):
    out_ref[...] = mm(a_ref[...], w_ref[...], ((1,), (1,))).astype(bf16)


def down_project(activated, weight, first):
    tokens, units = activated.shape
    width, block = weight.shape[0], 512
    return pl.pallas_call(
        down_kernel,
        grid=(width // block,),
        in_specs=[
            pl.BlockSpec((tokens, units), lambda n: (0, 0)),
            pl.BlockSpec((block, units), lambda n: (n, first // units)),
        ],
        out_specs=pl.BlockSpec((tokens, block), lambda n: (0, n)),
        out_shape=jax.ShapeDtypeStruct((tokens, width), bf16),
        compiler_params=pltpu.CompilerParams(vmem_limit_bytes=40 << 20),
        cost_estimate=SMALL_COST,
        name="down_project",
    )(activated, weight)


def d_middle_kernel(
    mine_ref, other_ref, middle_ref, dy_ref, gain_ref, w_ref, d_mid_ref, branch_ref, d_att_ref
):
    middle = middle_ref[...]
    scale = lax.rsqrt(jnp.mean(middle * middle, axis=-1, keepdims=True) + norm_eps)
    unit = middle * scale
    weighted = (mine_ref[...].astype(f32) + other_ref[...].astype(f32)) * gain_ref[...]
    d_mid = dy_ref[...].astype(f32) + scale * (
        weighted - unit * jnp.mean(weighted * unit, axis=-1, keepdims=True)
    )
    d_mid_ref[...] = d_mid
    branch = d_mid.astype(bf16)
    branch_ref[...] = branch
    d_att_ref[...] = mm(branch, w_ref[...]).astype(bf16).T


def d_middle_of(sent, middle, d_out, gain, weight, first, features):
    mine, other = sent
    tokens, width = middle.shape
    block = 256
    here = pl.BlockSpec((block, width), lambda n: (n, 0))
    row = pl.BlockSpec((1, width), lambda n: (0, 0))
    return pl.pallas_call(
        d_middle_kernel,
        grid=(tokens // block,),
        in_specs=[here, here, here, here, row]
        + [pl.BlockSpec((width, features), lambda n: (0, first // features))],
        out_specs=[here, here, pl.BlockSpec((features, block), lambda n: (0, n))],
        out_shape=[
            jax.ShapeDtypeStruct((tokens, width), f32),
            jax.ShapeDtypeStruct((tokens, width), bf16),
            jax.ShapeDtypeStruct((features, tokens), bf16),
        ],
        compiler_params=pltpu.CompilerParams(vmem_limit_bytes=48 << 20),
        cost_estimate=SMALL_COST,
        name="d_middle",
    )(mine, other, middle, d_out, gain, weight)


def turn_back_kernel(cos_ref, sin_ref, dq_ref, *refs):
    kv_refs, out_ref = refs[:-1], refs[-1]
    cos_table, sin_table = cos_ref[...], sin_ref[...]
    total = kv_refs[0][0].astype(f32)
    for ref in kv_refs[1:]:
        total = total + ref[0].astype(f32)
    for j in range(QUERY_PER_KV + 1):
        vector = dq_ref[0, j] if j < QUERY_PER_KV else total[0]
        front, back = vector[:HALF], vector[HALF:]
        first = j * HEAD_SIZE
        out_ref[first : first + HALF, :] = (front * cos_table + back * sin_table).astype(bf16)
        out_ref[first + HALF : first + HEAD_SIZE, :] = (
            back * cos_table - front * sin_table
        ).astype(bf16)
    out_ref[(QUERY_PER_KV + 1) * HEAD_SIZE :, :] = total[1].astype(bf16)


def turned_back(d_query, d_kv_terms, cos_table, sin_table):
    heads, _, _, tokens = d_query.shape
    columns = (QUERY_PER_KV + 2) * HEAD_SIZE
    whole = pl.BlockSpec((HALF, tokens), lambda h: (0, 0))
    head = lambda n: pl.BlockSpec((1, n, HEAD_SIZE, tokens), lambda h: (h, 0, 0, 0))
    return pl.pallas_call(
        turn_back_kernel,
        grid=(heads,),
        in_specs=[whole, whole, head(QUERY_PER_KV)] + [head(2)] * len(d_kv_terms),
        out_specs=pl.BlockSpec((columns, tokens), lambda h: (h, 0)),
        out_shape=jax.ShapeDtypeStruct((heads * columns, tokens), bf16),
        compiler_params=pltpu.CompilerParams(vmem_limit_bytes=32 << 20),
        cost_estimate=SMALL_COST,
        name="turn_back",
    )(cos_table, sin_table, d_query, *d_kv_terms)


def d_one_kernel(count, *refs):
    parts, w_ref, out_ref, rows_ref = refs[:count], refs[count], refs[count + 1], refs[count + 2]

    @pl.when(pl.program_id(0) == 0)
    def _():
        first = 0
        for part in parts:
            columns = part.shape[0]
            rows_ref[:, first : first + columns] = part[...].T
            first += columns

    out_ref[...] = mm(rows_ref[...], w_ref[...], ((1,), (1,))).astype(bf16)


def d_one_of(parts, weight):
    width, columns = weight.shape
    tokens, block = parts[0].shape[1], 512
    return pl.pallas_call(
        functools.partial(d_one_kernel, len(parts)),
        grid=(width // block,),
        in_specs=[pl.BlockSpec(p.shape, lambda n: (0, 0)) for p in parts]
        + [pl.BlockSpec((block, columns), lambda n: (n, 0))],
        out_specs=pl.BlockSpec((tokens, block), lambda n: (0, n)),
        out_shape=jax.ShapeDtypeStruct((tokens, width), bf16),
        scratch_shapes=[pltpu.VMEM((tokens, columns), bf16)],
        compiler_params=pltpu.CompilerParams(vmem_limit_bytes=40 << 20),
        cost_estimate=SMALL_COST,
        name="d_one",
    )(*parts, weight)


def ffn_kernel(
    h_ref, dy_ref, wg_ref, wu_ref, wd_ref, act_ref, dg_ref, du_ref, out_ref, acc_ref
):
    step = pl.program_id(0)
    w_gate, w_up = wg_ref[...], wu_ref[...]
    gate = mm(h_ref[...], w_gate)
    up = mm(h_ref[...], w_up)
    d_act = mm(dy_ref[...], wd_ref[...])
    sigmoid_gate = jax.nn.sigmoid(gate)
    silu_gate = gate * sigmoid_gate
    act_ref[...] = (silu_gate * up).astype(bf16)
    d_gate = (d_act * up * sigmoid_gate * (1.0 + gate * (1.0 - sigmoid_gate))).astype(bf16)
    d_up = (d_act * silu_gate).astype(bf16)
    dg_ref[...] = d_gate
    du_ref[...] = d_up
    term = mm(d_gate, w_gate, ((1,), (1,))) + mm(d_up, w_up, ((1,), (1,)))

    @pl.when(step == 0)
    def _():
        acc_ref[...] = term

    @pl.when(step > 0)
    def _():
        acc_ref[...] += term

    @pl.when(step == pl.num_programs(0) - 1)
    def _():
        out_ref[...] = acc_ref[...].astype(bf16)


FFN_BLOCK = 512


def feed_forward(normed, d_out, weights, units):
    tokens, width = normed.shape
    weight_spec = lambda i: pl.BlockSpec(
        (width, FFN_BLOCK), lambda n: (0, i * units // FFN_BLOCK + n)
    )
    column_spec = pl.BlockSpec((tokens, FFN_BLOCK), lambda n: (0, n))
    whole = pl.BlockSpec((tokens, width), lambda n: (0, 0))
    return pl.pallas_call(
        ffn_kernel,
        grid=(units // FFN_BLOCK,),
        in_specs=[whole, whole] + [weight_spec(i) for i in range(3)],
        out_specs=[column_spec] * 3 + [whole],
        out_shape=[jax.ShapeDtypeStruct((tokens, units), bf16)] * 3
        + [jax.ShapeDtypeStruct((tokens, width), bf16)],
        scratch_shapes=[pltpu.VMEM((tokens, width), f32)],
        compiler_params=pltpu.CompilerParams(vmem_limit_bytes=56 << 20),
        cost_estimate=SMALL_COST,
        name="feed_forward",
    )(normed, d_out, weights, weights, weights)


def turn_kernel(chips, rows, core_ref, x_ref, mine_ref, other_ref, turned_ref):
    turned_ref[...] = x_ref[...].T
    core = core_ref[0]
    for chip in range(chips):
        for ref, which in ((mine_ref, core), (other_ref, 1 - core)):
            first = pl.multiple_of((chip * 2 + which) * rows, 16)
            ref[0, chip] = turned_ref[pl.ds(first, rows), :]


def rows_for_cores(activation, core):
    tokens, width = activation.shape
    groups, chips = lax.axis_size("fsdp"), lax.axis_size("ctx") // 2
    rows = width // (groups * chips * 2)
    shape = (groups, chips, rows, tokens)
    if rows % 16 or (width // groups) % 128:
        turned = activation.T.reshape(groups, chips, 2, rows, tokens)
        return tuple(
            lax.dynamic_index_in_dim(turned, c, 2, keepdims=False) for c in (core, 1 - core)
        )
    spec = pl.BlockSpec((1, chips, rows, tokens), lambda g, _: (g, 0, 0, 0))
    return pl.pallas_call(
        functools.partial(turn_kernel, chips, rows),
        grid_spec=pltpu.PrefetchScalarGridSpec(
            num_scalar_prefetch=1,
            grid=(groups,),
            in_specs=[pl.BlockSpec((tokens, width // groups), lambda g, _: (0, g))],
            out_specs=[spec, spec],
            scratch_shapes=[pltpu.VMEM((width // groups, tokens), bf16)],
        ),
        out_shape=[jax.ShapeDtypeStruct(shape, bf16)] * 2,
        compiler_params=pltpu.CompilerParams(vmem_limit_bytes=32 << 20),
        cost_estimate=SMALL_COST,
        name="turn_rows",
    )(core[None], activation)


class Order:
    def __init__(self, always=None):
        self.last = ()
        self.always = always

    def __call__(self, function, *args):
        leaves, tree = jax.tree.flatten(args)
        held = lax.optimization_barrier((*leaves, *self.last))
        result = function(*jax.tree.unflatten(tree, held[: len(leaves)]))
        self.last = (jax.tree.leaves(result)[0],)
        return result

    def apart(self, function, *args):
        def guarded(*args):
            shapes = jax.eval_shape(function, *args)
            nothing = lambda *_: jax.tree.map(lambda s: jnp.zeros(s.shape, s.dtype), shapes)
            return lax.cond(self.always, function, nothing, *args)

        return self(guarded, *args)


def swapped_of(*values):
    return [core_swap(v) for v in values]


def core_swap(value):
    size = lax.axis_size("ctx")
    return lax.ppermute(value, "ctx", [(i, i ^ 1) for i in range(size)])


def chip_shift(value, by):
    size = lax.axis_size("ctx")
    return lax.ppermute(value, "ctx", [(i, (i + 2 * by) % size) for i in range(size)])


def group_shift(value, by):
    size = lax.axis_size("fsdp")
    return lax.ppermute(value, "fsdp", [(i, (i + by) % size) for i in range(size)])


def tp_swap(value):
    return lax.ppermute(value, "tp", [(0, 1), (1, 0)])


def tp_send(part):
    part = lax.optimization_barrier(part)
    return part, tp_swap(part)


def tp_add(sent):
    mine, other = sent
    return mine.astype(f32) + other.astype(f32)


def both_cores(value):
    return value, core_swap(value)


def gathered_rows(weight, gains, hold):
    groups, count = lax.axis_size("fsdp"), lax.axis_size("ctx")
    group, index = lax.axis_index("fsdp"), lax.axis_index("ctx")
    rows, columns = weight.shape
    share = rows // count
    mine = lax.dynamic_slice_in_dim(weight, index * share, share, 0)
    extra = jnp.pad(gains, ((0, 16 - gains.shape[0]), (0, columns - gains.shape[1])))
    mine = jnp.concatenate([mine, extra], axis=0)
    fetched = [group_shift(mine, by) for by in range(1, groups)]
    stack = jnp.stack([gains] + [p[share : share + 2, : gains.shape[1]] for p in fetched], axis=0)
    all_gains = jnp.concatenate(
        [
            lax.dynamic_index_in_dim(stack, (group - i) % groups, 0, keepdims=False)
            for i in range(groups)
        ],
        axis=1,
    ).astype(f32)
    weight, _ = lax.optimization_barrier((weight, hold))
    whole = jnp.zeros((groups * rows, columns), weight.dtype)
    whole = lax.dynamic_update_slice_in_dim(whole, weight, group * rows, 0)
    pieces = jnp.stack([p[:share] for p in fetched], axis=0)

    def placed(whole, pieces, source):
        for by in range(1, groups):
            first = (group - by) % groups * rows + source * share
            whole = lax.dynamic_update_slice_in_dim(whole, pieces[by - 1], first, 0)
        return whole

    passed = [pieces] + [chip_shift(pieces, by) for by in range(1, count // 2)]
    for by, moved in enumerate(passed):
        source = (index - 2 * by) % count
        whole = placed(whole, moved, source)
        whole = placed(whole, core_swap(moved), source ^ 1)
    return whole, all_gains


def gradient_kernel(pairs, turned, pieces, place_ref, *refs):
    total = None
    for i in range(pairs):
        left, right = refs[2 * i], refs[2 * i + 1]
        groups, _, rows, tokens = left.shape
        term = mm(
            left[...].reshape(groups * rows, tokens), right[...], ((1,), (1 if turned else 0,))
        )
        total = term if total is None else total + term
    total = total.reshape(groups, rows, total.shape[-1])
    refs = refs[2 * pairs :]
    arrived = refs[: -1 if not pieces else -1 - groups]
    for piece in arrived:
        total = total + piece[...].astype(f32)
    if not pieces:
        refs[-1][...] = total.astype(bf16)
        return
    outs, sum_ref = refs[-1 - groups : -1], refs[-1]
    sum_ref[...] = total
    group = place_ref[1]
    for by, out in enumerate(outs):
        out[...] = sum_ref[lax.rem(group + by, groups)].astype(out.dtype)


def gradient_call(left, right, which, turned, arrived, pieces):
    groups, chips, rows, tokens = left[0].shape
    group = lax.axis_index("fsdp")
    columns = right[0].shape[0 if turned else 1]
    block = next((b for b in (512, 384) if columns % b == 0), columns)
    if rows % 16 or columns % block:
        total = None
        for a, b in zip(left, right):
            picked = lax.dynamic_index_in_dim(a, which, 1, keepdims=False)
            term = mm(picked.reshape(groups * rows, -1), b, ((1,), (1 if turned else 0,)))
            total = term if total is None else total + term
        total = sum((piece.astype(f32) for piece in arrived), total.reshape(groups, rows, -1))
        if not pieces:
            return total.astype(bf16)
        parts = [
            lax.dynamic_index_in_dim(total, (group + by) % groups, 0, keepdims=False)
            for by in range(groups)
        ]
        return [parts[0]] + [p.astype(bf16) for p in parts[1:]]
    left_spec = pl.BlockSpec((groups, 1, rows, tokens), lambda n, place: (0, place[0], 0, 0))
    if turned:
        right_spec = pl.BlockSpec((block, tokens), lambda n, _: (n, 0))
    else:
        right_spec = pl.BlockSpec((tokens, block), lambda n, _: (0, n))
    sum_spec = pl.BlockSpec((groups, rows, block), lambda n, _: (0, 0, n))
    operands = [v for pair in zip(left, right) for v in pair] + list(arrived)
    if pieces:
        out_specs = [pl.BlockSpec((rows, block), lambda n, _: (0, n))] * groups
        out_shape = [
            jax.ShapeDtypeStruct((rows, columns), bf16 if by else f32) for by in range(groups)
        ]
        scratch = [pltpu.VMEM((groups, rows, block), f32)]
    else:
        out_specs, scratch = sum_spec, []
        out_shape = jax.ShapeDtypeStruct((groups, rows, columns), bf16)
    return pl.pallas_call(
        functools.partial(gradient_kernel, len(left), turned, pieces),
        grid_spec=pltpu.PrefetchScalarGridSpec(
            num_scalar_prefetch=1,
            grid=(columns // block,),
            in_specs=[left_spec, right_spec] * len(left) + [sum_spec] * len(arrived),
            out_specs=out_specs,
            scratch_shapes=scratch,
        ),
        out_shape=out_shape,
        compiler_params=pltpu.CompilerParams(vmem_limit_bytes=40 << 20),
        cost_estimate=SMALL_COST,
        name="gradient_chip" if arrived else "gradient_send",
    )(jnp.stack([which, group]), *operands)


def gradient_products(left, right, turned=False):
    chips, chip = lax.axis_size("ctx") // 2, lax.axis_index("ctx") // 2
    return [
        gradient_call(left, right, (chip + by) % chips, turned, (), False)
        for by in range(1, chips)
    ]


def gradient_send(products):
    return [chip_shift(p, by) for by, p in enumerate(products, 1)]


def gradient_chip(left, right, arrived, turned=False, pieces=False):
    return gradient_call(left, right, lax.axis_index("ctx") // 2, turned, arrived, pieces)


def gradient_groups(pieces):
    return [group_shift(piece, by) if by else piece for by, piece in enumerate(pieces)]


def gradient_scatter(total):
    groups, rows, columns = total.shape
    return lax.psum_scatter(
        total.reshape(groups * rows, columns), "fsdp", scatter_dimension=0, tiled=True
    )


def gradient_sum(terms):
    total = terms[0].astype(f32)
    for term in terms[1:]:
        total = total + term.astype(f32)
    return total


def gain_gradient(weights, gradients, gain):
    total = 0.0
    for weight, gradient in zip(weights, gradients):
        total = total + jnp.sum(weight.astype(f32) * gradient.astype(f32), axis=1)
    return total / gain


def slot_meta(ctx_index, tokens, stripe_row, lengths):
    count = stripe_row.shape[0]
    ends = jnp.cumsum(lengths)
    residue = jnp.sum(jnp.where(jnp.arange(count) == ctx_index, stripe_row, 0))
    packed = jnp.arange(tokens, dtype=jnp.int32) * count + residue
    passed = (packed[:, None] >= ends[None, :]).astype(jnp.int32)
    start = jnp.sum(passed * lengths[None, :], axis=1)
    return packed, start


def rms_normed(values, gain):
    scale_row = lax.rsqrt(jnp.mean(values * values, axis=-1, keepdims=True) + norm_eps)
    return (values * scale_row * gain, scale_row)


def norm_back(grad_normed, values, scale_row, gain):
    unit_rows = values * scale_row
    weighted = grad_normed * gain
    return scale_row * (weighted - unit_rows * jnp.mean(weighted * unit_rows, axis=-1, keepdims=True))


def on_device(
    hidden_in,
    cotangent,
    doc_lengths,
    stripe,
    query_key_value_weight,
    output_weight,
    feedforward_weight,
    gains,
):
    ctx_count, ctx_index = lax.axis_size("ctx"), lax.axis_index("ctx")
    group_count, group = lax.axis_size("fsdp"), lax.axis_index("fsdp")
    core = ctx_index % 2
    tokens, width = hidden_in.shape[1:]
    qkv_columns = query_key_value_weight.shape[1]
    att_columns = output_weight.shape[1]
    units = feedforward_weight.shape[2]
    kv_heads = qkv_columns // ((QUERY_PER_KV + 2) * HEAD_SIZE)

    def share(weight):
        rows = weight.shape[0] // ctx_count
        return lax.dynamic_slice_in_dim(weight, ctx_index * rows, rows, 0)

    tp_index = lax.axis_index("tp")
    out_share = share(output_weight)
    out_other = tp_swap(out_share)
    payload = packed_share(feedforward_weight, out_share, out_other, ctx_index, share)
    others = lax.all_gather(payload, ("fsdp", "ctx"), axis=0, tiled=True)
    wq, gain_rows = gathered_rows(query_key_value_weight, gains, payload)

    lengths, stripe_row = doc_lengths[0], stripe[0]
    packed, start = slot_meta(ctx_index, tokens, stripe_row, lengths)
    frequency = rope_base ** (-(2.0 * jnp.arange(HALF, dtype=f32)) / HEAD_SIZE)
    angles = frequency[:, None] * (packed - start).astype(f32)[None, :]
    cos_table, sin_table = jnp.cos(angles), jnp.sin(angles)
    block_starts = start[::BLOCK] // (ctx_count * BLOCK)
    sources = []
    for by in range(ctx_count // 2):
        source = (ctx_index - 2 * by) % ctx_count
        sources += [source, source ^ 1]
    stripes = jnp.stack(
        [lax.dynamic_index_in_dim(stripe_row, s, 0, keepdims=False) for s in sources]
    )
    meta = (block_starts, stripes, packed[None, :], start[None, :])

    order = Order(lengths[0] > 0)
    touch = lambda *v: v
    x, grad_low = hidden_in[0], cotangent[0]
    rows_dy = order(rows_for_cores, grad_low, core)

    def first_norm(x, gain):
        values = x.astype(f32)
        scale = lax.rsqrt(jnp.mean(values * values, axis=-1, keepdims=True) + norm_eps)
        return (values * scale * gain).astype(bf16), scale

    first_normed, scale_one = order(first_norm, x, gain_rows[0])
    rows_one = order(rows_for_cores, first_normed, core)
    first_normed, tables, *meta = lax.optimization_barrier(
        (first_normed, (cos_table, sin_table), *meta)
    )
    chunk = kv_heads // CHUNKS
    queries, own, moving, pieces, attended, lse = [], [], [], [], [], []
    for c in range(CHUNKS):
        query, kv_own = order(
            functools.partial(project, first=c * chunk, heads=chunk), first_normed, wq, *tables
        )
        queries.append(query)
        own.append(kv_own)
        moving.append([chip_shift(kv_own, by) for by in range(1, ctx_count // 2)])
    own_swapped = order.apart(swapped_of, *own)
    other_dy, other_one = order.apart(swapped_of, rows_dy[1], rows_one[1])
    left_dy, left_one = (rows_dy[0], other_dy), (rows_one[0], other_one)

    def attend(query, mine, partners, arrived, *meta):
        pieces = [mine, partners]
        for piece in arrived:
            pieces += [piece, core_swap(piece)]
        return attention_forward(query, pieces, *meta), pieces[3::2]

    attended_others = []
    for c in range(CHUNKS):
        (att, lse_c), swapped = order.apart(
            attend, queries[c], own[c], own_swapped[c], moving[c], *meta
        )
        both = [v for pair in zip(moving[c], swapped) for v in pair]
        pieces.append([own[c], own_swapped[c], *both])
        attended.append(att)
        lse.append(lse_c)
        attended_others.append(tp_swap(att.reshape(-1, tokens)))
    attended_rows = [a.reshape(-1, tokens) for a in attended]
    attended_others[0] = order(lambda v: v, attended_others[0])
    all_attended, other_attended = order.apart(
        lambda *parts: (jnp.concatenate(parts, axis=0), core_swap(jnp.concatenate(parts, axis=0))),
        *attended_rows,
    )
    right_att = (all_attended, other_attended)
    middle, second_normed = order(
        functools.partial(middle_of, first=3 * units),
        attended_rows,
        attended_others,
        tp_index,
        x,
        gain_rows[1:],
        others,
    )

    turned_products = functools.partial(gradient_products, turned=True)
    activated, d_gate, d_up, d_two_part = order(
        functools.partial(feed_forward, units=units), second_normed, grad_low, others
    )
    d_two_sent = tp_send(d_two_part)

    def down_part(activated, normed, left_dy, core):
        inner = Order()
        other = core_swap(activated)
        rows = inner(rows_for_cores, normed, core)
        rows_other = core_swap(rows[1])
        return inner(gradient_products, left_dy, (activated, other)), other, (rows[0], rows_other)

    down_products, other_act, left_two = order.apart(
        down_part, activated, second_normed, left_dy, core
    )
    right_act = (activated, other_act)
    down_arrived = gradient_send(down_products)

    def gate_part(activated, d_gate, d_up, left_two, others):
        inner = Order()
        other_gate = core_swap(d_gate)
        down_sum = inner(functools.partial(down_project, first=2 * units), activated, others)
        gate_products = inner(gradient_products, left_two, (d_gate, other_gate))
        other_up = core_swap(lax.optimization_barrier((d_up, down_sum))[0])
        up_products = inner(gradient_products, left_two, (d_up, other_up))
        return gate_products, up_products, down_sum, other_gate, other_up

    gate_products, up_products, down_sum, other_gate, other_up = order.apart(
        gate_part, activated, d_gate, d_up, left_two, others
    )
    right_gate, right_up = (d_gate, other_gate), (d_up, other_up)
    down_arrived, gate_products, down_sum, d_two_sent = order(
        touch, down_arrived, gate_products, down_sum, d_two_sent
    )
    gate_arrived = gradient_send(gate_products)
    down_sent = tp_send(down_sum)
    d_mid, d_branch, d_att = order(
        functools.partial(d_middle_of, first=3 * units, features=att_columns),
        d_two_sent,
        middle,
        grad_low,
        gain_rows[1:],
        others,
    )
    down_scattered = gradient_scatter(order(gradient_chip, left_dy, right_act, down_arrived))
    d_att = d_att.reshape(CHUNKS, chunk, QUERY_PER_KV, HEAD_SIZE, tokens)

    def attend_back(query, d_att, attended, lse, pieces, *meta):
        d_query, *d_pieces = attention_backward(query, d_att, attended, lse, pieces, *meta)
        sums = [
            (mine.astype(f32) + core_swap(partners).astype(f32)).astype(bf16)
            for mine, partners in zip(d_pieces[::2], d_pieces[1::2])
        ]
        return d_query, sums

    def attention_step(c):
        d_query, sums = order.apart(
            attend_back, queries[c], d_att[c], attended[c], lse[c], pieces[c], *meta
        )
        return d_query, [chip_shift(s, -by) if by else s for by, s in enumerate(sums)]

    d_query_0, d_kv_0 = attention_step(0)
    gate_arrived, up_products = order(touch, gate_arrived, up_products)
    up_arrived = gradient_send(up_products)
    gate_scattered = gradient_scatter(order(gradient_chip, left_two, right_gate, gate_arrived))
    d_query_1, d_kv_1 = attention_step(1)

    def branch_part(d_branch, core, right_att):
        inner = Order()
        rows = inner(rows_for_cores, d_branch, core)
        left = (rows[0], core_swap(rows[1]))
        return inner(turned_products, left, right_att), left

    out_products, left_branch = order.apart(branch_part, d_branch, core, right_att)
    out_arrived = gradient_send(out_products)
    d_kv_0, d_kv_1, down_sent = order(touch, d_kv_0, d_kv_1, down_sent)

    def project_back(d_query, d_kv, wq, *tables):
        inner = Order()
        parts = [inner(turned_back, q, kv, *tables) for q, kv in zip(d_query, d_kv)]
        others = [core_swap(p) for p in parts]
        return inner(d_one_of, parts, wq), parts, others

    d_one_part, d_proj, other_proj = order.apart(
        project_back, [d_query_0, d_query_1], [d_kv_0, d_kv_1], wq, *tables
    )
    d_one_sent = tp_send(d_one_part)
    up_scattered = gradient_scatter(order(gradient_chip, left_two, right_up, up_arrived))
    right_proj = list(zip(d_proj, other_proj))
    qkv_arrived = [
        gradient_send(order(turned_products, left_one, right_proj[c])) for c in range(CHUNKS)
    ]
    finish = functools.partial(gradient_chip, turned=True, pieces=True)
    out_terms = gradient_groups(order(finish, left_branch, right_att, out_arrived))
    hidden_out = order(lambda m, s: (m + tp_add(s)).astype(bf16), middle, down_sent)
    qkv_terms = [
        gradient_groups(order(finish, left_one, right_proj[c], qkv_arrived[c]))
        for c in range(CHUNKS)
    ]
    grad_out = order(gradient_sum, out_terms)
    grad_qkv = order(
        lambda *terms: jnp.concatenate([gradient_sum(t) for t in terms], axis=1), *qkv_terms
    )
    own_gains = lax.dynamic_slice_in_dim(
        gains, ctx_index * out_share.shape[0], out_share.shape[0], 1
    ).astype(f32)

    def gain_parts(grad_qkv, grad_gate, grad_up):
        return jnp.stack(
            [
                gain_gradient([share(query_key_value_weight)], [grad_qkv], own_gains[0]),
                gain_gradient(
                    [share(feedforward_weight[i]) for i in range(2)],
                    [grad_gate, grad_up],
                    own_gains[1],
                ),
            ],
            axis=0,
        )

    grad_gains = order(gain_parts, grad_qkv, gate_scattered, up_scattered)
    gains_other = tp_swap(grad_gains)
    grad_ffn = order(
        lambda *parts: jnp.stack(parts, axis=0).astype(f32),
        gate_scattered,
        up_scattered,
        down_scattered,
    )
    grad_gains = order(lambda a, b: a + b, grad_gains, gains_other)
    grad_in = order(input_gradient, d_one_sent, x, d_mid, gain_rows[:1])
    return (hidden_out[None], grad_in[None], grad_qkv, grad_out, grad_ffn, grad_gains)


def solution(mesh):
    return jax.shard_map(
        on_device,
        mesh=mesh,
        in_specs=(
            P("fsdp", "ctx", None),
            P("fsdp", "ctx", None),
            P("fsdp", None),
            P("fsdp", None),
            P("fsdp", "tp"),
            P("fsdp", "tp"),
            P(None, "fsdp", "tp"),
            P(None, "fsdp"),
        ),
        out_specs=(
            P("fsdp", "ctx", None),
            P("fsdp", "ctx", None),
            P(("fsdp", "ctx"), "tp"),
            P(("fsdp", "ctx"), "tp"),
            P(None, ("fsdp", "ctx"), "tp"),
            P(None, ("fsdp", "ctx")),
        ),
        check_vma=False,
    )
```

```python
import functools
import math

import jax
import jax.numpy as jnp
from jax import lax
from jax.experimental import pallas as pl
from jax.experimental.pallas import tpu as pltpu
from jax.sharding import PartitionSpec as P

HEAD_SIZE = 96
QUERY_PER_KV = 2
HALF = HEAD_SIZE // 2
BLOCK = 128
CHUNKS = 2

norm_eps = 1e-05
rope_base = 100000.0
masked_score = -1e30
SCORE_SCALE = HEAD_SIZE ** (-0.5)
SCORE_SCALE_2 = SCORE_SCALE * math.log2(math.e)

SMALL_COST = pl.CostEstimate(flops=1, bytes_accessed=1, transcendentals=0)

bf16 = jnp.bfloat16
f32 = jnp.float32


def mm(a, b, contract=((1,), (0,))):
    return lax.dot_general(a, b, (contract, ((), ())), preferred_element_type=f32)


def fill_keys(heads, count, blocks, kv_refs, kn_ref, kt_ref, vn_ref, vt_ref):
    for h in range(heads):
        for s in range(count):
            for b in range(blocks):
                columns = slice(b * BLOCK, (b + 1) * BLOCK)
                places = slice(s * BLOCK, (s + 1) * BLOCK)
                key = kv_refs[s][h, 0, :, columns]
                value = kv_refs[s][h, 1, :, columns]
                kn_ref[h, b, places, :] = key.T
                if kt_ref is not None:
                    kt_ref[h, b, :, places] = key
                if vn_ref is not None:
                    vn_ref[h, b, places, :] = value.T
                if vt_ref is not None:
                    vt_ref[h, b, :, places] = value


def fill_places(count, stripes_ref, place_ref):
    step = lax.broadcasted_iota(jnp.int32, (BLOCK, QUERY_PER_KV * BLOCK), 0) * count
    for s in range(count):
        place_ref[s * BLOCK : (s + 1) * BLOCK, :] = step + stripes_ref[s]


def twice(row):
    return jnp.concatenate([row] * QUERY_PER_KV, axis=1)


def block_of(ref, h, i):
    columns = slice(i * BLOCK, (i + 1) * BLOCK)
    return jnp.concatenate([ref[h, g, :, columns] for g in range(QUERY_PER_KV)], axis=1)


def allowed_keys(place_ref, count, b, place_q, start_q):
    place, offset = place_ref[...], b * (BLOCK * count)
    allowed = place >= start_q - offset
    return allowed if place_q is None else allowed & (place <= place_q - offset)


def forward_kernel(heads, count, blocks, starts_ref, stripes_ref, place_q_ref, start_q_ref, q_ref, *rest):
    kv_refs = rest[:count]
    o_ref, lse_ref, kn_ref, vt_ref, place_ref = rest[count:]
    fill_keys(heads, count, blocks, kv_refs, kn_ref, None, None, vt_ref)
    fill_places(count, stripes_ref, place_ref)
    for i in range(blocks):
        columns = slice(i * BLOCK, (i + 1) * BLOCK)
        queries = [block_of(q_ref, h, i) for h in range(heads)]
        place_q = twice(place_q_ref[:, columns])
        start_q = twice(start_q_ref[:, columns])

        def scores_of(b, place_q):
            allowed = allowed_keys(place_ref, count, b, place_q, start_q)
            scores = [mm(kn_ref[h, b], queries[h]) for h in range(heads)]
            return [jnp.where(allowed, s * SCORE_SCALE_2, masked_score) for s in scores]

        state = []
        for h, scores in enumerate(scores_of(i, place_q)):
            top = jnp.max(scores, axis=0, keepdims=True)
            weights = jnp.exp2(scores - top)
            total = jnp.sum(weights, axis=0, keepdims=True)
            state.append((top, total, mm(vt_ref[h, i], weights.astype(bf16))))

        def step(b, carry):
            result = []
            for h, scores in enumerate(scores_of(b, None)):
                top, total, accum = carry[h]
                new_top = jnp.maximum(top, jnp.max(scores, axis=0, keepdims=True))
                fade = jnp.exp2(top - new_top)
                weights = jnp.exp2(scores - new_top)
                total = total * fade + jnp.sum(weights, axis=0, keepdims=True)
                accum = accum * fade + mm(vt_ref[h, b], weights.astype(bf16))
                result.append((new_top, total, accum))
            return tuple(result)

        state = lax.fori_loop(starts_ref[i], i, step, tuple(state)) if i else state
        for h, (top, total, accum) in enumerate(state):
            result = (accum / total).astype(bf16)
            lse = top + jnp.log2(total)
            for g in range(QUERY_PER_KV):
                part = slice(g * BLOCK, (g + 1) * BLOCK)
                o_ref[h, g, :, columns] = result[:, part]
                lse_ref[h, g : g + 1, columns] = lse[:, part]


def backward_kernel(
    heads, count, blocks, starts_ref, stripes_ref, place_q_ref, start_q_ref, q_ref, do_ref, o_ref, lse_ref, *rest
):
    kv_refs = rest[:count]
    dq_ref = rest[count]
    dkv_refs = rest[count + 1 : 2 * count + 1]
    kn_ref, kt_ref, vn_ref, place_ref, dk_ref, dv_ref = rest[2 * count + 1 :]
    fill_keys(heads, count, blocks, kv_refs, kn_ref, kt_ref, vn_ref, None)
    fill_places(count, stripes_ref, place_ref)
    for i in range(blocks):
        columns = slice(i * BLOCK, (i + 1) * BLOCK)
        place_q = twice(place_q_ref[:, columns])
        start_q = twice(start_q_ref[:, columns])
        parts = []
        for h in range(heads):
            query, d_out, out = (block_of(ref, h, i) for ref in (q_ref, do_ref, o_ref))
            delta = jnp.sum(d_out.astype(f32) * out.astype(f32), axis=0, keepdims=True)
            lse = jnp.concatenate(
                [lse_ref[h, g : g + 1, columns] for g in range(QUERY_PER_KV)], axis=1
            )
            parts.append((query, query.T, d_out, d_out.T, delta, lse))

        def terms(b, place_q, first):
            allowed = allowed_keys(place_ref, count, b, place_q, start_q)
            d_queries = []
            for h, (query, query_rows, d_out, d_out_rows, delta, lse) in enumerate(parts):
                scores = mm(kn_ref[h, b], query)
                d_prob = mm(vn_ref[h, b], d_out)
                probs = jnp.exp2(jnp.where(allowed, scores * SCORE_SCALE_2, masked_score) - lse)
                d_score = (probs * (d_prob - delta)).astype(bf16)
                d_value = mm(probs.astype(bf16), d_out_rows)
                d_key = mm(d_score, query_rows)
                if first:
                    dv_ref[h, b] = d_value
                    dk_ref[h, b] = d_key
                else:
                    dv_ref[h, b] += d_value
                    dk_ref[h, b] += d_key
                d_queries.append(mm(kt_ref[h, b], d_score))
            return d_queries

        def step(b, carry):
            return tuple(a + t for a, t in zip(carry, terms(b, None, False)))

        d_queries = tuple(terms(i, place_q, True))
        if i:
            d_queries = lax.fori_loop(starts_ref[i], i, step, d_queries)
        for h in range(heads):
            for g in range(QUERY_PER_KV):
                dq_ref[h, g, :, columns] = d_queries[h][:, g * BLOCK : (g + 1) * BLOCK] * SCORE_SCALE
    for h in range(heads):
        for s in range(count):
            places = slice(s * BLOCK, (s + 1) * BLOCK)
            for b in range(blocks):
                columns = slice(b * BLOCK, (b + 1) * BLOCK)
                dkv_refs[s][h, 0, :, columns] = (dk_ref[h, b, places, :] * SCORE_SCALE).T.astype(bf16)
                dkv_refs[s][h, 1, :, columns] = dv_ref[h, b, places, :].T.astype(bf16)


def head_spec(heads, *dims):
    return pl.BlockSpec((heads, *dims), lambda n, *_: (0,) * (1 + len(dims)))


def row_spec(tokens):
    return pl.BlockSpec((1, tokens), lambda n, *_: (0, 0))


def attention_forward(queries, pieces, starts, stripes, place, start):
    heads, _, _, tokens = queries.shape
    count, blocks = len(pieces), tokens // BLOCK
    keys = count * BLOCK
    per_query = head_spec(heads, QUERY_PER_KV, HEAD_SIZE, tokens)
    per_kv = head_spec(heads, 2, HEAD_SIZE, tokens)
    return pl.pallas_call(
        functools.partial(forward_kernel, heads, count, blocks),
        grid_spec=pltpu.PrefetchScalarGridSpec(
            num_scalar_prefetch=2,
            grid=(1,),
            in_specs=[row_spec(tokens)] * 2 + [per_query] + [per_kv] * count,
            out_specs=[per_query, head_spec(heads, QUERY_PER_KV, tokens)],
            scratch_shapes=[
                pltpu.VMEM((heads, blocks, keys, HEAD_SIZE), bf16),
                pltpu.VMEM((heads, blocks, HEAD_SIZE, keys), bf16),
                pltpu.VMEM((keys, QUERY_PER_KV * BLOCK), jnp.int32),
            ],
        ),
        out_shape=[
            jax.ShapeDtypeStruct(queries.shape, bf16),
            jax.ShapeDtypeStruct((heads, QUERY_PER_KV, tokens), f32),
        ],
        compiler_params=pltpu.CompilerParams(vmem_limit_bytes=40 << 20),
        cost_estimate=SMALL_COST,
        name="attention_forward",
    )(starts, stripes, place, start, queries, *pieces)


def attention_backward(queries, d_att, attended, lse, pieces, starts, stripes, place, start):
    heads, _, _, tokens = queries.shape
    count, blocks = len(pieces), tokens // BLOCK
    keys = count * BLOCK
    per_query = head_spec(heads, QUERY_PER_KV, HEAD_SIZE, tokens)
    per_kv = head_spec(heads, 2, HEAD_SIZE, tokens)
    return pl.pallas_call(
        functools.partial(backward_kernel, heads, count, blocks),
        grid_spec=pltpu.PrefetchScalarGridSpec(
            num_scalar_prefetch=2,
            grid=(1,),
            in_specs=[row_spec(tokens)] * 2
            + [per_query] * 3
            + [head_spec(heads, QUERY_PER_KV, tokens)]
            + [per_kv] * count,
            out_specs=[per_query] + [per_kv] * count,
            scratch_shapes=[
                pltpu.VMEM((heads, blocks, keys, HEAD_SIZE), bf16),
                pltpu.VMEM((heads, blocks, HEAD_SIZE, keys), bf16),
                pltpu.VMEM((heads, blocks, keys, HEAD_SIZE), bf16),
                pltpu.VMEM((keys, QUERY_PER_KV * BLOCK), jnp.int32),
                pltpu.VMEM((heads, blocks, keys, HEAD_SIZE), f32),
                pltpu.VMEM((heads, blocks, keys, HEAD_SIZE), f32),
            ],
        ),
        out_shape=[jax.ShapeDtypeStruct(queries.shape, f32)]
        + [jax.ShapeDtypeStruct(pieces[0].shape, bf16)] * count,
        compiler_params=pltpu.CompilerParams(vmem_limit_bytes=48 << 20),
        cost_estimate=SMALL_COST,
        name="attention_backward",
    )(starts, stripes, place, start, queries, d_att, attended, lse, *pieces)


def pack_kernel(_, ffn_ref, out_ref, other_ref, packed_ref):
    units, columns = ffn_ref.shape[2], out_ref.shape[1]
    for i in range(3):
        packed_ref[:, i * units : (i + 1) * units] = ffn_ref[i]
    packed_ref[:, 3 * units : 3 * units + columns] = out_ref[...]
    packed_ref[:, 3 * units + columns :] = other_ref[...]


def packed_share(feedforward_weight, out_share, out_other, index, share_of):
    rows, columns = out_share.shape
    units = feedforward_weight.shape[2]
    if rows % 16:
        parts = [share_of(feedforward_weight[i]) for i in range(3)]
        return jnp.concatenate([*parts, out_share, out_other], axis=1)
    whole = pl.BlockSpec((rows, columns), lambda n, _: (0, 0))
    width = 3 * units + 2 * columns
    return pl.pallas_call(
        pack_kernel,
        grid_spec=pltpu.PrefetchScalarGridSpec(
            num_scalar_prefetch=1,
            grid=(1,),
            in_specs=[
                pl.BlockSpec((3, rows, units), lambda n, place: (0, place[0], 0)),
                whole,
                whole,
            ],
            out_specs=pl.BlockSpec((rows, width), lambda n, _: (0, 0)),
        ),
        out_shape=jax.ShapeDtypeStruct((rows, width), bf16),
        compiler_params=pltpu.CompilerParams(vmem_limit_bytes=60 << 20),
        cost_estimate=SMALL_COST,
        name="pack",
    )(index[None], feedforward_weight, out_share, out_other)


def input_gradient_kernel(mine_ref, other_ref, x_ref, d_mid_ref, gain_ref, out_ref):
    x = x_ref[...].astype(f32)
    scale = lax.rsqrt(jnp.mean(x * x, axis=-1, keepdims=True) + norm_eps)
    unit = x * scale
    weighted = (mine_ref[...].astype(f32) + other_ref[...].astype(f32)) * gain_ref[...]
    out_ref[...] = (
        d_mid_ref[...]
        + scale * (weighted - unit * jnp.mean(weighted * unit, axis=-1, keepdims=True))
    ).astype(bf16)


def input_gradient(sent, x, d_mid, gain):
    tokens, width = x.shape
    block = 256
    here = pl.BlockSpec((block, width), lambda n: (n, 0))
    return pl.pallas_call(
        input_gradient_kernel,
        grid=(tokens // block,),
        in_specs=[here] * 4 + [pl.BlockSpec((1, width), lambda n: (0, 0))],
        out_specs=here,
        out_shape=jax.ShapeDtypeStruct((tokens, width), bf16),
        compiler_params=pltpu.CompilerParams(vmem_limit_bytes=32 << 20),
        cost_estimate=SMALL_COST,
        name="input_gradient",
    )(*sent, x, d_mid, gain)


def project_kernel(x_ref, w_ref, cos_ref, sin_ref, q_ref, kv_ref):
    projected = mm(x_ref[...], w_ref[...]).T
    cos_table, sin_table = cos_ref[...], sin_ref[...]
    for j in range(QUERY_PER_KV + 1):
        first = j * HEAD_SIZE
        front = projected[first : first + HALF]
        back = projected[first + HALF : first + HEAD_SIZE]
        target = q_ref.at[0, j] if j < QUERY_PER_KV else kv_ref.at[0, 0]
        target[:HALF, :] = (front * cos_table - back * sin_table).astype(bf16)
        target[HALF:, :] = (back * cos_table + front * sin_table).astype(bf16)
    kv_ref[0, 1] = projected[(QUERY_PER_KV + 1) * HEAD_SIZE :].astype(bf16)


def project(normed, weight, cos_table, sin_table, first, heads):
    tokens, width = normed.shape
    columns = (QUERY_PER_KV + 2) * HEAD_SIZE
    whole = lambda shape: pl.BlockSpec(shape, lambda h: (0, 0))
    return pl.pallas_call(
        project_kernel,
        grid=(heads,),
        in_specs=[
            whole((tokens, width)),
            pl.BlockSpec((width, columns), lambda h: (0, first + h)),
            whole((HALF, tokens)),
            whole((HALF, tokens)),
        ],
        out_specs=[
            pl.BlockSpec((1, QUERY_PER_KV, HEAD_SIZE, tokens), lambda h: (h, 0, 0, 0)),
            pl.BlockSpec((1, 2, HEAD_SIZE, tokens), lambda h: (h, 0, 0, 0)),
        ],
        out_shape=[
            jax.ShapeDtypeStruct((heads, QUERY_PER_KV, HEAD_SIZE, tokens), bf16),
            jax.ShapeDtypeStruct((heads, 2, HEAD_SIZE, tokens), bf16),
        ],
        compiler_params=pltpu.CompilerParams(vmem_limit_bytes=40 << 20),
        cost_estimate=SMALL_COST,
        name="project",
    )(normed, weight, cos_table, sin_table)


def middle_kernel(count, tp_ref, x_ref, gain_ref, *refs):
    mine, others = refs[:count], refs[count : 2 * count]
    w_first, w_second, middle_ref, normed_ref, first_ref, second_ref = refs[2 * count :]

    def fill(first, second):
        first_ref[...] = jnp.concatenate([r[...] for r in first], axis=0).T
        second_ref[...] = jnp.concatenate([r[...] for r in second], axis=0).T

    @pl.when(tp_ref[0] == 0)
    def _():
        fill(mine, others)

    @pl.when(tp_ref[0] == 1)
    def _():
        fill(others, mine)

    branch = mm(first_ref[...], w_first[...], ((1,), (1,))) + mm(
        second_ref[...], w_second[...], ((1,), (1,))
    )
    middle = x_ref[...].astype(f32) + branch
    middle_ref[...] = middle
    scale = lax.rsqrt(jnp.mean(middle * middle, axis=-1, keepdims=True) + norm_eps)
    normed_ref[...] = (middle * scale * gain_ref[...]).astype(bf16)


def middle_of(mine, others, tp_index, x, gain, weight, first):
    tokens, width = x.shape
    features = sum(p.shape[0] for p in mine)
    block = 256
    half = first // features
    token_spec = pl.BlockSpec((block, width), lambda n, _: (n, 0))
    return pl.pallas_call(
        functools.partial(middle_kernel, len(mine)),
        grid_spec=pltpu.PrefetchScalarGridSpec(
            num_scalar_prefetch=1,
            grid=(tokens // block,),
            in_specs=[token_spec, pl.BlockSpec((1, width), lambda n, _: (0, 0))]
            + [pl.BlockSpec((p.shape[0], block), lambda n, _: (0, n)) for p in (*mine, *others)]
            + [
                pl.BlockSpec((width, features), lambda n, tp: (0, half + tp[0])),
                pl.BlockSpec((width, features), lambda n, tp: (0, half + 1 - tp[0])),
            ],
            out_specs=[token_spec] * 2,
            scratch_shapes=[pltpu.VMEM((block, features), bf16)] * 2,
        ),
        out_shape=[
            jax.ShapeDtypeStruct((tokens, width), f32),
            jax.ShapeDtypeStruct((tokens, width), bf16),
        ],
        compiler_params=pltpu.CompilerParams(vmem_limit_bytes=40 << 20),
        cost_estimate=SMALL_COST,
        name="middle",
    )(tp_index[None], x, gain, *mine, *others, weight, weight)


def down_kernel(a_ref, w_ref, out_ref):
    out_ref[...] = mm(a_ref[...], w_ref[...], ((1,), (1,))).astype(bf16)


def down_project(activated, weight, first):
    tokens, units = activated.shape
    width, block = weight.shape[0], 512
    return pl.pallas_call(
        down_kernel,
        grid=(width // block,),
        in_specs=[
            pl.BlockSpec((tokens, units), lambda n: (0, 0)),
            pl.BlockSpec((block, units), lambda n: (n, first // units)),
        ],
        out_specs=pl.BlockSpec((tokens, block), lambda n: (0, n)),
        out_shape=jax.ShapeDtypeStruct((tokens, width), bf16),
        compiler_params=pltpu.CompilerParams(vmem_limit_bytes=40 << 20),
        cost_estimate=SMALL_COST,
        name="down_project",
    )(activated, weight)


def d_middle_kernel(
    mine_ref, other_ref, middle_ref, dy_ref, gain_ref, w_ref, d_mid_ref, branch_ref, d_att_ref
):
    middle = middle_ref[...]
    scale = lax.rsqrt(jnp.mean(middle * middle, axis=-1, keepdims=True) + norm_eps)
    unit = middle * scale
    weighted = (mine_ref[...].astype(f32) + other_ref[...].astype(f32)) * gain_ref[...]
    d_mid = dy_ref[...].astype(f32) + scale * (
        weighted - unit * jnp.mean(weighted * unit, axis=-1, keepdims=True)
    )
    d_mid_ref[...] = d_mid
    branch = d_mid.astype(bf16)
    branch_ref[...] = branch
    d_att_ref[...] = mm(branch, w_ref[...]).astype(bf16).T


def d_middle_of(sent, middle, d_out, gain, weight, first, features):
    mine, other = sent
    tokens, width = middle.shape
    block = 256
    here = pl.BlockSpec((block, width), lambda n: (n, 0))
    row = pl.BlockSpec((1, width), lambda n: (0, 0))
    return pl.pallas_call(
        d_middle_kernel,
        grid=(tokens // block,),
        in_specs=[here, here, here, here, row]
        + [pl.BlockSpec((width, features), lambda n: (0, first // features))],
        out_specs=[here, here, pl.BlockSpec((features, block), lambda n: (0, n))],
        out_shape=[
            jax.ShapeDtypeStruct((tokens, width), f32),
            jax.ShapeDtypeStruct((tokens, width), bf16),
            jax.ShapeDtypeStruct((features, tokens), bf16),
        ],
        compiler_params=pltpu.CompilerParams(vmem_limit_bytes=48 << 20),
        cost_estimate=SMALL_COST,
        name="d_middle",
    )(mine, other, middle, d_out, gain, weight)


def turn_back_kernel(cos_ref, sin_ref, dq_ref, *refs):
    kv_refs, out_ref = refs[:-1], refs[-1]
    cos_table, sin_table = cos_ref[...], sin_ref[...]
    total = kv_refs[0][0].astype(f32)
    for ref in kv_refs[1:]:
        total = total + ref[0].astype(f32)
    for j in range(QUERY_PER_KV + 1):
        vector = dq_ref[0, j] if j < QUERY_PER_KV else total[0]
        front, back = vector[:HALF], vector[HALF:]
        first = j * HEAD_SIZE
        out_ref[first : first + HALF, :] = (front * cos_table + back * sin_table).astype(bf16)
        out_ref[first + HALF : first + HEAD_SIZE, :] = (
            back * cos_table - front * sin_table
        ).astype(bf16)
    out_ref[(QUERY_PER_KV + 1) * HEAD_SIZE :, :] = total[1].astype(bf16)


def turned_back(d_query, d_kv_terms, cos_table, sin_table):
    heads, _, _, tokens = d_query.shape
    columns = (QUERY_PER_KV + 2) * HEAD_SIZE
    whole = pl.BlockSpec((HALF, tokens), lambda h: (0, 0))
    head = lambda n: pl.BlockSpec((1, n, HEAD_SIZE, tokens), lambda h: (h, 0, 0, 0))
    return pl.pallas_call(
        turn_back_kernel,
        grid=(heads,),
        in_specs=[whole, whole, head(QUERY_PER_KV)] + [head(2)] * len(d_kv_terms),
        out_specs=pl.BlockSpec((columns, tokens), lambda h: (h, 0)),
        out_shape=jax.ShapeDtypeStruct((heads * columns, tokens), bf16),
        compiler_params=pltpu.CompilerParams(vmem_limit_bytes=32 << 20),
        cost_estimate=SMALL_COST,
        name="turn_back",
    )(cos_table, sin_table, d_query, *d_kv_terms)


def d_one_kernel(count, *refs):
    parts, w_ref, out_ref, rows_ref = refs[:count], refs[count], refs[count + 1], refs[count + 2]

    @pl.when(pl.program_id(0) == 0)
    def _():
        first = 0
        for part in parts:
            columns = part.shape[0]
            rows_ref[:, first : first + columns] = part[...].T
            first += columns

    out_ref[...] = mm(rows_ref[...], w_ref[...], ((1,), (1,))).astype(bf16)


def d_one_of(parts, weight):
    width, columns = weight.shape
    tokens, block = parts[0].shape[1], 512
    return pl.pallas_call(
        functools.partial(d_one_kernel, len(parts)),
        grid=(width // block,),
        in_specs=[pl.BlockSpec(p.shape, lambda n: (0, 0)) for p in parts]
        + [pl.BlockSpec((block, columns), lambda n: (n, 0))],
        out_specs=pl.BlockSpec((tokens, block), lambda n: (0, n)),
        out_shape=jax.ShapeDtypeStruct((tokens, width), bf16),
        scratch_shapes=[pltpu.VMEM((tokens, columns), bf16)],
        compiler_params=pltpu.CompilerParams(vmem_limit_bytes=40 << 20),
        cost_estimate=SMALL_COST,
        name="d_one",
    )(*parts, weight)


def ffn_kernel(
    h_ref, dy_ref, wg_ref, wu_ref, wd_ref, act_ref, dg_ref, du_ref, out_ref, acc_ref
):
    step = pl.program_id(0)
    w_gate, w_up = wg_ref[...], wu_ref[...]
    gate = mm(h_ref[...], w_gate)
    up = mm(h_ref[...], w_up)
    d_act = mm(dy_ref[...], wd_ref[...])
    sigmoid_gate = jax.nn.sigmoid(gate)
    silu_gate = gate * sigmoid_gate
    act_ref[...] = (silu_gate * up).astype(bf16)
    d_gate = (d_act * up * sigmoid_gate * (1.0 + gate * (1.0 - sigmoid_gate))).astype(bf16)
    d_up = (d_act * silu_gate).astype(bf16)
    dg_ref[...] = d_gate
    du_ref[...] = d_up
    term = mm(d_gate, w_gate, ((1,), (1,))) + mm(d_up, w_up, ((1,), (1,)))

    @pl.when(step == 0)
    def _():
        acc_ref[...] = term

    @pl.when(step > 0)
    def _():
        acc_ref[...] += term

    @pl.when(step == pl.num_programs(0) - 1)
    def _():
        out_ref[...] = acc_ref[...].astype(bf16)


FFN_BLOCK = 512


def feed_forward(normed, d_out, weights, units):
    tokens, width = normed.shape
    weight_spec = lambda i: pl.BlockSpec(
        (width, FFN_BLOCK), lambda n: (0, i * units // FFN_BLOCK + n)
    )
    column_spec = pl.BlockSpec((tokens, FFN_BLOCK), lambda n: (0, n))
    whole = pl.BlockSpec((tokens, width), lambda n: (0, 0))
    return pl.pallas_call(
        ffn_kernel,
        grid=(units // FFN_BLOCK,),
        in_specs=[whole, whole] + [weight_spec(i) for i in range(3)],
        out_specs=[column_spec] * 3 + [whole],
        out_shape=[jax.ShapeDtypeStruct((tokens, units), bf16)] * 3
        + [jax.ShapeDtypeStruct((tokens, width), bf16)],
        scratch_shapes=[pltpu.VMEM((tokens, width), f32)],
        compiler_params=pltpu.CompilerParams(vmem_limit_bytes=56 << 20),
        cost_estimate=SMALL_COST,
        name="feed_forward",
    )(normed, d_out, weights, weights, weights)


def turn_kernel(chips, rows, core_ref, x_ref, mine_ref, other_ref, turned_ref):
    turned_ref[...] = x_ref[...].T
    core = core_ref[0]
    for chip in range(chips):
        for ref, which in ((mine_ref, core), (other_ref, 1 - core)):
            first = pl.multiple_of((chip * 2 + which) * rows, 16)
            ref[0, chip] = turned_ref[pl.ds(first, rows), :]


def rows_for_cores(activation, core):
    tokens, width = activation.shape
    groups, chips = lax.axis_size("fsdp"), lax.axis_size("ctx") // 2
    rows = width // (groups * chips * 2)
    shape = (groups, chips, rows, tokens)
    if rows % 16 or (width // groups) % 128:
        turned = activation.T.reshape(groups, chips, 2, rows, tokens)
        return tuple(
            lax.dynamic_index_in_dim(turned, c, 2, keepdims=False) for c in (core, 1 - core)
        )
    spec = pl.BlockSpec((1, chips, rows, tokens), lambda g, _: (g, 0, 0, 0))
    return pl.pallas_call(
        functools.partial(turn_kernel, chips, rows),
        grid_spec=pltpu.PrefetchScalarGridSpec(
            num_scalar_prefetch=1,
            grid=(groups,),
            in_specs=[pl.BlockSpec((tokens, width // groups), lambda g, _: (0, g))],
            out_specs=[spec, spec],
            scratch_shapes=[pltpu.VMEM((width // groups, tokens), bf16)],
        ),
        out_shape=[jax.ShapeDtypeStruct(shape, bf16)] * 2,
        compiler_params=pltpu.CompilerParams(vmem_limit_bytes=32 << 20),
        cost_estimate=SMALL_COST,
        name="turn_rows",
    )(core[None], activation)


class Order:
    def __init__(self, always=None):
        self.last = ()
        self.always = always

    def __call__(self, function, *args):
        leaves, tree = jax.tree.flatten(args)
        held = lax.optimization_barrier((*leaves, *self.last))
        result = function(*jax.tree.unflatten(tree, held[: len(leaves)]))
        self.last = (jax.tree.leaves(result)[0],)
        return result

    def apart(self, function, *args):
        def guarded(*args):
            shapes = jax.eval_shape(function, *args)
            nothing = lambda *_: jax.tree.map(lambda s: jnp.zeros(s.shape, s.dtype), shapes)
            return lax.cond(self.always, function, nothing, *args)

        return self(guarded, *args)


def swapped_of(*values):
    return [core_swap(v) for v in values]


def core_swap(value):
    size = lax.axis_size("ctx")
    return lax.ppermute(value, "ctx", [(i, i ^ 1) for i in range(size)])


def chip_shift(value, by):
    size = lax.axis_size("ctx")
    return lax.ppermute(value, "ctx", [(i, (i + 2 * by) % size) for i in range(size)])


def group_shift(value, by):
    size = lax.axis_size("fsdp")
    return lax.ppermute(value, "fsdp", [(i, (i + by) % size) for i in range(size)])


def tp_swap(value):
    return lax.ppermute(value, "tp", [(0, 1), (1, 0)])


def tp_send(part):
    part = lax.optimization_barrier(part)
    return part, tp_swap(part)


def tp_add(sent):
    mine, other = sent
    return mine.astype(f32) + other.astype(f32)


def both_cores(value):
    return value, core_swap(value)


def gathered_rows(weight, gains, hold):
    groups, count = lax.axis_size("fsdp"), lax.axis_size("ctx")
    group, index = lax.axis_index("fsdp"), lax.axis_index("ctx")
    rows, columns = weight.shape
    share = rows // count
    mine = lax.dynamic_slice_in_dim(weight, index * share, share, 0)
    extra = jnp.pad(gains, ((0, 16 - gains.shape[0]), (0, columns - gains.shape[1])))
    mine = jnp.concatenate([mine, extra], axis=0)
    fetched = [group_shift(mine, by) for by in range(1, groups)]
    stack = jnp.stack([gains] + [p[share : share + 2, : gains.shape[1]] for p in fetched], axis=0)
    all_gains = jnp.concatenate(
        [
            lax.dynamic_index_in_dim(stack, (group - i) % groups, 0, keepdims=False)
            for i in range(groups)
        ],
        axis=1,
    ).astype(f32)
    weight, _ = lax.optimization_barrier((weight, hold))
    whole = jnp.zeros((groups * rows, columns), weight.dtype)
    whole = lax.dynamic_update_slice_in_dim(whole, weight, group * rows, 0)
    pieces = jnp.stack([p[:share] for p in fetched], axis=0)

    def placed(whole, pieces, source):
        for by in range(1, groups):
            first = (group - by) % groups * rows + source * share
            whole = lax.dynamic_update_slice_in_dim(whole, pieces[by - 1], first, 0)
        return whole

    passed = [pieces] + [chip_shift(pieces, by) for by in range(1, count // 2)]
    for by, moved in enumerate(passed):
        source = (index - 2 * by) % count
        whole = placed(whole, moved, source)
        whole = placed(whole, core_swap(moved), source ^ 1)
    return whole, all_gains, fetched


def gradient_kernel(pairs, turned, pieces, place_ref, *refs):
    total = None
    for i in range(pairs):
        left, right = refs[2 * i], refs[2 * i + 1]
        groups, _, rows, tokens = left.shape
        term = mm(
            left[...].reshape(groups * rows, tokens), right[...], ((1,), (1 if turned else 0,))
        )
        total = term if total is None else total + term
    total = total.reshape(groups, rows, total.shape[-1])
    refs = refs[2 * pairs :]
    arrived = refs[: -1 if not pieces else -1 - groups]
    for piece in arrived:
        total = total + piece[...].astype(f32)
    if not pieces:
        refs[-1][...] = total.astype(bf16)
        return
    outs, sum_ref = refs[-1 - groups : -1], refs[-1]
    sum_ref[...] = total
    group = place_ref[1]
    for by, out in enumerate(outs):
        out[...] = sum_ref[lax.rem(group + by, groups)].astype(out.dtype)


def gradient_call(left, right, which, turned, arrived, pieces):
    groups, chips, rows, tokens = left[0].shape
    group = lax.axis_index("fsdp")
    columns = right[0].shape[0 if turned else 1]
    block = next((b for b in (512, 384) if columns % b == 0), columns)
    if rows % 16 or columns % block:
        total = None
        for a, b in zip(left, right):
            picked = lax.dynamic_index_in_dim(a, which, 1, keepdims=False)
            term = mm(picked.reshape(groups * rows, -1), b, ((1,), (1 if turned else 0,)))
            total = term if total is None else total + term
        total = sum((piece.astype(f32) for piece in arrived), total.reshape(groups, rows, -1))
        if not pieces:
            return total.astype(bf16)
        parts = [
            lax.dynamic_index_in_dim(total, (group + by) % groups, 0, keepdims=False)
            for by in range(groups)
        ]
        return [parts[0]] + [p.astype(bf16) for p in parts[1:]]
    left_spec = pl.BlockSpec((groups, 1, rows, tokens), lambda n, place: (0, place[0], 0, 0))
    if turned:
        right_spec = pl.BlockSpec((block, tokens), lambda n, _: (n, 0))
    else:
        right_spec = pl.BlockSpec((tokens, block), lambda n, _: (0, n))
    sum_spec = pl.BlockSpec((groups, rows, block), lambda n, _: (0, 0, n))
    operands = [v for pair in zip(left, right) for v in pair] + list(arrived)
    if pieces:
        out_specs = [pl.BlockSpec((rows, block), lambda n, _: (0, n))] * groups
        out_shape = [
            jax.ShapeDtypeStruct((rows, columns), bf16 if by else f32) for by in range(groups)
        ]
        scratch = [pltpu.VMEM((groups, rows, block), f32)]
    else:
        out_specs, scratch = sum_spec, []
        out_shape = jax.ShapeDtypeStruct((groups, rows, columns), bf16)
    return pl.pallas_call(
        functools.partial(gradient_kernel, len(left), turned, pieces),
        grid_spec=pltpu.PrefetchScalarGridSpec(
            num_scalar_prefetch=1,
            grid=(columns // block,),
            in_specs=[left_spec, right_spec] * len(left) + [sum_spec] * len(arrived),
            out_specs=out_specs,
            scratch_shapes=scratch,
        ),
        out_shape=out_shape,
        compiler_params=pltpu.CompilerParams(vmem_limit_bytes=40 << 20),
        cost_estimate=SMALL_COST,
        name="gradient_chip" if arrived else "gradient_send",
    )(jnp.stack([which, group]), *operands)


def gradient_products(left, right, turned=False):
    chips, chip = lax.axis_size("ctx") // 2, lax.axis_index("ctx") // 2
    return [
        gradient_call(left, right, (chip + by) % chips, turned, (), False)
        for by in range(1, chips)
    ]


def gradient_send(products):
    return [chip_shift(p, by) for by, p in enumerate(products, 1)]


def gradient_chip(left, right, arrived, turned=False, pieces=False):
    return gradient_call(left, right, lax.axis_index("ctx") // 2, turned, arrived, pieces)


def gradient_groups(pieces):
    return [group_shift(piece, by) if by else piece for by, piece in enumerate(pieces)]


def gradient_scatter(total):
    groups, rows, columns = total.shape
    return lax.psum_scatter(
        total.reshape(groups * rows, columns), "fsdp", scatter_dimension=0, tiled=True
    )


def gradient_sum(terms):
    total = terms[0].astype(f32)
    for term in terms[1:]:
        total = total + term.astype(f32)
    return total


def gain_gradient(weights, gradients, gain):
    total = 0.0
    for weight, gradient in zip(weights, gradients):
        total = total + jnp.sum(weight.astype(f32) * gradient.astype(f32), axis=1)
    return total / gain


def slot_meta(ctx_index, tokens, stripe_row, lengths):
    count = stripe_row.shape[0]
    ends = jnp.cumsum(lengths)
    residue = jnp.sum(jnp.where(jnp.arange(count) == ctx_index, stripe_row, 0))
    packed = jnp.arange(tokens, dtype=jnp.int32) * count + residue
    passed = (packed[:, None] >= ends[None, :]).astype(jnp.int32)
    start = jnp.sum(passed * lengths[None, :], axis=1)
    return packed, start


def rms_normed(values, gain):
    scale_row = lax.rsqrt(jnp.mean(values * values, axis=-1, keepdims=True) + norm_eps)
    return (values * scale_row * gain, scale_row)


def norm_back(grad_normed, values, scale_row, gain):
    unit_rows = values * scale_row
    weighted = grad_normed * gain
    return scale_row * (weighted - unit_rows * jnp.mean(weighted * unit_rows, axis=-1, keepdims=True))


def on_device(
    hidden_in,
    cotangent,
    doc_lengths,
    stripe,
    query_key_value_weight,
    output_weight,
    feedforward_weight,
    gains,
):
    ctx_count, ctx_index = lax.axis_size("ctx"), lax.axis_index("ctx")
    group_count, group = lax.axis_size("fsdp"), lax.axis_index("fsdp")
    core = ctx_index % 2
    tokens, width = hidden_in.shape[1:]
    qkv_columns = query_key_value_weight.shape[1]
    att_columns = output_weight.shape[1]
    units = feedforward_weight.shape[2]
    kv_heads = qkv_columns // ((QUERY_PER_KV + 2) * HEAD_SIZE)

    def share(weight):
        rows = weight.shape[0] // ctx_count
        return lax.dynamic_slice_in_dim(weight, ctx_index * rows, rows, 0)

    tp_index = lax.axis_index("tp")
    out_share = share(output_weight)
    out_other = tp_swap(out_share)
    payload = packed_share(feedforward_weight, out_share, out_other, ctx_index, share)
    wq, gain_rows, fetched = gathered_rows(query_key_value_weight, gains, payload)
    payload = lax.optimization_barrier((payload, fetched[0]))[0]
    others = lax.all_gather(payload, ("fsdp", "ctx"), axis=0, tiled=True)

    lengths, stripe_row = doc_lengths[0], stripe[0]
    packed, start = slot_meta(ctx_index, tokens, stripe_row, lengths)
    frequency = rope_base ** (-(2.0 * jnp.arange(HALF, dtype=f32)) / HEAD_SIZE)
    angles = frequency[:, None] * (packed - start).astype(f32)[None, :]
    cos_table, sin_table = jnp.cos(angles), jnp.sin(angles)
    block_starts = start[::BLOCK] // (ctx_count * BLOCK)
    sources = []
    for by in range(ctx_count // 2):
        source = (ctx_index - 2 * by) % ctx_count
        sources += [source, source ^ 1]
    stripes = jnp.stack(
        [lax.dynamic_index_in_dim(stripe_row, s, 0, keepdims=False) for s in sources]
    )
    meta = (block_starts, stripes, packed[None, :], start[None, :])

    order = Order(lengths[0] > 0)
    touch = lambda *v: v
    x, grad_low = hidden_in[0], cotangent[0]
    rows_dy = order(rows_for_cores, grad_low, core)

    def first_norm(x, gain):
        values = x.astype(f32)
        scale = lax.rsqrt(jnp.mean(values * values, axis=-1, keepdims=True) + norm_eps)
        return (values * scale * gain).astype(bf16), scale

    first_normed, scale_one = order(first_norm, x, gain_rows[0])
    rows_one = order(rows_for_cores, first_normed, core)
    first_normed, tables, *meta = lax.optimization_barrier(
        (first_normed, (cos_table, sin_table), *meta)
    )
    chunk = kv_heads // CHUNKS
    queries, own, moving, pieces, attended, lse = [], [], [], [], [], []
    for c in range(CHUNKS):
        query, kv_own = order(
            functools.partial(project, first=c * chunk, heads=chunk), first_normed, wq, *tables
        )
        queries.append(query)
        own.append(kv_own)
        moving.append([chip_shift(kv_own, by) for by in range(1, ctx_count // 2)])
    own_swapped = order.apart(swapped_of, *own)
    other_dy, other_one = order.apart(swapped_of, rows_dy[1], rows_one[1])
    left_dy, left_one = (rows_dy[0], other_dy), (rows_one[0], other_one)

    def attend(query, mine, partners, arrived, *meta):
        pieces = [mine, partners]
        for piece in arrived:
            pieces += [piece, core_swap(piece)]
        return attention_forward(query, pieces, *meta), pieces[3::2]

    attended_others = []
    for c in range(CHUNKS):
        (att, lse_c), swapped = order.apart(
            attend, queries[c], own[c], own_swapped[c], moving[c], *meta
        )
        both = [v for pair in zip(moving[c], swapped) for v in pair]
        pieces.append([own[c], own_swapped[c], *both])
        attended.append(att)
        lse.append(lse_c)
        attended_others.append(tp_swap(att.reshape(-1, tokens)))
    attended_rows = [a.reshape(-1, tokens) for a in attended]
    attended_others[0] = order(lambda v: v, attended_others[0])
    all_attended, other_attended = order.apart(
        lambda *parts: (jnp.concatenate(parts, axis=0), core_swap(jnp.concatenate(parts, axis=0))),
        *attended_rows,
    )
    right_att = (all_attended, other_attended)
    middle, second_normed = order(
        functools.partial(middle_of, first=3 * units),
        attended_rows,
        attended_others,
        tp_index,
        x,
        gain_rows[1:],
        others,
    )

    turned_products = functools.partial(gradient_products, turned=True)
    activated, d_gate, d_up, d_two_part = order(
        functools.partial(feed_forward, units=units), second_normed, grad_low, others
    )
    d_two_sent = tp_send(d_two_part)

    def down_part(activated, normed, left_dy, core):
        inner = Order()
        other = core_swap(activated)
        rows = inner(rows_for_cores, normed, core)
        rows_other = core_swap(rows[1])
        return inner(gradient_products, left_dy, (activated, other)), other, (rows[0], rows_other)

    down_products, other_act, left_two = order.apart(
        down_part, activated, second_normed, left_dy, core
    )
    right_act = (activated, other_act)
    down_arrived = gradient_send(down_products)

    def gate_part(activated, d_gate, d_up, left_two, others):
        inner = Order()
        other_gate = core_swap(d_gate)
        down_sum = inner(functools.partial(down_project, first=2 * units), activated, others)
        gate_products = inner(gradient_products, left_two, (d_gate, other_gate))
        other_up = core_swap(lax.optimization_barrier((d_up, down_sum))[0])
        up_products = inner(gradient_products, left_two, (d_up, other_up))
        return gate_products, up_products, down_sum, other_gate, other_up

    gate_products, up_products, down_sum, other_gate, other_up = order.apart(
        gate_part, activated, d_gate, d_up, left_two, others
    )
    right_gate, right_up = (d_gate, other_gate), (d_up, other_up)
    shares = order(
        lambda ffn, qkv: [share(ffn[0]), share(ffn[1]), share(qkv)],
        feedforward_weight,
        query_key_value_weight,
    )
    down_arrived, gate_products, down_sum, d_two_sent = order(
        touch, down_arrived, gate_products, down_sum, d_two_sent
    )
    gate_arrived = gradient_send(gate_products)
    down_sent = tp_send(down_sum)
    d_mid, d_branch, d_att = order(
        functools.partial(d_middle_of, first=3 * units, features=att_columns),
        d_two_sent,
        middle,
        grad_low,
        gain_rows[1:],
        others,
    )
    d_att = d_att.reshape(CHUNKS, chunk, QUERY_PER_KV, HEAD_SIZE, tokens)

    def attend_back(query, d_att, attended, lse, pieces, *meta):
        d_query, *d_pieces = attention_backward(query, d_att, attended, lse, pieces, *meta)
        sums = [
            (mine.astype(f32) + core_swap(partners).astype(f32)).astype(bf16)
            for mine, partners in zip(d_pieces[::2], d_pieces[1::2])
        ]
        return d_query, sums

    def attention_step(c):
        d_query, sums = order.apart(
            attend_back, queries[c], d_att[c], attended[c], lse[c], pieces[c], *meta
        )
        return d_query, [chip_shift(s, -by) if by else s for by, s in enumerate(sums)]

    d_query_0, d_kv_0 = attention_step(0)
    gate_arrived, up_products = order(touch, gate_arrived, up_products)
    up_arrived = gradient_send(up_products)
    down_chip = order(gradient_chip, left_dy, right_act, down_arrived)
    gate_chip = order(gradient_chip, left_two, right_gate, gate_arrived)
    two_scattered = gradient_scatter(jnp.concatenate([down_chip, gate_chip], axis=2))
    d_query_1, d_kv_1 = attention_step(1)

    def branch_part(d_branch, core, right_att):
        inner = Order()
        rows = inner(rows_for_cores, d_branch, core)
        left = (rows[0], core_swap(rows[1]))
        return inner(turned_products, left, right_att), left

    out_products, left_branch = order.apart(branch_part, d_branch, core, right_att)
    up_chip = order(gradient_chip, left_two, right_up, up_arrived)
    d_kv_0, d_kv_1, down_sent, up_chip = order(touch, d_kv_0, d_kv_1, down_sent, up_chip)
    up_scattered = gradient_scatter(up_chip)

    def project_back(d_query, d_kv, wq, *tables):
        inner = Order()
        parts = [inner(turned_back, q, kv, *tables) for q, kv in zip(d_query, d_kv)]
        others = [core_swap(p) for p in parts]
        return inner(d_one_of, parts, wq), parts, others

    d_one_part, d_proj, other_proj = order.apart(
        project_back, [d_query_0, d_query_1], [d_kv_0, d_kv_1], wq, *tables
    )
    d_one_sent = tp_send(d_one_part)
    right_proj = list(zip(d_proj, other_proj))

    two_scattered = order(touch, two_scattered)[0]

    def tail(left_one, right_proj, left_branch, right_att, out_products, middle, down_sent):
        inner = Order()
        out_arrived = gradient_send(out_products)
        finish = functools.partial(gradient_chip, turned=True, pieces=True)
        arrived = gradient_send(inner(turned_products, left_one, right_proj[0]))
        terms = gradient_groups(inner(finish, left_branch, right_att, out_arrived))
        products = inner(turned_products, left_one, right_proj[1])
        hidden_out = inner(lambda m, s: (m + tp_add(s)).astype(bf16), middle, down_sent)
        grad_out = inner(gradient_sum, terms)
        arrived_1 = gradient_send(lax.optimization_barrier((products, grad_out))[0])
        terms = gradient_groups(inner(finish, left_one, right_proj[0], arrived))
        chip = inner(finish, left_one, right_proj[1], arrived_1)
        return grad_out, hidden_out, inner(gradient_sum, terms), chip

    grad_out, hidden_out, grad_qkv_0, chip = order.apart(
        tail, left_one, right_proj, left_branch, right_att, out_products, middle, down_sent
    )
    terms = gradient_groups(chip)
    own_gains = lax.dynamic_slice_in_dim(
        gains, ctx_index * out_share.shape[0], out_share.shape[0], 1
    ).astype(f32)

    def ffn_gradient(two, up):
        down, gate = two[:, :units], two[:, units:]
        gain = gain_gradient(shares[:2], [gate, up], own_gains[1])
        return jnp.stack([gate, up, down], axis=0).astype(f32), gain

    grad_ffn, gain_two = order(ffn_gradient, two_scattered, up_scattered)
    grad_in = order(input_gradient, d_one_sent, x, d_mid, gain_rows[:1])

    def qkv_gradient(first, terms, gain_two):
        whole = jnp.concatenate([first, gradient_sum(terms)], axis=1)
        gain_one = gain_gradient(shares[2:], [whole], own_gains[0])
        return jnp.stack([gain_one, gain_two], axis=0), whole

    grad_gains, grad_qkv = order(qkv_gradient, grad_qkv_0, terms, gain_two)
    grad_gains = grad_gains + tp_swap(grad_gains)
    return (hidden_out[None], grad_in[None], grad_qkv, grad_out, grad_ffn, grad_gains)


def solution(mesh):
    return jax.shard_map(
        on_device,
        mesh=mesh,
        in_specs=(
            P("fsdp", "ctx", None),
            P("fsdp", "ctx", None),
            P("fsdp", None),
            P("fsdp", None),
            P("fsdp", "tp"),
            P("fsdp", "tp"),
            P(None, "fsdp", "tp"),
            P(None, "fsdp"),
        ),
        out_specs=(
            P("fsdp", "ctx", None),
            P("fsdp", "ctx", None),
            P(("fsdp", "ctx"), "tp"),
            P(("fsdp", "ctx"), "tp"),
            P(None, ("fsdp", "ctx"), "tp"),
            P(None, ("fsdp", "ctx")),
        ),
        check_vma=False,
    )
```

```python
import functools
import math

import jax
import jax.numpy as jnp
from jax import lax
from jax.experimental import pallas as pl
from jax.experimental.pallas import tpu as pltpu
from jax.sharding import PartitionSpec as P

HEAD_SIZE = 96
QUERY_PER_KV = 2
HALF = HEAD_SIZE // 2
BLOCK = 128

norm_eps = 1e-05
rope_base = 100000.0
masked_score = -1e30
SCORE_SCALE = HEAD_SIZE ** (-0.5)
SCORE_SCALE_2 = SCORE_SCALE * math.log2(math.e)

SMALL_COST = pl.CostEstimate(flops=1, bytes_accessed=1, transcendentals=0)

bf16 = jnp.bfloat16
f32 = jnp.float32


def mm(a, b, contract=((1,), (0,))):
    return lax.dot_general(a, b, (contract, ((), ())), preferred_element_type=f32)


def fill_keys(heads, count, blocks, kv_refs, kn_ref, kt_ref, vn_ref, vt_ref):
    for h in range(heads):
        for s in range(count):
            for b in range(blocks):
                columns = slice(b * BLOCK, (b + 1) * BLOCK)
                places = slice(s * BLOCK, (s + 1) * BLOCK)
                key = kv_refs[s][h, 0, :, columns]
                value = kv_refs[s][h, 1, :, columns]
                kn_ref[h, b, places, :] = key.T
                if kt_ref is not None:
                    kt_ref[h, b, :, places] = key
                if vn_ref is not None:
                    vn_ref[h, b, places, :] = value.T
                if vt_ref is not None:
                    vt_ref[h, b, :, places] = value


def fill_places(count, stripes_ref, place_ref):
    step = lax.broadcasted_iota(jnp.int32, (BLOCK, QUERY_PER_KV * BLOCK), 0) * count
    for s in range(count):
        place_ref[s * BLOCK : (s + 1) * BLOCK, :] = step + stripes_ref[s]


def twice(row):
    return jnp.concatenate([row] * QUERY_PER_KV, axis=1)


def block_of(ref, h, i):
    columns = slice(i * BLOCK, (i + 1) * BLOCK)
    return jnp.concatenate([ref[h, g, :, columns] for g in range(QUERY_PER_KV)], axis=1)


def allowed_keys(place_ref, count, b, place_q, start_q):
    place, offset = place_ref[...], b * (BLOCK * count)
    allowed = place >= start_q - offset
    return allowed if place_q is None else allowed & (place <= place_q - offset)


def forward_kernel(heads, count, blocks, starts_ref, stripes_ref, place_q_ref, start_q_ref, q_ref, *rest):
    kv_refs = rest[:count]
    o_ref, lse_ref, kn_ref, vt_ref, place_ref = rest[count:]
    fill_keys(heads, count, blocks, kv_refs, kn_ref, None, None, vt_ref)
    fill_places(count, stripes_ref, place_ref)
    for i in range(blocks):
        columns = slice(i * BLOCK, (i + 1) * BLOCK)
        queries = [block_of(q_ref, h, i) for h in range(heads)]
        place_q = twice(place_q_ref[:, columns])
        start_q = twice(start_q_ref[:, columns])

        def scores_of(b, place_q):
            allowed = allowed_keys(place_ref, count, b, place_q, start_q)
            scores = [mm(kn_ref[h, b], queries[h]) for h in range(heads)]
            return [jnp.where(allowed, s * SCORE_SCALE_2, masked_score) for s in scores]

        state = []
        for h, scores in enumerate(scores_of(i, place_q)):
            top = jnp.max(scores, axis=0, keepdims=True)
            weights = jnp.exp2(scores - top)
            total = jnp.sum(weights, axis=0, keepdims=True)
            state.append((top, total, mm(vt_ref[h, i], weights.astype(bf16))))

        def step(b, carry):
            result = []
            for h, scores in enumerate(scores_of(b, None)):
                top, total, accum = carry[h]
                new_top = jnp.maximum(top, jnp.max(scores, axis=0, keepdims=True))
                fade = jnp.exp2(top - new_top)
                weights = jnp.exp2(scores - new_top)
                total = total * fade + jnp.sum(weights, axis=0, keepdims=True)
                accum = accum * fade + mm(vt_ref[h, b], weights.astype(bf16))
                result.append((new_top, total, accum))
            return tuple(result)

        state = lax.fori_loop(starts_ref[i], i, step, tuple(state)) if i else state
        for h, (top, total, accum) in enumerate(state):
            result = (accum / total).astype(bf16)
            lse = top + jnp.log2(total)
            for g in range(QUERY_PER_KV):
                part = slice(g * BLOCK, (g + 1) * BLOCK)
                o_ref[h, g, :, columns] = result[:, part]
                lse_ref[h, g : g + 1, columns] = lse[:, part]


def backward_kernel(
    heads, count, blocks, starts_ref, stripes_ref, place_q_ref, start_q_ref, q_ref, do_ref, o_ref, lse_ref, *rest
):
    kv_refs = rest[:count]
    dq_ref = rest[count]
    dkv_refs = rest[count + 1 : 2 * count + 1]
    kn_ref, kt_ref, vn_ref, place_ref, dk_ref, dv_ref = rest[2 * count + 1 :]
    fill_keys(heads, count, blocks, kv_refs, kn_ref, kt_ref, vn_ref, None)
    fill_places(count, stripes_ref, place_ref)
    for i in range(blocks):
        columns = slice(i * BLOCK, (i + 1) * BLOCK)
        place_q = twice(place_q_ref[:, columns])
        start_q = twice(start_q_ref[:, columns])
        parts = []
        for h in range(heads):
            query, d_out, out = (block_of(ref, h, i) for ref in (q_ref, do_ref, o_ref))
            delta = jnp.sum(d_out.astype(f32) * out.astype(f32), axis=0, keepdims=True)
            lse = jnp.concatenate(
                [lse_ref[h, g : g + 1, columns] for g in range(QUERY_PER_KV)], axis=1
            )
            parts.append((query, query.T, d_out, d_out.T, delta, lse))

        def terms(b, place_q, first):
            allowed = allowed_keys(place_ref, count, b, place_q, start_q)
            d_queries = []
            for h, (query, query_rows, d_out, d_out_rows, delta, lse) in enumerate(parts):
                scores = mm(kn_ref[h, b], query)
                d_prob = mm(vn_ref[h, b], d_out)
                probs = jnp.exp2(jnp.where(allowed, scores * SCORE_SCALE_2, masked_score) - lse)
                d_score = (probs * (d_prob - delta)).astype(bf16)
                d_value = mm(probs.astype(bf16), d_out_rows)
                d_key = mm(d_score, query_rows)
                if first:
                    dv_ref[h, b] = d_value
                    dk_ref[h, b] = d_key
                else:
                    dv_ref[h, b] += d_value
                    dk_ref[h, b] += d_key
                d_queries.append(mm(kt_ref[h, b], d_score))
            return d_queries

        def step(b, carry):
            return tuple(a + t for a, t in zip(carry, terms(b, None, False)))

        d_queries = tuple(terms(i, place_q, True))
        if i:
            d_queries = lax.fori_loop(starts_ref[i], i, step, d_queries)
        for h in range(heads):
            for g in range(QUERY_PER_KV):
                dq_ref[h, g, :, columns] = d_queries[h][:, g * BLOCK : (g + 1) * BLOCK] * SCORE_SCALE
    for h in range(heads):
        for s in range(count):
            places = slice(s * BLOCK, (s + 1) * BLOCK)
            for b in range(blocks):
                columns = slice(b * BLOCK, (b + 1) * BLOCK)
                dkv_refs[s][h, 0, :, columns] = (dk_ref[h, b, places, :] * SCORE_SCALE).T.astype(bf16)
                dkv_refs[s][h, 1, :, columns] = dv_ref[h, b, places, :].T.astype(bf16)


def head_spec(heads, *dims):
    return pl.BlockSpec((heads, *dims), lambda n, *_: (0,) * (1 + len(dims)))


def row_spec(tokens):
    return pl.BlockSpec((1, tokens), lambda n, *_: (0, 0))


def attention_forward(queries, pieces, starts, stripes, place, start):
    heads, _, _, tokens = queries.shape
    count, blocks = len(pieces), tokens // BLOCK
    keys = count * BLOCK
    per_query = head_spec(heads, QUERY_PER_KV, HEAD_SIZE, tokens)
    per_kv = head_spec(heads, 2, HEAD_SIZE, tokens)
    return pl.pallas_call(
        functools.partial(forward_kernel, heads, count, blocks),
        grid_spec=pltpu.PrefetchScalarGridSpec(
            num_scalar_prefetch=2,
            grid=(1,),
            in_specs=[row_spec(tokens)] * 2 + [per_query] + [per_kv] * count,
            out_specs=[per_query, head_spec(heads, QUERY_PER_KV, tokens)],
            scratch_shapes=[
                pltpu.VMEM((heads, blocks, keys, HEAD_SIZE), bf16),
                pltpu.VMEM((heads, blocks, HEAD_SIZE, keys), bf16),
                pltpu.VMEM((keys, QUERY_PER_KV * BLOCK), jnp.int32),
            ],
        ),
        out_shape=[
            jax.ShapeDtypeStruct(queries.shape, bf16),
            jax.ShapeDtypeStruct((heads, QUERY_PER_KV, tokens), f32),
        ],
        compiler_params=pltpu.CompilerParams(vmem_limit_bytes=40 << 20),
        cost_estimate=SMALL_COST,
        name="attention_forward",
    )(starts, stripes, place, start, queries, *pieces)


def attention_backward(queries, d_att, attended, lse, pieces, starts, stripes, place, start):
    heads, _, _, tokens = queries.shape
    count, blocks = len(pieces), tokens // BLOCK
    keys = count * BLOCK
    per_query = head_spec(heads, QUERY_PER_KV, HEAD_SIZE, tokens)
    per_kv = head_spec(heads, 2, HEAD_SIZE, tokens)
    return pl.pallas_call(
        functools.partial(backward_kernel, heads, count, blocks),
        grid_spec=pltpu.PrefetchScalarGridSpec(
            num_scalar_prefetch=2,
            grid=(1,),
            in_specs=[row_spec(tokens)] * 2
            + [per_query] * 3
            + [head_spec(heads, QUERY_PER_KV, tokens)]
            + [per_kv] * count,
            out_specs=[per_query] + [per_kv] * count,
            scratch_shapes=[
                pltpu.VMEM((heads, blocks, keys, HEAD_SIZE), bf16),
                pltpu.VMEM((heads, blocks, HEAD_SIZE, keys), bf16),
                pltpu.VMEM((heads, blocks, keys, HEAD_SIZE), bf16),
                pltpu.VMEM((keys, QUERY_PER_KV * BLOCK), jnp.int32),
                pltpu.VMEM((heads, blocks, keys, HEAD_SIZE), f32),
                pltpu.VMEM((heads, blocks, keys, HEAD_SIZE), f32),
            ],
        ),
        out_shape=[jax.ShapeDtypeStruct(queries.shape, f32)]
        + [jax.ShapeDtypeStruct(pieces[0].shape, bf16)] * count,
        compiler_params=pltpu.CompilerParams(vmem_limit_bytes=48 << 20),
        cost_estimate=SMALL_COST,
        name="attention_backward",
    )(starts, stripes, place, start, queries, d_att, attended, lse, *pieces)


def pack_kernel(_, ffn_ref, out_ref, other_ref, packed_ref):
    units, columns = ffn_ref.shape[2], out_ref.shape[1]
    for i in range(3):
        packed_ref[:, i * units : (i + 1) * units] = ffn_ref[i]
    packed_ref[:, 3 * units : 3 * units + columns] = out_ref[...]
    packed_ref[:, 3 * units + columns :] = other_ref[...]


def packed_share(feedforward_weight, out_share, out_other, index, share_of):
    rows, columns = out_share.shape
    units = feedforward_weight.shape[2]
    if rows % 16:
        parts = [share_of(feedforward_weight[i]) for i in range(3)]
        return jnp.concatenate([*parts, out_share, out_other], axis=1)
    whole = pl.BlockSpec((rows, columns), lambda n, _: (0, 0))
    width = 3 * units + 2 * columns
    return pl.pallas_call(
        pack_kernel,
        grid_spec=pltpu.PrefetchScalarGridSpec(
            num_scalar_prefetch=1,
            grid=(1,),
            in_specs=[
                pl.BlockSpec((3, rows, units), lambda n, place: (0, place[0], 0)),
                whole,
                whole,
            ],
            out_specs=pl.BlockSpec((rows, width), lambda n, _: (0, 0)),
        ),
        out_shape=jax.ShapeDtypeStruct((rows, width), bf16),
        compiler_params=pltpu.CompilerParams(vmem_limit_bytes=60 << 20),
        cost_estimate=SMALL_COST,
        name="pack",
    )(index[None], feedforward_weight, out_share, out_other)


def input_gradient_kernel(mine_ref, other_ref, x_ref, d_mid_ref, gain_ref, out_ref):
    x = x_ref[...].astype(f32)
    scale = lax.rsqrt(jnp.mean(x * x, axis=-1, keepdims=True) + norm_eps)
    unit = x * scale
    weighted = (mine_ref[...].astype(f32) + other_ref[...].astype(f32)) * gain_ref[...]
    out_ref[...] = (
        d_mid_ref[...].astype(f32)
        + scale * (weighted - unit * jnp.mean(weighted * unit, axis=-1, keepdims=True))
    ).astype(bf16)


def input_gradient(sent, x, d_mid, gain):
    tokens, width = x.shape
    block = 256
    here = pl.BlockSpec((block, width), lambda n: (n, 0))
    return pl.pallas_call(
        input_gradient_kernel,
        grid=(tokens // block,),
        in_specs=[here] * 4 + [pl.BlockSpec((1, width), lambda n: (0, 0))],
        out_specs=here,
        out_shape=jax.ShapeDtypeStruct((tokens, width), bf16),
        compiler_params=pltpu.CompilerParams(vmem_limit_bytes=32 << 20),
        cost_estimate=SMALL_COST,
        name="input_gradient",
    )(*sent, x, d_mid, gain)


def project_kernel(x_ref, w_ref, cos_ref, sin_ref, q_ref, kv_ref):
    projected = mm(x_ref[...], w_ref[...]).T
    cos_table, sin_table = cos_ref[...], sin_ref[...]
    for j in range(QUERY_PER_KV + 1):
        first = j * HEAD_SIZE
        front = projected[first : first + HALF]
        back = projected[first + HALF : first + HEAD_SIZE]
        target = q_ref.at[0, j] if j < QUERY_PER_KV else kv_ref.at[0, 0]
        target[:HALF, :] = (front * cos_table - back * sin_table).astype(bf16)
        target[HALF:, :] = (back * cos_table + front * sin_table).astype(bf16)
    kv_ref[0, 1] = projected[(QUERY_PER_KV + 1) * HEAD_SIZE :].astype(bf16)


def project(normed, weight, cos_table, sin_table, first, heads):
    tokens, width = normed.shape
    columns = (QUERY_PER_KV + 2) * HEAD_SIZE
    whole = lambda shape: pl.BlockSpec(shape, lambda h: (0, 0))
    return pl.pallas_call(
        project_kernel,
        grid=(heads,),
        in_specs=[
            whole((tokens, width)),
            pl.BlockSpec((width, columns), lambda h: (0, first + h)),
            whole((HALF, tokens)),
            whole((HALF, tokens)),
        ],
        out_specs=[
            pl.BlockSpec((1, QUERY_PER_KV, HEAD_SIZE, tokens), lambda h: (h, 0, 0, 0)),
            pl.BlockSpec((1, 2, HEAD_SIZE, tokens), lambda h: (h, 0, 0, 0)),
        ],
        out_shape=[
            jax.ShapeDtypeStruct((heads, QUERY_PER_KV, HEAD_SIZE, tokens), bf16),
            jax.ShapeDtypeStruct((heads, 2, HEAD_SIZE, tokens), bf16),
        ],
        compiler_params=pltpu.CompilerParams(vmem_limit_bytes=40 << 20),
        cost_estimate=SMALL_COST,
        name="project",
    )(normed, weight, cos_table, sin_table)


def middle_kernel(count, tp_ref, x_ref, gain_ref, *refs):
    mine, others = refs[:count], refs[count : 2 * count]
    w_first, w_second, middle_ref, normed_ref, first_ref, second_ref = refs[2 * count :]

    def fill(first, second):
        first_ref[...] = jnp.concatenate([r[...] for r in first], axis=0).T
        second_ref[...] = jnp.concatenate([r[...] for r in second], axis=0).T

    @pl.when(tp_ref[0] == 0)
    def _():
        fill(mine, others)

    @pl.when(tp_ref[0] == 1)
    def _():
        fill(others, mine)

    branch = mm(first_ref[...], w_first[...], ((1,), (1,))) + mm(
        second_ref[...], w_second[...], ((1,), (1,))
    )
    middle = x_ref[...].astype(f32) + branch
    middle_ref[...] = middle
    scale = lax.rsqrt(jnp.mean(middle * middle, axis=-1, keepdims=True) + norm_eps)
    normed_ref[...] = (middle * scale * gain_ref[...]).astype(bf16)


def middle_of(mine, others, tp_index, x, gain, weight, first):
    tokens, width = x.shape
    features = sum(p.shape[0] for p in mine)
    block = 256
    half = first // features
    token_spec = pl.BlockSpec((block, width), lambda n, _: (n, 0))
    return pl.pallas_call(
        functools.partial(middle_kernel, len(mine)),
        grid_spec=pltpu.PrefetchScalarGridSpec(
            num_scalar_prefetch=1,
            grid=(tokens // block,),
            in_specs=[token_spec, pl.BlockSpec((1, width), lambda n, _: (0, 0))]
            + [pl.BlockSpec((p.shape[0], block), lambda n, _: (0, n)) for p in (*mine, *others)]
            + [
                pl.BlockSpec((width, features), lambda n, tp: (0, half + tp[0])),
                pl.BlockSpec((width, features), lambda n, tp: (0, half + 1 - tp[0])),
            ],
            out_specs=[token_spec] * 2,
            scratch_shapes=[pltpu.VMEM((block, features), bf16)] * 2,
        ),
        out_shape=[
            jax.ShapeDtypeStruct((tokens, width), f32),
            jax.ShapeDtypeStruct((tokens, width), bf16),
        ],
        compiler_params=pltpu.CompilerParams(vmem_limit_bytes=40 << 20),
        cost_estimate=SMALL_COST,
        name="middle",
    )(tp_index[None], x, gain, *mine, *others, weight, weight)


def down_kernel(a_ref, w_ref, out_ref):
    out_ref[...] = mm(a_ref[...], w_ref[...], ((1,), (1,))).astype(bf16)


def down_project(activated, weight, first):
    tokens, units = activated.shape
    width, block = weight.shape[0], 512
    return pl.pallas_call(
        down_kernel,
        grid=(width // block,),
        in_specs=[
            pl.BlockSpec((tokens, units), lambda n: (0, 0)),
            pl.BlockSpec((block, units), lambda n: (n, first // units)),
        ],
        out_specs=pl.BlockSpec((tokens, block), lambda n: (0, n)),
        out_shape=jax.ShapeDtypeStruct((tokens, width), bf16),
        compiler_params=pltpu.CompilerParams(vmem_limit_bytes=40 << 20),
        cost_estimate=SMALL_COST,
        name="down_project",
    )(activated, weight)


def d_middle_kernel(
    mine_ref, other_ref, middle_ref, dy_ref, gain_ref, w_ref, branch_ref, *d_att_refs
):
    middle = middle_ref[...]
    scale = lax.rsqrt(jnp.mean(middle * middle, axis=-1, keepdims=True) + norm_eps)
    unit = middle * scale
    weighted = (mine_ref[...].astype(f32) + other_ref[...].astype(f32)) * gain_ref[...]
    d_mid = dy_ref[...].astype(f32) + scale * (
        weighted - unit * jnp.mean(weighted * unit, axis=-1, keepdims=True)
    )
    branch = d_mid.astype(bf16)
    branch_ref[...] = branch
    d_att = mm(branch, w_ref[...]).astype(bf16).T
    first = 0
    for ref in d_att_refs:
        ref[...] = d_att[first : first + ref.shape[0]]
        first += ref.shape[0]


def d_middle_of(sent, middle, d_out, gain, weight, first, parts):
    mine, other = sent
    tokens, width = middle.shape
    features = sum(parts)
    block = 256
    here = pl.BlockSpec((block, width), lambda n: (n, 0))
    row = pl.BlockSpec((1, width), lambda n: (0, 0))
    branch, *d_att = pl.pallas_call(
        d_middle_kernel,
        grid=(tokens // block,),
        in_specs=[here, here, here, here, row]
        + [pl.BlockSpec((width, features), lambda n: (0, first // features))],
        out_specs=[here] + [pl.BlockSpec((p, block), lambda n: (0, n)) for p in parts],
        out_shape=[jax.ShapeDtypeStruct((tokens, width), bf16)]
        + [jax.ShapeDtypeStruct((p, tokens), bf16) for p in parts],
        compiler_params=pltpu.CompilerParams(vmem_limit_bytes=48 << 20),
        cost_estimate=SMALL_COST,
        name="d_middle",
    )(mine, other, middle, d_out, gain, weight)
    return branch, d_att


def turn_back_kernel(cos_ref, sin_ref, dq_ref, *refs):
    kv_refs, out_ref = refs[:-1], refs[-1]
    cos_table, sin_table = cos_ref[...], sin_ref[...]
    total = kv_refs[0][0].astype(f32)
    for ref in kv_refs[1:]:
        total = total + ref[0].astype(f32)
    for j in range(QUERY_PER_KV + 1):
        vector = dq_ref[0, j] if j < QUERY_PER_KV else total[0]
        front, back = vector[:HALF], vector[HALF:]
        first = j * HEAD_SIZE
        out_ref[first : first + HALF, :] = (front * cos_table + back * sin_table).astype(bf16)
        out_ref[first + HALF : first + HEAD_SIZE, :] = (
            back * cos_table - front * sin_table
        ).astype(bf16)
    out_ref[(QUERY_PER_KV + 1) * HEAD_SIZE :, :] = total[1].astype(bf16)


def turned_back(d_query, d_kv_terms, cos_table, sin_table):
    heads, _, _, tokens = d_query.shape
    columns = (QUERY_PER_KV + 2) * HEAD_SIZE
    whole = pl.BlockSpec((HALF, tokens), lambda h: (0, 0))
    head = lambda n: pl.BlockSpec((1, n, HEAD_SIZE, tokens), lambda h: (h, 0, 0, 0))
    return pl.pallas_call(
        turn_back_kernel,
        grid=(heads,),
        in_specs=[whole, whole, head(QUERY_PER_KV)] + [head(2)] * len(d_kv_terms),
        out_specs=pl.BlockSpec((columns, tokens), lambda h: (h, 0)),
        out_shape=jax.ShapeDtypeStruct((heads * columns, tokens), bf16),
        compiler_params=pltpu.CompilerParams(vmem_limit_bytes=32 << 20),
        cost_estimate=SMALL_COST,
        name="turn_back",
    )(cos_table, sin_table, d_query, *d_kv_terms)


def d_one_kernel(count, *refs):
    parts, w_ref, out_ref, rows_ref = refs[:count], refs[count], refs[count + 1], refs[count + 2]

    @pl.when(pl.program_id(0) == 0)
    def _():
        first = 0
        for part in parts:
            columns = part.shape[0]
            rows_ref[:, first : first + columns] = part[...].T
            first += columns

    out_ref[...] = mm(rows_ref[...], w_ref[...], ((1,), (1,))).astype(bf16)


def d_one_of(parts, weight):
    width, columns = weight.shape
    tokens, block = parts[0].shape[1], 512
    return pl.pallas_call(
        functools.partial(d_one_kernel, len(parts)),
        grid=(width // block,),
        in_specs=[pl.BlockSpec(p.shape, lambda n: (0, 0)) for p in parts]
        + [pl.BlockSpec((block, columns), lambda n: (n, 0))],
        out_specs=pl.BlockSpec((tokens, block), lambda n: (0, n)),
        out_shape=jax.ShapeDtypeStruct((tokens, width), bf16),
        scratch_shapes=[pltpu.VMEM((tokens, columns), bf16)],
        compiler_params=pltpu.CompilerParams(vmem_limit_bytes=40 << 20),
        cost_estimate=SMALL_COST,
        name="d_one",
    )(*parts, weight)


def ffn_kernel(
    h_ref, dy_ref, wg_ref, wu_ref, wd_ref, act_ref, dg_ref, du_ref, out_ref, acc_ref
):
    step = pl.program_id(0)
    w_gate, w_up = wg_ref[...], wu_ref[...]
    gate = mm(h_ref[...], w_gate)
    up = mm(h_ref[...], w_up)
    d_act = mm(dy_ref[...], wd_ref[...])
    sigmoid_gate = jax.nn.sigmoid(gate)
    silu_gate = gate * sigmoid_gate
    act_ref[...] = (silu_gate * up).astype(bf16)
    d_gate = (d_act * up * sigmoid_gate * (1.0 + gate * (1.0 - sigmoid_gate))).astype(bf16)
    d_up = (d_act * silu_gate).astype(bf16)
    dg_ref[...] = d_gate
    du_ref[...] = d_up
    term = mm(d_gate, w_gate, ((1,), (1,))) + mm(d_up, w_up, ((1,), (1,)))

    @pl.when(step == 0)
    def _():
        acc_ref[...] = term

    @pl.when(step > 0)
    def _():
        acc_ref[...] += term

    @pl.when(step == pl.num_programs(0) - 1)
    def _():
        out_ref[...] = acc_ref[...].astype(bf16)


FFN_BLOCK = 512


def feed_forward(normed, d_out, weights, units):
    tokens, width = normed.shape
    weight_spec = lambda i: pl.BlockSpec(
        (width, FFN_BLOCK), lambda n: (0, i * units // FFN_BLOCK + n)
    )
    column_spec = pl.BlockSpec((tokens, FFN_BLOCK), lambda n: (0, n))
    whole = pl.BlockSpec((tokens, width), lambda n: (0, 0))
    return pl.pallas_call(
        ffn_kernel,
        grid=(units // FFN_BLOCK,),
        in_specs=[whole, whole] + [weight_spec(i) for i in range(3)],
        out_specs=[column_spec] * 3 + [whole],
        out_shape=[jax.ShapeDtypeStruct((tokens, units), bf16)] * 3
        + [jax.ShapeDtypeStruct((tokens, width), bf16)],
        scratch_shapes=[pltpu.VMEM((tokens, width), f32)],
        compiler_params=pltpu.CompilerParams(vmem_limit_bytes=56 << 20),
        cost_estimate=SMALL_COST,
        name="feed_forward",
    )(normed, d_out, weights, weights, weights)


def turn_kernel(chips, rows, core_ref, x_ref, mine_ref, other_ref, turned_ref):
    turned_ref[...] = x_ref[...].T
    core = core_ref[0]
    for chip in range(chips):
        for ref, which in ((mine_ref, core), (other_ref, 1 - core)):
            first = pl.multiple_of((chip * 2 + which) * rows, 16)
            ref[0, chip] = turned_ref[pl.ds(first, rows), :]


def rows_for_cores(activation, core):
    tokens, width = activation.shape
    groups, chips = lax.axis_size("fsdp"), lax.axis_size("ctx") // 2
    rows = width // (groups * chips * 2)
    shape = (groups, chips, rows, tokens)
    if rows % 16 or (width // groups) % 128:
        turned = activation.T.reshape(groups, chips, 2, rows, tokens)
        return tuple(
            lax.dynamic_index_in_dim(turned, c, 2, keepdims=False) for c in (core, 1 - core)
        )
    spec = pl.BlockSpec((1, chips, rows, tokens), lambda g, _: (g, 0, 0, 0))
    return pl.pallas_call(
        functools.partial(turn_kernel, chips, rows),
        grid_spec=pltpu.PrefetchScalarGridSpec(
            num_scalar_prefetch=1,
            grid=(groups,),
            in_specs=[pl.BlockSpec((tokens, width // groups), lambda g, _: (0, g))],
            out_specs=[spec, spec],
            scratch_shapes=[pltpu.VMEM((width // groups, tokens), bf16)],
        ),
        out_shape=[jax.ShapeDtypeStruct(shape, bf16)] * 2,
        compiler_params=pltpu.CompilerParams(vmem_limit_bytes=32 << 20),
        cost_estimate=SMALL_COST,
        name="turn_rows",
    )(core[None], activation)


class Order:
    def __init__(self, always=None):
        self.last = ()
        self.always = always

    def __call__(self, function, *args):
        leaves, tree = jax.tree.flatten(args)
        held = lax.optimization_barrier((*leaves, *self.last))
        result = function(*jax.tree.unflatten(tree, held[: len(leaves)]))
        self.last = (jax.tree.leaves(result)[0],)
        return result

    def apart(self, function, *args):
        def guarded(*args):
            shapes = jax.eval_shape(function, *args)
            nothing = lambda *_: jax.tree.map(lambda s: jnp.zeros(s.shape, s.dtype), shapes)
            return lax.cond(self.always, function, nothing, *args)

        return self(guarded, *args)


def swapped_of(*values):
    return [core_swap(v) for v in values]


def core_swap(value):
    size = lax.axis_size("ctx")
    return lax.ppermute(value, "ctx", [(i, i ^ 1) for i in range(size)])


def chip_shift(value, by):
    size = lax.axis_size("ctx")
    return lax.ppermute(value, "ctx", [(i, (i + 2 * by) % size) for i in range(size)])


def group_shift(value, by):
    size = lax.axis_size("fsdp")
    return lax.ppermute(value, "fsdp", [(i, (i + by) % size) for i in range(size)])


def tp_swap(value):
    return lax.ppermute(value, "tp", [(0, 1), (1, 0)])


def tp_send(part):
    part = lax.optimization_barrier(part)
    return part, tp_swap(part)


def tp_add(sent):
    mine, other = sent
    return mine.astype(f32) + other.astype(f32)


def both_cores(value):
    return value, core_swap(value)


def gathered_rows(weight, gains, hold):
    groups, count = lax.axis_size("fsdp"), lax.axis_size("ctx")
    group, index = lax.axis_index("fsdp"), lax.axis_index("ctx")
    rows, columns = weight.shape
    share = rows // count
    mine = lax.dynamic_slice_in_dim(weight, index * share, share, 0)
    extra = jnp.pad(gains, ((0, 16 - gains.shape[0]), (0, columns - gains.shape[1])))
    mine = jnp.concatenate([mine, extra], axis=0)
    fetched = [group_shift(mine, by) for by in range(1, groups)]
    stack = jnp.stack([gains] + [p[share : share + 2, : gains.shape[1]] for p in fetched], axis=0)
    all_gains = jnp.concatenate(
        [
            lax.dynamic_index_in_dim(stack, (group - i) % groups, 0, keepdims=False)
            for i in range(groups)
        ],
        axis=1,
    ).astype(f32)
    weight, _ = lax.optimization_barrier((weight, hold))
    whole = jnp.zeros((groups * rows, columns), weight.dtype)
    whole = lax.dynamic_update_slice_in_dim(whole, weight, group * rows, 0)
    pieces = jnp.stack([p[:share] for p in fetched], axis=0)

    def placed(whole, pieces, source):
        for by in range(1, groups):
            first = (group - by) % groups * rows + source * share
            whole = lax.dynamic_update_slice_in_dim(whole, pieces[by - 1], first, 0)
        return whole

    passed = [pieces] + [chip_shift(pieces, by) for by in range(1, count // 2)]
    for by, moved in enumerate(passed):
        source = (index - 2 * by) % count
        whole = placed(whole, moved, source)
        whole = placed(whole, core_swap(moved), source ^ 1)
    return whole, all_gains, fetched


def gradient_kernel(pairs, count, turned, pieces, place_ref, *refs):
    total = None
    for i in range(pairs):
        left, right = refs[2 * i], refs[2 * i + 1]
        groups, _, rows, tokens = left.shape
        term = mm(
            left[...].reshape(groups * rows, tokens), right[...], ((1,), (1 if turned else 0,))
        )
        total = term if total is None else total + term
    total = total.reshape(groups, rows, total.shape[-1])
    refs = refs[2 * pairs :]
    arrived = refs[:count]
    for piece in arrived:
        total = total + piece[...].astype(f32)
    if not pieces:
        refs[-1][...] = total.astype(bf16)
        return
    outs, sum_ref = refs[-1 - groups : -1], refs[-1]
    sum_ref[...] = total
    group = place_ref[1]
    for by, out in enumerate(outs):
        out[...] = sum_ref[lax.rem(group + by, groups)].astype(out.dtype)


def gradient_call(left, right, which, turned, arrived, pieces, inside=None):
    groups, chips, rows, tokens = left[0].shape
    group = lax.axis_index("fsdp")
    columns = right[0].shape[0 if turned else 1]
    block = next((b for b in (512, 384) if columns % b == 0), columns)
    if rows % 16 or columns % block:
        total = None
        for a, b in zip(left, right):
            picked = lax.dynamic_index_in_dim(a, which, 1, keepdims=False)
            term = mm(picked.reshape(groups * rows, -1), b, ((1,), (1 if turned else 0,)))
            total = term if total is None else total + term
        total = sum((piece.astype(f32) for piece in arrived), total.reshape(groups, rows, -1))
        if not pieces:
            return total.astype(bf16)
        parts = [
            lax.dynamic_index_in_dim(total, (group + by) % groups, 0, keepdims=False)
            for by in range(groups)
        ]
        return [parts[0]] + [p.astype(bf16) for p in parts[1:]]
    left_spec = pl.BlockSpec((groups, 1, rows, tokens), lambda n, place: (0, place[0], 0, 0))
    if turned:
        right_spec = pl.BlockSpec((block, tokens), lambda n, _: (n, 0))
    else:
        right_spec = pl.BlockSpec((tokens, block), lambda n, _: (0, n))
    sum_spec = pl.BlockSpec((groups, rows, block), lambda n, _: (0, 0, n))
    operands = [v for pair in zip(left, right) for v in pair] + list(arrived)
    if pieces:
        out_specs = [pl.BlockSpec((rows, block), lambda n, _: (0, n))] * groups
        out_shape = [
            jax.ShapeDtypeStruct((rows, columns), bf16 if by else f32) for by in range(groups)
        ]
        scratch = [pltpu.VMEM((groups, rows, block), f32)]
    else:
        first, total, whole = inside or (0, columns, ())
        out_specs, scratch = pl.BlockSpec((groups, rows, block), lambda n, _: (0, 0, first // block + n)), []
        out_shape = jax.ShapeDtypeStruct((groups, rows, total), bf16)
        operands += whole
    return pl.pallas_call(
        functools.partial(gradient_kernel, len(left), len(arrived), turned, pieces),
        grid_spec=pltpu.PrefetchScalarGridSpec(
            num_scalar_prefetch=1,
            grid=(columns // block,),
            in_specs=[left_spec, right_spec] * len(left)
            + [sum_spec] * len(arrived)
            + [pl.BlockSpec(memory_space=pl.ANY)] * (len(operands) - 2 * len(left) - len(arrived)),
            out_specs=out_specs,
            scratch_shapes=scratch,
        ),
        out_shape=out_shape,
        input_output_aliases={len(operands): 0} if inside and inside[2] else {},
        compiler_params=pltpu.CompilerParams(vmem_limit_bytes=40 << 20),
        cost_estimate=SMALL_COST,
        name="gradient_chip" if arrived else "gradient_send",
    )(jnp.stack([which, group]), *operands)


def gradient_products(left, right, turned=False):
    chips, chip = lax.axis_size("ctx") // 2, lax.axis_index("ctx") // 2
    return [
        gradient_call(left, right, (chip + by) % chips, turned, (), False)
        for by in range(1, chips)
    ]


def gradient_send(products):
    return [chip_shift(p, by) for by, p in enumerate(products, 1)]


def gradient_chip(left, right, arrived, turned=False, pieces=False):
    return gradient_call(left, right, lax.axis_index("ctx") // 2, turned, arrived, pieces)


def gradient_groups(pieces):
    return [group_shift(piece, by) if by else piece for by, piece in enumerate(pieces)]


def gradient_scatter(total):
    groups, rows, columns = total.shape
    return lax.psum_scatter(
        total.reshape(groups * rows, columns), "fsdp", scatter_dimension=0, tiled=True
    )


def gradient_sum(terms):
    total = terms[0].astype(f32)
    for term in terms[1:]:
        total = total + term.astype(f32)
    return total


def gain_gradient(weights, gradients, gain):
    total = 0.0
    for weight, gradient in zip(weights, gradients):
        total = total + jnp.sum(weight.astype(f32) * gradient.astype(f32), axis=1)
    return total / gain


def slot_meta(ctx_index, tokens, stripe_row, lengths):
    count = stripe_row.shape[0]
    ends = jnp.cumsum(lengths)
    residue = jnp.sum(jnp.where(jnp.arange(count) == ctx_index, stripe_row, 0))
    packed = jnp.arange(tokens, dtype=jnp.int32) * count + residue
    passed = (packed[:, None] >= ends[None, :]).astype(jnp.int32)
    start = jnp.sum(passed * lengths[None, :], axis=1)
    return packed, start


def rms_normed(values, gain):
    scale_row = lax.rsqrt(jnp.mean(values * values, axis=-1, keepdims=True) + norm_eps)
    return (values * scale_row * gain, scale_row)


def norm_back(grad_normed, values, scale_row, gain):
    unit_rows = values * scale_row
    weighted = grad_normed * gain
    return scale_row * (weighted - unit_rows * jnp.mean(weighted * unit_rows, axis=-1, keepdims=True))


def on_device(
    hidden_in,
    cotangent,
    doc_lengths,
    stripe,
    query_key_value_weight,
    output_weight,
    feedforward_weight,
    gains,
):
    ctx_count, ctx_index = lax.axis_size("ctx"), lax.axis_index("ctx")
    group_count, group = lax.axis_size("fsdp"), lax.axis_index("fsdp")
    core = ctx_index % 2
    tokens, width = hidden_in.shape[1:]
    qkv_columns = query_key_value_weight.shape[1]
    att_columns = output_weight.shape[1]
    units = feedforward_weight.shape[2]
    kv_heads = qkv_columns // ((QUERY_PER_KV + 2) * HEAD_SIZE)

    def share(weight):
        rows = weight.shape[0] // ctx_count
        return lax.dynamic_slice_in_dim(weight, ctx_index * rows, rows, 0)

    tp_index = lax.axis_index("tp")
    out_share = share(output_weight)
    out_other = tp_swap(out_share)
    payload = packed_share(feedforward_weight, out_share, out_other, ctx_index, share)
    wq, gain_rows, fetched = gathered_rows(query_key_value_weight, gains, payload)
    payload = lax.optimization_barrier((payload, fetched[0]))[0]
    others = lax.all_gather(payload, ("fsdp", "ctx"), axis=0, tiled=True)

    lengths, stripe_row = doc_lengths[0], stripe[0]
    packed, start = slot_meta(ctx_index, tokens, stripe_row, lengths)
    frequency = rope_base ** (-(2.0 * jnp.arange(HALF, dtype=f32)) / HEAD_SIZE)
    angles = frequency[:, None] * (packed - start).astype(f32)[None, :]
    cos_table, sin_table = jnp.cos(angles), jnp.sin(angles)
    block_starts = start[::BLOCK] // (ctx_count * BLOCK)
    sources = []
    for by in range(ctx_count // 2):
        source = (ctx_index - 2 * by) % ctx_count
        sources += [source, source ^ 1]
    stripes = jnp.stack(
        [lax.dynamic_index_in_dim(stripe_row, s, 0, keepdims=False) for s in sources]
    )
    meta = (block_starts, stripes, packed[None, :], start[None, :])

    order = Order(lengths[0] > 0)
    touch = lambda *v: v
    x, grad_low = hidden_in[0], cotangent[0]
    rows_dy = order(rows_for_cores, grad_low, core)

    def first_norm(x, gain):
        values = x.astype(f32)
        scale = lax.rsqrt(jnp.mean(values * values, axis=-1, keepdims=True) + norm_eps)
        return (values * scale * gain).astype(bf16), scale

    first_normed, scale_one = order(first_norm, x, gain_rows[0])
    rows_one = order(rows_for_cores, first_normed, core)
    first_normed, tables, *meta = lax.optimization_barrier(
        (first_normed, (cos_table, sin_table), *meta)
    )
    sizes = (kv_heads // 2, kv_heads - kv_heads // 2)
    chunks = range(len(sizes))
    queries, own, moving, pieces, attended, lse = [], [], [], [], [], []
    for c in chunks:
        query, kv_own = order(
            functools.partial(project, first=sum(sizes[:c]), heads=sizes[c]),
            first_normed,
            wq,
            *tables,
        )
        queries.append(query)
        own.append(kv_own)
        moving.append([chip_shift(kv_own, by) for by in range(1, ctx_count // 2)])
    own_swapped = order.apart(swapped_of, *own)
    other_dy, other_one = order.apart(swapped_of, rows_dy[1], rows_one[1])
    left_dy, left_one = (rows_dy[0], other_dy), (rows_one[0], other_one)

    def attend(query, mine, partners, arrived, *meta):
        pieces = [mine, partners]
        for piece in arrived:
            pieces += [piece, core_swap(piece)]
        return attention_forward(query, pieces, *meta), pieces[3::2]

    attended_others = []
    for c in chunks:
        (att, lse_c), swapped = order.apart(
            attend, queries[c], own[c], own_swapped[c], moving[c], *meta
        )
        both = [v for pair in zip(moving[c], swapped) for v in pair]
        pieces.append([own[c], own_swapped[c], *both])
        attended.append(att)
        lse.append(lse_c)
        attended_others.append(tp_swap(att.reshape(-1, tokens)))
    attended_rows = [a.reshape(-1, tokens) for a in attended]
    attended_others[0] = order(lambda v: v, attended_others[0])
    all_attended, other_attended = order.apart(
        lambda *parts: (jnp.concatenate(parts, axis=0), core_swap(jnp.concatenate(parts, axis=0))),
        *attended_rows,
    )
    right_att = (all_attended, other_attended)
    middle, second_normed = order(
        functools.partial(middle_of, first=3 * units),
        attended_rows,
        attended_others,
        tp_index,
        x,
        gain_rows[1:],
        others,
    )

    turned_products = functools.partial(gradient_products, turned=True)
    activated, d_gate, d_up, d_two_part = order(
        functools.partial(feed_forward, units=units), second_normed, grad_low, others
    )
    d_two_sent = tp_send(d_two_part)

    def down_part(activated, normed, left_dy, core):
        inner = Order()
        other = core_swap(activated)
        rows = inner(rows_for_cores, normed, core)
        rows_other = core_swap(rows[1])
        return inner(gradient_products, left_dy, (activated, other)), other, (rows[0], rows_other)

    down_products, other_act, left_two = order.apart(
        down_part, activated, second_normed, left_dy, core
    )
    right_act = (activated, other_act)
    down_arrived = gradient_send(down_products)

    def gate_part(activated, d_gate, d_up, left_two, others):
        inner = Order()
        other_gate = core_swap(d_gate)
        down_sum = inner(functools.partial(down_project, first=2 * units), activated, others)
        gate_products = inner(gradient_products, left_two, (d_gate, other_gate))
        other_up = core_swap(lax.optimization_barrier((d_up, down_sum))[0])
        up_products = inner(gradient_products, left_two, (d_up, other_up))
        early = units // 4
        up_products = [[p[:, :, :early] for p in up_products], [p[:, :, early:] for p in up_products]]
        return gate_products, up_products, down_sum, other_gate, other_up

    gate_products, up_products, down_sum, other_gate, other_up = order.apart(
        gate_part, activated, d_gate, d_up, left_two, others
    )
    right_gate, right_up = (d_gate, other_gate), (d_up, other_up)
    shares = order(
        lambda ffn, qkv: [share(ffn[0]), share(ffn[1]), share(qkv)],
        feedforward_weight,
        query_key_value_weight,
    )
    down_arrived, gate_products, up_products, down_sum, d_two_sent = order(
        touch, down_arrived, gate_products, up_products, down_sum, d_two_sent
    )
    gate_arrived, up_first = gradient_send(gate_products), gradient_send(up_products[0])
    down_scattered = gradient_scatter(order(gradient_chip, left_dy, right_act, down_arrived))
    down_sent = tp_send(down_sum)
    d_branch, d_att = order(
        functools.partial(
            d_middle_of, first=3 * units, parts=[s * QUERY_PER_KV * HEAD_SIZE for s in sizes]
        ),
        d_two_sent,
        middle,
        grad_low,
        gain_rows[1:],
        others,
    )
    d_att = [d.reshape(-1, QUERY_PER_KV, HEAD_SIZE, tokens) for d in d_att]

    def attend_back(query, d_att, attended, lse, pieces, *meta):
        d_query, *d_pieces = attention_backward(query, d_att, attended, lse, pieces, *meta)
        sums = [
            (mine.astype(f32) + core_swap(partners).astype(f32)).astype(bf16)
            for mine, partners in zip(d_pieces[::2], d_pieces[1::2])
        ]
        return d_query, sums

    def attention_step(c):
        d_query, sums = order.apart(
            attend_back, queries[c], d_att[c], attended[c], lse[c], pieces[c], *meta
        )
        return d_query, [chip_shift(s, -by) if by else s for by, s in enumerate(sums)]

    d_query_0, d_kv_0 = attention_step(0)
    gate_arrived, up_products = order(touch, gate_arrived, up_products)
    up_second = gradient_send(up_products[1])
    gate_chip = order(gradient_chip, left_two, right_gate, gate_arrived)
    gate_chip, up_first = order(touch, gate_chip, up_first)
    gate_scattered = gradient_scatter(gate_chip)
    d_query_1, d_kv_1 = attention_step(1)

    def branch_part(d_branch, core, right_att):
        inner = Order()
        rows = inner(rows_for_cores, d_branch, core)
        left = (rows[0], core_swap(rows[1]))
        return inner(turned_products, left, right_att), left

    out_products, left_branch = order.apart(branch_part, d_branch, core, right_att)
    up_first, up_second = order(touch, up_first, up_second)
    up_arrived = [jnp.concatenate(pair, axis=2) for pair in zip(up_first, up_second)]
    up_chip = order(gradient_chip, left_two, right_up, up_arrived)
    d_kv_0, d_kv_1, down_sent, up_chip = order(touch, d_kv_0, d_kv_1, down_sent, up_chip)
    up_scattered = gradient_scatter(up_chip)

    def project_back(d_query, d_kv, wq, *tables):
        inner = Order()
        parts = [inner(turned_back, q, kv, *tables) for q, kv in zip(d_query, d_kv)]
        others = [core_swap(p) for p in parts]
        return inner(d_one_of, parts, wq), parts, others

    d_one_part, d_proj, other_proj = order.apart(
        project_back, [d_query_0, d_query_1], [d_kv_0, d_kv_1], wq, *tables
    )
    d_one_sent = tp_send(d_one_part)
    right_proj = list(zip(d_proj, other_proj))

    grad_down = order(lambda v: v.astype(f32), down_scattered)
    gate_scattered = order(touch, gate_scattered)[0]

    def tail(left_one, right_proj, left_branch, right_att, out_products, middle, down_sent):
        inner = Order()
        out_arrived = gradient_send(out_products)
        finish = functools.partial(gradient_chip, turned=True, pieces=True)
        arrived = gradient_send(inner(turned_products, left_one, right_proj[0]))
        terms = gradient_groups(inner(finish, left_branch, right_att, out_arrived))
        products = inner(turned_products, left_one, right_proj[1])
        hidden_out = inner(lambda m, s: (m + tp_add(s)).astype(bf16), middle, down_sent)
        grad_out = inner(gradient_sum, terms)
        arrived_1 = gradient_send(lax.optimization_barrier((products, grad_out))[0])
        terms = gradient_groups(inner(finish, left_one, right_proj[0], arrived))
        chip = inner(finish, left_one, right_proj[1], arrived_1)
        return grad_out, hidden_out, inner(gradient_sum, terms), chip

    grad_out, hidden_out, grad_qkv_0, chip = order.apart(
        tail, left_one, right_proj, left_branch, right_att, out_products, middle, down_sent
    )
    terms = gradient_groups(chip)
    own_gains = lax.dynamic_slice_in_dim(
        gains, ctx_index * out_share.shape[0], out_share.shape[0], 1
    ).astype(f32)

    def ffn_gradient(down, gate, up):
        gain = gain_gradient(shares[:2], [gate, up], own_gains[1])
        return jnp.stack([gate.astype(f32), up.astype(f32), down], axis=0), gain

    grad_ffn, gain_two = order(ffn_gradient, grad_down, gate_scattered, up_scattered)
    grad_in = order(input_gradient, d_one_sent, x, d_branch, gain_rows[:1])

    def qkv_gradient(first, terms, gain_two):
        whole = jnp.concatenate([first, gradient_sum(terms)], axis=1)
        gain_one = gain_gradient(shares[2:], [whole], own_gains[0])
        return jnp.stack([gain_one, gain_two], axis=0), whole

    grad_gains, grad_qkv = order(qkv_gradient, grad_qkv_0, terms, gain_two)
    grad_gains = grad_gains + tp_swap(grad_gains)
    return (hidden_out[None], grad_in[None], grad_qkv, grad_out, grad_ffn, grad_gains)


def solution(mesh):
    return jax.shard_map(
        on_device,
        mesh=mesh,
        in_specs=(
            P("fsdp", "ctx", None),
            P("fsdp", "ctx", None),
            P("fsdp", None),
            P("fsdp", None),
            P("fsdp", "tp"),
            P("fsdp", "tp"),
            P(None, "fsdp", "tp"),
            P(None, "fsdp"),
        ),
        out_specs=(
            P("fsdp", "ctx", None),
            P("fsdp", "ctx", None),
            P(("fsdp", "ctx"), "tp"),
            P(("fsdp", "ctx"), "tp"),
            P(None, ("fsdp", "ctx"), "tp"),
            P(None, ("fsdp", "ctx")),
        ),
        check_vma=False,
    )
```

```python
import functools
import math

import jax
import jax.numpy as jnp
from jax import lax
from jax.experimental import pallas as pl
from jax.experimental.pallas import tpu as pltpu
from jax.sharding import PartitionSpec as P

HEAD_SIZE = 96
QUERY_PER_KV = 2
HALF = HEAD_SIZE // 2
BLOCK = 128

norm_eps = 1e-05
rope_base = 100000.0
masked_score = -1e30
SCORE_SCALE = HEAD_SIZE ** (-0.5)
SCORE_SCALE_2 = SCORE_SCALE * math.log2(math.e)

SMALL_COST = pl.CostEstimate(flops=1, bytes_accessed=1, transcendentals=0)

bf16 = jnp.bfloat16
f32 = jnp.float32


def mm(a, b, contract=((1,), (0,))):
    return lax.dot_general(a, b, (contract, ((), ())), preferred_element_type=f32)


def fill_keys(heads, count, blocks, kv_refs, kn_ref, kt_ref, vn_ref, vt_ref):
    for h in range(heads):
        for s in range(count):
            for b in range(blocks):
                columns = slice(b * BLOCK, (b + 1) * BLOCK)
                places = slice(s * BLOCK, (s + 1) * BLOCK)
                key = kv_refs[s][h, 0, :, columns]
                value = kv_refs[s][h, 1, :, columns]
                kn_ref[h, b, places, :] = key.T
                if kt_ref is not None:
                    kt_ref[h, b, :, places] = key
                if vn_ref is not None:
                    vn_ref[h, b, places, :] = value.T
                if vt_ref is not None:
                    vt_ref[h, b, :, places] = value


def fill_places(count, stripes_ref, place_ref):
    step = lax.broadcasted_iota(jnp.int32, (BLOCK, QUERY_PER_KV * BLOCK), 0) * count
    for s in range(count):
        place_ref[s * BLOCK : (s + 1) * BLOCK, :] = step + stripes_ref[s]


def twice(row):
    return jnp.concatenate([row] * QUERY_PER_KV, axis=1)


def block_of(ref, h, i):
    columns = slice(i * BLOCK, (i + 1) * BLOCK)
    return jnp.concatenate([ref[h, g, :, columns] for g in range(QUERY_PER_KV)], axis=1)


def allowed_keys(place_ref, count, b, place_q, start_q):
    place, offset = place_ref[...], b * (BLOCK * count)
    allowed = place >= start_q - offset
    return allowed if place_q is None else allowed & (place <= place_q - offset)


def forward_kernel(heads, count, blocks, starts_ref, stripes_ref, place_q_ref, start_q_ref, q_ref, *rest):
    kv_refs = rest[:count]
    o_ref, lse_ref, kn_ref, vt_ref, place_ref = rest[count:]
    fill_keys(heads, count, blocks, kv_refs, kn_ref, None, None, vt_ref)
    fill_places(count, stripes_ref, place_ref)
    for i in range(blocks):
        columns = slice(i * BLOCK, (i + 1) * BLOCK)
        queries = [block_of(q_ref, h, i) for h in range(heads)]
        place_q = twice(place_q_ref[:, columns])
        start_q = twice(start_q_ref[:, columns])

        def scores_of(b, place_q):
            allowed = allowed_keys(place_ref, count, b, place_q, start_q)
            scores = [mm(kn_ref[h, b], queries[h]) for h in range(heads)]
            return [jnp.where(allowed, s * SCORE_SCALE_2, masked_score) for s in scores]

        state = []
        for h, scores in enumerate(scores_of(i, place_q)):
            top = jnp.max(scores, axis=0, keepdims=True)
            weights = jnp.exp2(scores - top)
            total = jnp.sum(weights, axis=0, keepdims=True)
            state.append((top, total, mm(vt_ref[h, i], weights.astype(bf16))))

        def step(b, carry):
            result = []
            for h, scores in enumerate(scores_of(b, None)):
                top, total, accum = carry[h]
                new_top = jnp.maximum(top, jnp.max(scores, axis=0, keepdims=True))
                fade = jnp.exp2(top - new_top)
                weights = jnp.exp2(scores - new_top)
                total = total * fade + jnp.sum(weights, axis=0, keepdims=True)
                accum = accum * fade + mm(vt_ref[h, b], weights.astype(bf16))
                result.append((new_top, total, accum))
            return tuple(result)

        state = lax.fori_loop(starts_ref[i], i, step, tuple(state)) if i else state
        for h, (top, total, accum) in enumerate(state):
            result = (accum / total).astype(bf16)
            lse = top + jnp.log2(total)
            for g in range(QUERY_PER_KV):
                part = slice(g * BLOCK, (g + 1) * BLOCK)
                o_ref[h, g, :, columns] = result[:, part]
                lse_ref[h, g : g + 1, columns] = lse[:, part]


def backward_kernel(
    heads, count, blocks, starts_ref, stripes_ref, place_q_ref, start_q_ref, q_ref, do_ref, o_ref, lse_ref, *rest
):
    kv_refs = rest[:count]
    dq_ref = rest[count]
    dkv_refs = rest[count + 1 : 2 * count + 1]
    kn_ref, kt_ref, vn_ref, place_ref, dk_ref, dv_ref = rest[2 * count + 1 :]
    fill_keys(heads, count, blocks, kv_refs, kn_ref, kt_ref, vn_ref, None)
    fill_places(count, stripes_ref, place_ref)
    for i in range(blocks):
        columns = slice(i * BLOCK, (i + 1) * BLOCK)
        place_q = twice(place_q_ref[:, columns])
        start_q = twice(start_q_ref[:, columns])
        parts = []
        for h in range(heads):
            query, d_out, out = (block_of(ref, h, i) for ref in (q_ref, do_ref, o_ref))
            delta = jnp.sum(d_out.astype(f32) * out.astype(f32), axis=0, keepdims=True)
            lse = jnp.concatenate(
                [lse_ref[h, g : g + 1, columns] for g in range(QUERY_PER_KV)], axis=1
            )
            parts.append((query, query.T, d_out, d_out.T, delta, lse))

        def terms(b, place_q, first):
            allowed = allowed_keys(place_ref, count, b, place_q, start_q)
            d_queries = []
            for h, (query, query_rows, d_out, d_out_rows, delta, lse) in enumerate(parts):
                scores = mm(kn_ref[h, b], query)
                d_prob = mm(vn_ref[h, b], d_out)
                probs = jnp.exp2(jnp.where(allowed, scores * SCORE_SCALE_2, masked_score) - lse)
                d_score = (probs * (d_prob - delta)).astype(bf16)
                d_value = mm(probs.astype(bf16), d_out_rows)
                d_key = mm(d_score, query_rows)
                if first:
                    dv_ref[h, b] = d_value
                    dk_ref[h, b] = d_key
                else:
                    dv_ref[h, b] += d_value
                    dk_ref[h, b] += d_key
                d_queries.append(mm(kt_ref[h, b], d_score))
            return d_queries

        def step(b, carry):
            return tuple(a + t for a, t in zip(carry, terms(b, None, False)))

        d_queries = tuple(terms(i, place_q, True))
        if i:
            d_queries = lax.fori_loop(starts_ref[i], i, step, d_queries)
        for h in range(heads):
            for g in range(QUERY_PER_KV):
                dq_ref[h, g, :, columns] = d_queries[h][:, g * BLOCK : (g + 1) * BLOCK] * SCORE_SCALE
    for h in range(heads):
        for s in range(count):
            places = slice(s * BLOCK, (s + 1) * BLOCK)
            for b in range(blocks):
                columns = slice(b * BLOCK, (b + 1) * BLOCK)
                dkv_refs[s][h, 0, :, columns] = (dk_ref[h, b, places, :] * SCORE_SCALE).T.astype(bf16)
                dkv_refs[s][h, 1, :, columns] = dv_ref[h, b, places, :].T.astype(bf16)


def head_spec(heads, *dims):
    return pl.BlockSpec((heads, *dims), lambda n, *_: (0,) * (1 + len(dims)))


def row_spec(tokens):
    return pl.BlockSpec((1, tokens), lambda n, *_: (0, 0))


def attention_forward(queries, pieces, starts, stripes, place, start):
    heads, _, _, tokens = queries.shape
    count, blocks = len(pieces), tokens // BLOCK
    keys = count * BLOCK
    per_query = head_spec(heads, QUERY_PER_KV, HEAD_SIZE, tokens)
    per_kv = head_spec(heads, 2, HEAD_SIZE, tokens)
    return pl.pallas_call(
        functools.partial(forward_kernel, heads, count, blocks),
        grid_spec=pltpu.PrefetchScalarGridSpec(
            num_scalar_prefetch=2,
            grid=(1,),
            in_specs=[row_spec(tokens)] * 2 + [per_query] + [per_kv] * count,
            out_specs=[per_query, head_spec(heads, QUERY_PER_KV, tokens)],
            scratch_shapes=[
                pltpu.VMEM((heads, blocks, keys, HEAD_SIZE), bf16),
                pltpu.VMEM((heads, blocks, HEAD_SIZE, keys), bf16),
                pltpu.VMEM((keys, QUERY_PER_KV * BLOCK), jnp.int32),
            ],
        ),
        out_shape=[
            jax.ShapeDtypeStruct(queries.shape, bf16),
            jax.ShapeDtypeStruct((heads, QUERY_PER_KV, tokens), f32),
        ],
        compiler_params=pltpu.CompilerParams(vmem_limit_bytes=40 << 20),
        cost_estimate=SMALL_COST,
        name="attention_forward",
    )(starts, stripes, place, start, queries, *pieces)


def attention_backward(queries, d_att, attended, lse, pieces, starts, stripes, place, start):
    heads, _, _, tokens = queries.shape
    count, blocks = len(pieces), tokens // BLOCK
    keys = count * BLOCK
    per_query = head_spec(heads, QUERY_PER_KV, HEAD_SIZE, tokens)
    per_kv = head_spec(heads, 2, HEAD_SIZE, tokens)
    return pl.pallas_call(
        functools.partial(backward_kernel, heads, count, blocks),
        grid_spec=pltpu.PrefetchScalarGridSpec(
            num_scalar_prefetch=2,
            grid=(1,),
            in_specs=[row_spec(tokens)] * 2
            + [per_query] * 3
            + [head_spec(heads, QUERY_PER_KV, tokens)]
            + [per_kv] * count,
            out_specs=[per_query] + [per_kv] * count,
            scratch_shapes=[
                pltpu.VMEM((heads, blocks, keys, HEAD_SIZE), bf16),
                pltpu.VMEM((heads, blocks, HEAD_SIZE, keys), bf16),
                pltpu.VMEM((heads, blocks, keys, HEAD_SIZE), bf16),
                pltpu.VMEM((keys, QUERY_PER_KV * BLOCK), jnp.int32),
                pltpu.VMEM((heads, blocks, keys, HEAD_SIZE), f32),
                pltpu.VMEM((heads, blocks, keys, HEAD_SIZE), f32),
            ],
        ),
        out_shape=[jax.ShapeDtypeStruct(queries.shape, f32)]
        + [jax.ShapeDtypeStruct(pieces[0].shape, bf16)] * count,
        compiler_params=pltpu.CompilerParams(vmem_limit_bytes=48 << 20),
        cost_estimate=SMALL_COST,
        name="attention_backward",
    )(starts, stripes, place, start, queries, d_att, attended, lse, *pieces)


def pack_kernel(_, ffn_ref, out_ref, other_ref, packed_ref):
    units, columns = ffn_ref.shape[2], out_ref.shape[1]
    for i in range(3):
        packed_ref[:, i * units : (i + 1) * units] = ffn_ref[i]
    packed_ref[:, 3 * units : 3 * units + columns] = out_ref[...]
    packed_ref[:, 3 * units + columns :] = other_ref[...]


def packed_share(feedforward_weight, out_share, out_other, index, share_of):
    rows, columns = out_share.shape
    units = feedforward_weight.shape[2]
    if rows % 16:
        parts = [share_of(feedforward_weight[i]) for i in range(3)]
        return jnp.concatenate([*parts, out_share, out_other], axis=1)
    whole = pl.BlockSpec((rows, columns), lambda n, _: (0, 0))
    width = 3 * units + 2 * columns
    return pl.pallas_call(
        pack_kernel,
        grid_spec=pltpu.PrefetchScalarGridSpec(
            num_scalar_prefetch=1,
            grid=(1,),
            in_specs=[
                pl.BlockSpec((3, rows, units), lambda n, place: (0, place[0], 0)),
                whole,
                whole,
            ],
            out_specs=pl.BlockSpec((rows, width), lambda n, _: (0, 0)),
        ),
        out_shape=jax.ShapeDtypeStruct((rows, width), bf16),
        compiler_params=pltpu.CompilerParams(vmem_limit_bytes=60 << 20),
        cost_estimate=SMALL_COST,
        name="pack",
    )(index[None], feedforward_weight, out_share, out_other)


def input_gradient_kernel(mine_ref, other_ref, x_ref, d_mid_ref, gain_ref, out_ref):
    x = x_ref[...].astype(f32)
    scale = lax.rsqrt(jnp.mean(x * x, axis=-1, keepdims=True) + norm_eps)
    unit = x * scale
    weighted = (mine_ref[...].astype(f32) + other_ref[...].astype(f32)) * gain_ref[...]
    out_ref[...] = (
        d_mid_ref[...].astype(f32)
        + scale * (weighted - unit * jnp.mean(weighted * unit, axis=-1, keepdims=True))
    ).astype(bf16)


def input_gradient(sent, x, d_mid, gain):
    tokens, width = x.shape
    block = 256
    here = pl.BlockSpec((block, width), lambda n: (n, 0))
    return pl.pallas_call(
        input_gradient_kernel,
        grid=(tokens // block,),
        in_specs=[here] * 4 + [pl.BlockSpec((1, width), lambda n: (0, 0))],
        out_specs=here,
        out_shape=jax.ShapeDtypeStruct((tokens, width), bf16),
        compiler_params=pltpu.CompilerParams(vmem_limit_bytes=32 << 20),
        cost_estimate=SMALL_COST,
        name="input_gradient",
    )(*sent, x, d_mid, gain)


def project_kernel(x_ref, w_ref, cos_ref, sin_ref, q_ref, kv_ref):
    projected = mm(x_ref[...], w_ref[...]).T
    cos_table, sin_table = cos_ref[...], sin_ref[...]
    for j in range(QUERY_PER_KV + 1):
        first = j * HEAD_SIZE
        front = projected[first : first + HALF]
        back = projected[first + HALF : first + HEAD_SIZE]
        target = q_ref.at[0, j] if j < QUERY_PER_KV else kv_ref.at[0, 0]
        target[:HALF, :] = (front * cos_table - back * sin_table).astype(bf16)
        target[HALF:, :] = (back * cos_table + front * sin_table).astype(bf16)
    kv_ref[0, 1] = projected[(QUERY_PER_KV + 1) * HEAD_SIZE :].astype(bf16)


def project(normed, weight, cos_table, sin_table, first, heads):
    tokens, width = normed.shape
    columns = (QUERY_PER_KV + 2) * HEAD_SIZE
    whole = lambda shape: pl.BlockSpec(shape, lambda h: (0, 0))
    return pl.pallas_call(
        project_kernel,
        grid=(heads,),
        in_specs=[
            whole((tokens, width)),
            pl.BlockSpec((width, columns), lambda h: (0, first + h)),
            whole((HALF, tokens)),
            whole((HALF, tokens)),
        ],
        out_specs=[
            pl.BlockSpec((1, QUERY_PER_KV, HEAD_SIZE, tokens), lambda h: (h, 0, 0, 0)),
            pl.BlockSpec((1, 2, HEAD_SIZE, tokens), lambda h: (h, 0, 0, 0)),
        ],
        out_shape=[
            jax.ShapeDtypeStruct((heads, QUERY_PER_KV, HEAD_SIZE, tokens), bf16),
            jax.ShapeDtypeStruct((heads, 2, HEAD_SIZE, tokens), bf16),
        ],
        compiler_params=pltpu.CompilerParams(vmem_limit_bytes=40 << 20),
        cost_estimate=SMALL_COST,
        name="project",
    )(normed, weight, cos_table, sin_table)


def middle_kernel(count, tp_ref, x_ref, gain_ref, *refs):
    mine, others = refs[:count], refs[count : 2 * count]
    w_first, w_second, middle_ref, normed_ref, first_ref, second_ref = refs[2 * count :]

    def fill(first, second):
        first_ref[...] = jnp.concatenate([r[...] for r in first], axis=0).T
        second_ref[...] = jnp.concatenate([r[...] for r in second], axis=0).T

    @pl.when(tp_ref[0] == 0)
    def _():
        fill(mine, others)

    @pl.when(tp_ref[0] == 1)
    def _():
        fill(others, mine)

    branch = mm(first_ref[...], w_first[...], ((1,), (1,))) + mm(
        second_ref[...], w_second[...], ((1,), (1,))
    )
    middle = x_ref[...].astype(f32) + branch
    middle_ref[...] = middle
    scale = lax.rsqrt(jnp.mean(middle * middle, axis=-1, keepdims=True) + norm_eps)
    normed_ref[...] = (middle * scale * gain_ref[...]).astype(bf16)


def middle_of(mine, others, tp_index, x, gain, weight, first):
    tokens, width = x.shape
    features = sum(p.shape[0] for p in mine)
    block = 256
    half = first // features
    token_spec = pl.BlockSpec((block, width), lambda n, _: (n, 0))
    return pl.pallas_call(
        functools.partial(middle_kernel, len(mine)),
        grid_spec=pltpu.PrefetchScalarGridSpec(
            num_scalar_prefetch=1,
            grid=(tokens // block,),
            in_specs=[token_spec, pl.BlockSpec((1, width), lambda n, _: (0, 0))]
            + [pl.BlockSpec((p.shape[0], block), lambda n, _: (0, n)) for p in (*mine, *others)]
            + [
                pl.BlockSpec((width, features), lambda n, tp: (0, half + tp[0])),
                pl.BlockSpec((width, features), lambda n, tp: (0, half + 1 - tp[0])),
            ],
            out_specs=[token_spec] * 2,
            scratch_shapes=[pltpu.VMEM((block, features), bf16)] * 2,
        ),
        out_shape=[
            jax.ShapeDtypeStruct((tokens, width), f32),
            jax.ShapeDtypeStruct((tokens, width), bf16),
        ],
        compiler_params=pltpu.CompilerParams(vmem_limit_bytes=40 << 20),
        cost_estimate=SMALL_COST,
        name="middle",
    )(tp_index[None], x, gain, *mine, *others, weight, weight)


def down_kernel(a_ref, w_ref, out_ref):
    out_ref[...] = mm(a_ref[...], w_ref[...], ((1,), (1,))).astype(bf16)


def down_project(activated, weight, first):
    tokens, units = activated.shape
    width, block = weight.shape[0], 512
    return pl.pallas_call(
        down_kernel,
        grid=(width // block,),
        in_specs=[
            pl.BlockSpec((tokens, units), lambda n: (0, 0)),
            pl.BlockSpec((block, units), lambda n: (n, first // units)),
        ],
        out_specs=pl.BlockSpec((tokens, block), lambda n: (0, n)),
        out_shape=jax.ShapeDtypeStruct((tokens, width), bf16),
        compiler_params=pltpu.CompilerParams(vmem_limit_bytes=40 << 20),
        cost_estimate=SMALL_COST,
        name="down_project",
    )(activated, weight)


def d_middle_kernel(
    mine_ref, other_ref, middle_ref, dy_ref, gain_ref, w_ref, branch_ref, *d_att_refs
):
    middle = middle_ref[...]
    scale = lax.rsqrt(jnp.mean(middle * middle, axis=-1, keepdims=True) + norm_eps)
    unit = middle * scale
    weighted = (mine_ref[...].astype(f32) + other_ref[...].astype(f32)) * gain_ref[...]
    d_mid = dy_ref[...].astype(f32) + scale * (
        weighted - unit * jnp.mean(weighted * unit, axis=-1, keepdims=True)
    )
    branch = d_mid.astype(bf16)
    branch_ref[...] = branch
    d_att = mm(branch, w_ref[...]).astype(bf16).T
    first = 0
    for ref in d_att_refs:
        ref[...] = d_att[first : first + ref.shape[0]]
        first += ref.shape[0]


def d_middle_of(sent, middle, d_out, gain, weight, first, parts):
    mine, other = sent
    tokens, width = middle.shape
    features = sum(parts)
    block = 256
    here = pl.BlockSpec((block, width), lambda n: (n, 0))
    row = pl.BlockSpec((1, width), lambda n: (0, 0))
    branch, *d_att = pl.pallas_call(
        d_middle_kernel,
        grid=(tokens // block,),
        in_specs=[here, here, here, here, row]
        + [pl.BlockSpec((width, features), lambda n: (0, first // features))],
        out_specs=[here] + [pl.BlockSpec((p, block), lambda n: (0, n)) for p in parts],
        out_shape=[jax.ShapeDtypeStruct((tokens, width), bf16)]
        + [jax.ShapeDtypeStruct((p, tokens), bf16) for p in parts],
        compiler_params=pltpu.CompilerParams(vmem_limit_bytes=48 << 20),
        cost_estimate=SMALL_COST,
        name="d_middle",
    )(mine, other, middle, d_out, gain, weight)
    return branch, d_att


def turn_back_kernel(cos_ref, sin_ref, dq_ref, *refs):
    kv_refs, out_ref = refs[:-1], refs[-1]
    cos_table, sin_table = cos_ref[...], sin_ref[...]
    total = kv_refs[0][0].astype(f32)
    for ref in kv_refs[1:]:
        total = total + ref[0].astype(f32)
    for j in range(QUERY_PER_KV + 1):
        vector = dq_ref[0, j] if j < QUERY_PER_KV else total[0]
        front, back = vector[:HALF], vector[HALF:]
        first = j * HEAD_SIZE
        out_ref[first : first + HALF, :] = (front * cos_table + back * sin_table).astype(bf16)
        out_ref[first + HALF : first + HEAD_SIZE, :] = (
            back * cos_table - front * sin_table
        ).astype(bf16)
    out_ref[(QUERY_PER_KV + 1) * HEAD_SIZE :, :] = total[1].astype(bf16)


def turned_back(d_query, d_kv_terms, cos_table, sin_table):
    heads, _, _, tokens = d_query.shape
    columns = (QUERY_PER_KV + 2) * HEAD_SIZE
    whole = pl.BlockSpec((HALF, tokens), lambda h: (0, 0))
    head = lambda n: pl.BlockSpec((1, n, HEAD_SIZE, tokens), lambda h: (h, 0, 0, 0))
    return pl.pallas_call(
        turn_back_kernel,
        grid=(heads,),
        in_specs=[whole, whole, head(QUERY_PER_KV)] + [head(2)] * len(d_kv_terms),
        out_specs=pl.BlockSpec((columns, tokens), lambda h: (h, 0)),
        out_shape=jax.ShapeDtypeStruct((heads * columns, tokens), bf16),
        compiler_params=pltpu.CompilerParams(vmem_limit_bytes=32 << 20),
        cost_estimate=SMALL_COST,
        name="turn_back",
    )(cos_table, sin_table, d_query, *d_kv_terms)


def d_one_kernel(count, *refs):
    parts, w_ref, out_ref, rows_ref = refs[:count], refs[count], refs[count + 1], refs[count + 2]

    @pl.when(pl.program_id(0) == 0)
    def _():
        first = 0
        for part in parts:
            columns = part.shape[0]
            rows_ref[:, first : first + columns] = part[...].T
            first += columns

    out_ref[...] = mm(rows_ref[...], w_ref[...], ((1,), (1,))).astype(bf16)


def d_one_of(parts, weight):
    width, columns = weight.shape
    tokens, block = parts[0].shape[1], 512
    return pl.pallas_call(
        functools.partial(d_one_kernel, len(parts)),
        grid=(width // block,),
        in_specs=[pl.BlockSpec(p.shape, lambda n: (0, 0)) for p in parts]
        + [pl.BlockSpec((block, columns), lambda n: (n, 0))],
        out_specs=pl.BlockSpec((tokens, block), lambda n: (0, n)),
        out_shape=jax.ShapeDtypeStruct((tokens, width), bf16),
        scratch_shapes=[pltpu.VMEM((tokens, columns), bf16)],
        compiler_params=pltpu.CompilerParams(vmem_limit_bytes=40 << 20),
        cost_estimate=SMALL_COST,
        name="d_one",
    )(*parts, weight)


def ffn_kernel(
    h_ref, dy_ref, wg_ref, wu_ref, wd_ref, act_ref, dg_ref, du_ref, out_ref, acc_ref
):
    step = pl.program_id(0)
    w_gate, w_up = wg_ref[...], wu_ref[...]
    gate = mm(h_ref[...], w_gate)
    up = mm(h_ref[...], w_up)
    d_act = mm(dy_ref[...], wd_ref[...])
    sigmoid_gate = jax.nn.sigmoid(gate)
    silu_gate = gate * sigmoid_gate
    act_ref[...] = (silu_gate * up).astype(bf16)
    d_gate = (d_act * up * sigmoid_gate * (1.0 + gate * (1.0 - sigmoid_gate))).astype(bf16)
    d_up = (d_act * silu_gate).astype(bf16)
    dg_ref[...] = d_gate
    du_ref[...] = d_up
    term = mm(d_gate, w_gate, ((1,), (1,))) + mm(d_up, w_up, ((1,), (1,)))

    @pl.when(step == 0)
    def _():
        acc_ref[...] = term

    @pl.when(step > 0)
    def _():
        acc_ref[...] += term

    @pl.when(step == pl.num_programs(0) - 1)
    def _():
        out_ref[...] = acc_ref[...].astype(bf16)


FFN_BLOCK = 512


def feed_forward(normed, d_out, weights, units):
    tokens, width = normed.shape
    weight_spec = lambda i: pl.BlockSpec(
        (width, FFN_BLOCK), lambda n: (0, i * units // FFN_BLOCK + n)
    )
    column_spec = pl.BlockSpec((tokens, FFN_BLOCK), lambda n: (0, n))
    whole = pl.BlockSpec((tokens, width), lambda n: (0, 0))
    return pl.pallas_call(
        ffn_kernel,
        grid=(units // FFN_BLOCK,),
        in_specs=[whole, whole] + [weight_spec(i) for i in range(3)],
        out_specs=[column_spec] * 3 + [whole],
        out_shape=[jax.ShapeDtypeStruct((tokens, units), bf16)] * 3
        + [jax.ShapeDtypeStruct((tokens, width), bf16)],
        scratch_shapes=[pltpu.VMEM((tokens, width), f32)],
        compiler_params=pltpu.CompilerParams(vmem_limit_bytes=56 << 20),
        cost_estimate=SMALL_COST,
        name="feed_forward",
    )(normed, d_out, weights, weights, weights)


def turn_kernel(chips, rows, core_ref, x_ref, mine_ref, other_ref, turned_ref):
    turned_ref[...] = x_ref[...].T
    core = core_ref[0]
    for chip in range(chips):
        for ref, which in ((mine_ref, core), (other_ref, 1 - core)):
            first = pl.multiple_of((chip * 2 + which) * rows, 16)
            ref[0, chip] = turned_ref[pl.ds(first, rows), :]


def rows_for_cores(activation, core):
    tokens, width = activation.shape
    groups, chips = lax.axis_size("fsdp"), lax.axis_size("ctx") // 2
    rows = width // (groups * chips * 2)
    shape = (groups, chips, rows, tokens)
    if rows % 16 or (width // groups) % 128:
        turned = activation.T.reshape(groups, chips, 2, rows, tokens)
        return tuple(
            lax.dynamic_index_in_dim(turned, c, 2, keepdims=False) for c in (core, 1 - core)
        )
    spec = pl.BlockSpec((1, chips, rows, tokens), lambda g, _: (g, 0, 0, 0))
    return pl.pallas_call(
        functools.partial(turn_kernel, chips, rows),
        grid_spec=pltpu.PrefetchScalarGridSpec(
            num_scalar_prefetch=1,
            grid=(groups,),
            in_specs=[pl.BlockSpec((tokens, width // groups), lambda g, _: (0, g))],
            out_specs=[spec, spec],
            scratch_shapes=[pltpu.VMEM((width // groups, tokens), bf16)],
        ),
        out_shape=[jax.ShapeDtypeStruct(shape, bf16)] * 2,
        compiler_params=pltpu.CompilerParams(vmem_limit_bytes=32 << 20),
        cost_estimate=SMALL_COST,
        name="turn_rows",
    )(core[None], activation)


class Order:
    def __init__(self, always=None):
        self.last = ()
        self.always = always

    def __call__(self, function, *args):
        leaves, tree = jax.tree.flatten(args)
        held = lax.optimization_barrier((*leaves, *self.last))
        result = function(*jax.tree.unflatten(tree, held[: len(leaves)]))
        self.last = (jax.tree.leaves(result)[0],)
        return result

    def apart(self, function, *args):
        def guarded(*args):
            shapes = jax.eval_shape(function, *args)
            nothing = lambda *_: jax.tree.map(lambda s: jnp.zeros(s.shape, s.dtype), shapes)
            return lax.cond(self.always, function, nothing, *args)

        return self(guarded, *args)


def swapped_of(*values):
    return [core_swap(v) for v in values]


def core_swap(value):
    size = lax.axis_size("ctx")
    return lax.ppermute(value, "ctx", [(i, i ^ 1) for i in range(size)])


def chip_shift(value, by):
    size = lax.axis_size("ctx")
    return lax.ppermute(value, "ctx", [(i, (i + 2 * by) % size) for i in range(size)])


def group_shift(value, by):
    size = lax.axis_size("fsdp")
    return lax.ppermute(value, "fsdp", [(i, (i + by) % size) for i in range(size)])


def tp_swap(value):
    return lax.ppermute(value, "tp", [(0, 1), (1, 0)])


def tp_send(part):
    part = lax.optimization_barrier(part)
    return part, tp_swap(part)


def tp_add(sent):
    mine, other = sent
    return mine.astype(f32) + other.astype(f32)


def both_cores(value):
    return value, core_swap(value)


def gathered_rows(weight, gains, hold):
    groups, count = lax.axis_size("fsdp"), lax.axis_size("ctx")
    group, index = lax.axis_index("fsdp"), lax.axis_index("ctx")
    rows, columns = weight.shape
    share = rows // count
    mine = lax.dynamic_slice_in_dim(weight, index * share, share, 0)
    extra = jnp.pad(gains, ((0, 16 - gains.shape[0]), (0, columns - gains.shape[1])))
    mine = jnp.concatenate([mine, extra], axis=0)
    fetched = [group_shift(mine, by) for by in range(1, groups)]
    stack = jnp.stack([gains] + [p[share : share + 2, : gains.shape[1]] for p in fetched], axis=0)
    all_gains = jnp.concatenate(
        [
            lax.dynamic_index_in_dim(stack, (group - i) % groups, 0, keepdims=False)
            for i in range(groups)
        ],
        axis=1,
    ).astype(f32)
    weight, _ = lax.optimization_barrier((weight, hold))
    whole = jnp.zeros((groups * rows, columns), weight.dtype)
    whole = lax.dynamic_update_slice_in_dim(whole, weight, group * rows, 0)
    pieces = jnp.stack([p[:share] for p in fetched], axis=0)

    def placed(whole, pieces, source):
        for by in range(1, groups):
            first = (group - by) % groups * rows + source * share
            whole = lax.dynamic_update_slice_in_dim(whole, pieces[by - 1], first, 0)
        return whole

    passed = [pieces] + [chip_shift(pieces, by) for by in range(1, count // 2)]
    for by, moved in enumerate(passed):
        source = (index - 2 * by) % count
        whole = placed(whole, moved, source)
        whole = placed(whole, core_swap(moved), source ^ 1)
    return whole, all_gains, fetched


def gradient_kernel(pairs, count, turned, pieces, place_ref, *refs):
    total = None
    for i in range(pairs):
        left, right = refs[2 * i], refs[2 * i + 1]
        groups, _, rows, tokens = left.shape
        term = mm(
            left[...].reshape(groups * rows, tokens), right[...], ((1,), (1 if turned else 0,))
        )
        total = term if total is None else total + term
    total = total.reshape(groups, rows, total.shape[-1])
    refs = refs[2 * pairs :]
    arrived = refs[:count]
    for piece in arrived:
        total = total + piece[...].astype(f32)
    if not pieces:
        refs[-1][...] = total.astype(bf16)
        return
    outs, sum_ref = refs[-1 - groups : -1], refs[-1]
    sum_ref[...] = total
    group = place_ref[1]
    for by, out in enumerate(outs):
        out[...] = sum_ref[lax.rem(group + by, groups)].astype(out.dtype)


def gradient_call(left, right, which, turned, arrived, pieces, inside=None):
    groups, chips, rows, tokens = left[0].shape
    group = lax.axis_index("fsdp")
    columns = right[0].shape[0 if turned else 1]
    block = next((b for b in (512, 384) if columns % b == 0), columns)
    if rows % 16 or columns % block:
        total = None
        for a, b in zip(left, right):
            picked = lax.dynamic_index_in_dim(a, which, 1, keepdims=False)
            term = mm(picked.reshape(groups * rows, -1), b, ((1,), (1 if turned else 0,)))
            total = term if total is None else total + term
        total = sum((piece.astype(f32) for piece in arrived), total.reshape(groups, rows, -1))
        if not pieces:
            return total.astype(bf16)
        parts = [
            lax.dynamic_index_in_dim(total, (group + by) % groups, 0, keepdims=False)
            for by in range(groups)
        ]
        return [parts[0]] + [p.astype(bf16) for p in parts[1:]]
    left_spec = pl.BlockSpec((groups, 1, rows, tokens), lambda n, place: (0, place[0], 0, 0))
    if turned:
        right_spec = pl.BlockSpec((block, tokens), lambda n, _: (n, 0))
    else:
        right_spec = pl.BlockSpec((tokens, block), lambda n, _: (0, n))
    sum_spec = pl.BlockSpec((groups, rows, block), lambda n, _: (0, 0, n))
    operands = [v for pair in zip(left, right) for v in pair] + list(arrived)
    if pieces:
        out_specs = [pl.BlockSpec((rows, block), lambda n, _: (0, n))] * groups
        out_shape = [
            jax.ShapeDtypeStruct((rows, columns), bf16 if by else f32) for by in range(groups)
        ]
        scratch = [pltpu.VMEM((groups, rows, block), f32)]
    else:
        first, total, whole = inside or (0, columns, ())
        out_specs, scratch = pl.BlockSpec((groups, rows, block), lambda n, _: (0, 0, first // block + n)), []
        out_shape = jax.ShapeDtypeStruct((groups, rows, total), bf16)
        operands += whole
    return pl.pallas_call(
        functools.partial(gradient_kernel, len(left), len(arrived), turned, pieces),
        grid_spec=pltpu.PrefetchScalarGridSpec(
            num_scalar_prefetch=1,
            grid=(columns // block,),
            in_specs=[left_spec, right_spec] * len(left)
            + [sum_spec] * len(arrived)
            + [pl.BlockSpec(memory_space=pl.ANY)] * (len(operands) - 2 * len(left) - len(arrived)),
            out_specs=out_specs,
            scratch_shapes=scratch,
        ),
        out_shape=out_shape,
        input_output_aliases={len(operands): 0} if inside and inside[2] else {},
        compiler_params=pltpu.CompilerParams(vmem_limit_bytes=40 << 20),
        cost_estimate=SMALL_COST,
        name="gradient_chip" if arrived else "gradient_send",
    )(jnp.stack([which, group]), *operands)


def gradient_products(left, right, turned=False):
    chips, chip = lax.axis_size("ctx") // 2, lax.axis_index("ctx") // 2
    return [
        gradient_call(left, right, (chip + by) % chips, turned, (), False)
        for by in range(1, chips)
    ]


def gradient_send(products):
    return [chip_shift(p, by) for by, p in enumerate(products, 1)]


def gradient_chip(left, right, arrived, turned=False, pieces=False):
    return gradient_call(left, right, lax.axis_index("ctx") // 2, turned, arrived, pieces)


def gradient_groups(pieces):
    return [group_shift(piece, by) if by else piece for by, piece in enumerate(pieces)]


def gradient_scatter(total):
    groups, rows, columns = total.shape
    return lax.psum_scatter(
        total.reshape(groups * rows, columns), "fsdp", scatter_dimension=0, tiled=True
    )


def gradient_sum(terms):
    total = terms[0].astype(f32)
    for term in terms[1:]:
        total = total + term.astype(f32)
    return total


def gain_gradient(weights, gradients, gain):
    total = 0.0
    for weight, gradient in zip(weights, gradients):
        total = total + jnp.sum(weight.astype(f32) * gradient.astype(f32), axis=1)
    return total / gain


def slot_meta(ctx_index, tokens, stripe_row, lengths):
    count = stripe_row.shape[0]
    ends = jnp.cumsum(lengths)
    residue = jnp.sum(jnp.where(jnp.arange(count) == ctx_index, stripe_row, 0))
    packed = jnp.arange(tokens, dtype=jnp.int32) * count + residue
    passed = (packed[:, None] >= ends[None, :]).astype(jnp.int32)
    start = jnp.sum(passed * lengths[None, :], axis=1)
    return packed, start


def rms_normed(values, gain):
    scale_row = lax.rsqrt(jnp.mean(values * values, axis=-1, keepdims=True) + norm_eps)
    return (values * scale_row * gain, scale_row)


def norm_back(grad_normed, values, scale_row, gain):
    unit_rows = values * scale_row
    weighted = grad_normed * gain
    return scale_row * (weighted - unit_rows * jnp.mean(weighted * unit_rows, axis=-1, keepdims=True))


def on_device(
    hidden_in,
    cotangent,
    doc_lengths,
    stripe,
    query_key_value_weight,
    output_weight,
    feedforward_weight,
    gains,
):
    ctx_count, ctx_index = lax.axis_size("ctx"), lax.axis_index("ctx")
    group_count, group = lax.axis_size("fsdp"), lax.axis_index("fsdp")
    core = ctx_index % 2
    tokens, width = hidden_in.shape[1:]
    qkv_columns = query_key_value_weight.shape[1]
    att_columns = output_weight.shape[1]
    units = feedforward_weight.shape[2]
    kv_heads = qkv_columns // ((QUERY_PER_KV + 2) * HEAD_SIZE)

    def share(weight):
        rows = weight.shape[0] // ctx_count
        return lax.dynamic_slice_in_dim(weight, ctx_index * rows, rows, 0)

    tp_index = lax.axis_index("tp")
    out_share = share(output_weight)
    out_other = tp_swap(out_share)
    payload = packed_share(feedforward_weight, out_share, out_other, ctx_index, share)
    wq, gain_rows, fetched = gathered_rows(query_key_value_weight, gains, payload)
    payload = lax.optimization_barrier((payload, fetched[0]))[0]
    others = lax.all_gather(payload, ("fsdp", "ctx"), axis=0, tiled=True)

    lengths, stripe_row = doc_lengths[0], stripe[0]
    packed, start = slot_meta(ctx_index, tokens, stripe_row, lengths)
    frequency = rope_base ** (-(2.0 * jnp.arange(HALF, dtype=f32)) / HEAD_SIZE)
    angles = frequency[:, None] * (packed - start).astype(f32)[None, :]
    cos_table, sin_table = jnp.cos(angles), jnp.sin(angles)
    block_starts = start[::BLOCK] // (ctx_count * BLOCK)
    sources = []
    for by in range(ctx_count // 2):
        source = (ctx_index - 2 * by) % ctx_count
        sources += [source, source ^ 1]
    stripes = jnp.stack(
        [lax.dynamic_index_in_dim(stripe_row, s, 0, keepdims=False) for s in sources]
    )
    meta = (block_starts, stripes, packed[None, :], start[None, :])

    order = Order(lengths[0] > 0)
    touch = lambda *v: v
    x, grad_low = hidden_in[0], cotangent[0]
    rows_dy = order(rows_for_cores, grad_low, core)

    def first_norm(x, gain):
        values = x.astype(f32)
        scale = lax.rsqrt(jnp.mean(values * values, axis=-1, keepdims=True) + norm_eps)
        return (values * scale * gain).astype(bf16), scale

    first_normed, scale_one = order(first_norm, x, gain_rows[0])
    rows_one = order(rows_for_cores, first_normed, core)
    first_normed, tables, *meta = lax.optimization_barrier(
        (first_normed, (cos_table, sin_table), *meta)
    )
    sizes = (kv_heads // 2, kv_heads - kv_heads // 2)
    chunks = range(len(sizes))
    queries, own, moving, pieces, attended, lse = [], [], [], [], [], []
    for c in chunks:
        query, kv_own = order(
            functools.partial(project, first=sum(sizes[:c]), heads=sizes[c]),
            first_normed,
            wq,
            *tables,
        )
        queries.append(query)
        own.append(kv_own)
        moving.append([chip_shift(kv_own, by) for by in range(1, ctx_count // 2)])
    own_swapped = order.apart(swapped_of, *own)
    other_dy, other_one = order.apart(swapped_of, rows_dy[1], rows_one[1])
    left_dy, left_one = (rows_dy[0], other_dy), (rows_one[0], other_one)

    def attend(query, mine, partners, arrived, *meta):
        pieces = [mine, partners]
        for piece in arrived:
            pieces += [piece, core_swap(piece)]
        return attention_forward(query, pieces, *meta), pieces[3::2]

    attended_others = []
    for c in chunks:
        (att, lse_c), swapped = order.apart(
            attend, queries[c], own[c], own_swapped[c], moving[c], *meta
        )
        both = [v for pair in zip(moving[c], swapped) for v in pair]
        pieces.append([own[c], own_swapped[c], *both])
        attended.append(att)
        lse.append(lse_c)
        attended_others.append(tp_swap(att.reshape(-1, tokens)))
    attended_rows = [a.reshape(-1, tokens) for a in attended]
    attended_others[0] = order(lambda v: v, attended_others[0])
    all_attended, other_attended = order.apart(
        lambda *parts: (jnp.concatenate(parts, axis=0), core_swap(jnp.concatenate(parts, axis=0))),
        *attended_rows,
    )
    right_att = (all_attended, other_attended)
    middle, second_normed = order(
        functools.partial(middle_of, first=3 * units),
        attended_rows,
        attended_others,
        tp_index,
        x,
        gain_rows[1:],
        others,
    )

    turned_products = functools.partial(gradient_products, turned=True)
    activated, d_gate, d_up, d_two_part = order(
        functools.partial(feed_forward, units=units), second_normed, grad_low, others
    )
    d_two_sent = tp_send(d_two_part)

    def down_part(activated, normed, left_dy, core):
        inner = Order()
        other = core_swap(activated)
        rows = inner(rows_for_cores, normed, core)
        rows_other = core_swap(rows[1])
        return inner(gradient_products, left_dy, (activated, other)), other, (rows[0], rows_other)

    down_products, other_act, left_two = order.apart(
        down_part, activated, second_normed, left_dy, core
    )
    right_act = (activated, other_act)
    down_arrived = gradient_send(down_products)

    def gate_part(activated, d_gate, d_up, left_two, others):
        inner = Order()
        other_gate = core_swap(d_gate)
        down_sum = inner(functools.partial(down_project, first=2 * units), activated, others)
        gate_products = inner(gradient_products, left_two, (d_gate, other_gate))
        other_up = core_swap(lax.optimization_barrier((d_up, down_sum))[0])
        up_products = inner(gradient_products, left_two, (d_up, other_up))
        early = units // 4
        up_products = [[p[:, :, :early] for p in up_products], [p[:, :, early:] for p in up_products]]
        return gate_products, up_products, down_sum, other_gate, other_up

    gate_products, up_products, down_sum, other_gate, other_up = order.apart(
        gate_part, activated, d_gate, d_up, left_two, others
    )
    right_gate, right_up = (d_gate, other_gate), (d_up, other_up)
    shares = order(
        lambda ffn, qkv: [share(ffn[0]), share(ffn[1]), share(qkv)],
        feedforward_weight,
        query_key_value_weight,
    )
    down_arrived, gate_products, up_products, down_sum, d_two_sent = order(
        touch, down_arrived, gate_products, up_products, down_sum, d_two_sent
    )
    gate_arrived, up_first = gradient_send(gate_products), gradient_send(up_products[0])
    down_scattered = gradient_scatter(order(gradient_chip, left_dy, right_act, down_arrived))
    down_sent = tp_send(down_sum)
    d_branch, d_att = order(
        functools.partial(
            d_middle_of, first=3 * units, parts=[s * QUERY_PER_KV * HEAD_SIZE for s in sizes]
        ),
        d_two_sent,
        middle,
        grad_low,
        gain_rows[1:],
        others,
    )
    d_att = [d.reshape(-1, QUERY_PER_KV, HEAD_SIZE, tokens) for d in d_att]

    def attend_back(query, d_att, attended, lse, pieces, *meta):
        d_query, *d_pieces = attention_backward(query, d_att, attended, lse, pieces, *meta)
        sums = [
            (mine.astype(f32) + core_swap(partners).astype(f32)).astype(bf16)
            for mine, partners in zip(d_pieces[::2], d_pieces[1::2])
        ]
        return d_query, sums

    def attention_step(c):
        d_query, sums = order.apart(
            attend_back, queries[c], d_att[c], attended[c], lse[c], pieces[c], *meta
        )
        return d_query, [chip_shift(s, -by) if by else s for by, s in enumerate(sums)]

    d_query_0, d_kv_0 = attention_step(0)
    gate_arrived, up_products = order(touch, gate_arrived, up_products)
    up_second = gradient_send(up_products[1])
    gate_chip = order(gradient_chip, left_two, right_gate, gate_arrived)
    gate_chip, up_first = order(touch, gate_chip, up_first)
    gate_scattered = gradient_scatter(gate_chip)
    d_query_1, d_kv_1 = attention_step(1)

    def branch_part(d_branch, core, right_att):
        inner = Order()
        rows = inner(rows_for_cores, d_branch, core)
        left = (rows[0], core_swap(rows[1]))
        return inner(turned_products, left, right_att), left

    out_products, left_branch = order.apart(branch_part, d_branch, core, right_att)
    up_first, up_second = order(touch, up_first, up_second)
    up_arrived = [jnp.concatenate(pair, axis=2) for pair in zip(up_first, up_second)]
    up_chip = order(gradient_chip, left_two, right_up, up_arrived)
    d_kv_0, d_kv_1, down_sent, up_chip = order(touch, d_kv_0, d_kv_1, down_sent, up_chip)
    up_scattered = gradient_scatter(up_chip)

    def project_back(out_products, d_query, d_kv, wq, *tables):
        inner = Order()
        out_arrived = gradient_send(out_products)
        parts = [inner(turned_back, q, kv, *tables) for q, kv in zip(d_query, d_kv)]
        return inner(d_one_of, parts, wq), parts, out_arrived

    d_one_part, d_proj, out_arrived = order.apart(
        project_back, out_products, [d_query_0, d_query_1], [d_kv_0, d_kv_1], wq, *tables
    )
    d_one_sent = tp_send(d_one_part)

    grad_down = order(lambda v: v.astype(f32), down_scattered)
    gate_scattered = order(touch, gate_scattered)[0]

    def tail(left_one, d_proj, left_branch, right_att, out_arrived, middle, down_sent):
        inner = Order()
        finish = functools.partial(gradient_chip, turned=True, pieces=True)
        other_proj = [core_swap(p) for p in d_proj]
        chip = inner(finish, left_branch, right_att, out_arrived)
        right_proj = list(zip(d_proj, inner(touch, *other_proj)))
        products = inner(turned_products, left_one, right_proj[0])
        arrived = gradient_send(products)
        terms = gradient_groups(lax.optimization_barrier((chip, products))[0])
        products = inner(turned_products, left_one, right_proj[1])
        hidden_out = inner(lambda m, s: (m + tp_add(s)).astype(bf16), middle, down_sent)
        grad_out = inner(gradient_sum, terms)
        arrived_1 = gradient_send(lax.optimization_barrier((products, grad_out))[0])
        terms = gradient_groups(inner(finish, left_one, right_proj[0], arrived))
        chip = inner(finish, left_one, right_proj[1], arrived_1)
        return grad_out, hidden_out, inner(gradient_sum, terms), chip

    grad_out, hidden_out, grad_qkv_0, chip = order.apart(
        tail, left_one, d_proj, left_branch, right_att, out_arrived, middle, down_sent
    )
    terms = gradient_groups(chip)
    own_gains = lax.dynamic_slice_in_dim(
        gains, ctx_index * out_share.shape[0], out_share.shape[0], 1
    ).astype(f32)

    def ffn_gradient(down, gate, up):
        gain = gain_gradient(shares[:2], [gate, up], own_gains[1])
        return jnp.stack([gate.astype(f32), up.astype(f32), down], axis=0), gain

    grad_ffn, gain_two = order(ffn_gradient, grad_down, gate_scattered, up_scattered)
    grad_in = order(input_gradient, d_one_sent, x, d_branch, gain_rows[:1])

    def qkv_gradient(first, terms, gain_two):
        whole = jnp.concatenate([first, gradient_sum(terms)], axis=1)
        gain_one = gain_gradient(shares[2:], [whole], own_gains[0])
        return jnp.stack([gain_one, gain_two], axis=0), whole

    grad_gains, grad_qkv = order(qkv_gradient, grad_qkv_0, terms, gain_two)
    grad_gains = grad_gains + tp_swap(grad_gains)
    return (hidden_out[None], grad_in[None], grad_qkv, grad_out, grad_ffn, grad_gains)


def solution(mesh):
    return jax.shard_map(
        on_device,
        mesh=mesh,
        in_specs=(
            P("fsdp", "ctx", None),
            P("fsdp", "ctx", None),
            P("fsdp", None),
            P("fsdp", None),
            P("fsdp", "tp"),
            P("fsdp", "tp"),
            P(None, "fsdp", "tp"),
            P(None, "fsdp"),
        ),
        out_specs=(
            P("fsdp", "ctx", None),
            P("fsdp", "ctx", None),
            P(("fsdp", "ctx"), "tp"),
            P(("fsdp", "ctx"), "tp"),
            P(None, ("fsdp", "ctx"), "tp"),
            P(None, ("fsdp", "ctx")),
        ),
        check_vma=False,
    )
```

```python
import functools
import math

import jax
import jax.numpy as jnp
from jax import lax
from jax.experimental import pallas as pl
from jax.experimental.pallas import tpu as pltpu
from jax.sharding import PartitionSpec as P

HEAD_SIZE = 96
QUERY_PER_KV = 2
HALF = HEAD_SIZE // 2
BLOCK = 128

norm_eps = 1e-05
rope_base = 100000.0
masked_score = -1e30
SCORE_SCALE = HEAD_SIZE ** (-0.5)
SCORE_SCALE_2 = SCORE_SCALE * math.log2(math.e)

SMALL_COST = pl.CostEstimate(flops=1, bytes_accessed=1, transcendentals=0)

bf16 = jnp.bfloat16
f32 = jnp.float32


def mm(a, b, contract=((1,), (0,))):
    return lax.dot_general(a, b, (contract, ((), ())), preferred_element_type=f32)


def fill_keys(heads, count, blocks, kv_refs, kn_ref, kt_ref, vn_ref, vt_ref):
    for h in range(heads):
        for s in range(count):
            for b in range(blocks):
                columns = slice(b * BLOCK, (b + 1) * BLOCK)
                places = slice(s * BLOCK, (s + 1) * BLOCK)
                key = kv_refs[s][h, 0, :, columns]
                value = kv_refs[s][h, 1, :, columns]
                kn_ref[h, b, places, :] = key.T
                if kt_ref is not None:
                    kt_ref[h, b, :, places] = key
                if vn_ref is not None:
                    vn_ref[h, b, places, :] = value.T
                if vt_ref is not None:
                    vt_ref[h, b, :, places] = value


def fill_places(count, stripes_ref, place_ref):
    step = lax.broadcasted_iota(jnp.int32, (BLOCK, QUERY_PER_KV * BLOCK), 0) * count
    for s in range(count):
        place_ref[s * BLOCK : (s + 1) * BLOCK, :] = step + stripes_ref[s]


def twice(row):
    return jnp.concatenate([row] * QUERY_PER_KV, axis=1)


def block_of(ref, h, i):
    columns = slice(i * BLOCK, (i + 1) * BLOCK)
    return jnp.concatenate([ref[h, g, :, columns] for g in range(QUERY_PER_KV)], axis=1)


def allowed_keys(place_ref, count, b, place_q, start_q):
    place, offset = place_ref[...], b * (BLOCK * count)
    allowed = place >= start_q - offset
    return allowed if place_q is None else allowed & (place <= place_q - offset)


def forward_kernel(heads, count, blocks, starts_ref, stripes_ref, place_q_ref, start_q_ref, q_ref, *rest):
    kv_refs = rest[:count]
    o_ref, lse_ref, kn_ref, vt_ref, place_ref = rest[count:]
    fill_keys(heads, count, blocks, kv_refs, kn_ref, None, None, vt_ref)
    fill_places(count, stripes_ref, place_ref)
    for i in range(blocks):
        columns = slice(i * BLOCK, (i + 1) * BLOCK)
        queries = [block_of(q_ref, h, i) for h in range(heads)]
        place_q = twice(place_q_ref[:, columns])
        start_q = twice(start_q_ref[:, columns])

        def scores_of(b, place_q):
            allowed = allowed_keys(place_ref, count, b, place_q, start_q)
            scores = [mm(kn_ref[h, b], queries[h]) for h in range(heads)]
            return [jnp.where(allowed, s * SCORE_SCALE_2, masked_score) for s in scores]

        state = []
        for h, scores in enumerate(scores_of(i, place_q)):
            top = jnp.max(scores, axis=0, keepdims=True)
            weights = jnp.exp2(scores - top)
            total = jnp.sum(weights, axis=0, keepdims=True)
            state.append((top, total, mm(vt_ref[h, i], weights.astype(bf16))))

        def step(b, carry):
            result = []
            for h, scores in enumerate(scores_of(b, None)):
                top, total, accum = carry[h]
                new_top = jnp.maximum(top, jnp.max(scores, axis=0, keepdims=True))
                fade = jnp.exp2(top - new_top)
                weights = jnp.exp2(scores - new_top)
                total = total * fade + jnp.sum(weights, axis=0, keepdims=True)
                accum = accum * fade + mm(vt_ref[h, b], weights.astype(bf16))
                result.append((new_top, total, accum))
            return tuple(result)

        state = lax.fori_loop(starts_ref[i], i, step, tuple(state)) if i else state
        for h, (top, total, accum) in enumerate(state):
            result = (accum / total).astype(bf16)
            lse = top + jnp.log2(total)
            for g in range(QUERY_PER_KV):
                part = slice(g * BLOCK, (g + 1) * BLOCK)
                o_ref[h, g, :, columns] = result[:, part]
                lse_ref[h, g : g + 1, columns] = lse[:, part]


def backward_kernel(
    heads, count, blocks, starts_ref, stripes_ref, place_q_ref, start_q_ref, q_ref, do_ref, o_ref, lse_ref, *rest
):
    kv_refs = rest[:count]
    dq_ref = rest[count]
    dkv_refs = rest[count + 1 : 2 * count + 1]
    kn_ref, kt_ref, vn_ref, place_ref, dk_ref, dv_ref = rest[2 * count + 1 :]
    fill_keys(heads, count, blocks, kv_refs, kn_ref, kt_ref, vn_ref, None)
    fill_places(count, stripes_ref, place_ref)
    for i in range(blocks):
        columns = slice(i * BLOCK, (i + 1) * BLOCK)
        place_q = twice(place_q_ref[:, columns])
        start_q = twice(start_q_ref[:, columns])
        parts = []
        for h in range(heads):
            query, d_out, out = (block_of(ref, h, i) for ref in (q_ref, do_ref, o_ref))
            delta = jnp.sum(d_out.astype(f32) * out.astype(f32), axis=0, keepdims=True)
            lse = jnp.concatenate(
                [lse_ref[h, g : g + 1, columns] for g in range(QUERY_PER_KV)], axis=1
            )
            parts.append((query, query.T, d_out, d_out.T, delta, lse))

        def terms(b, place_q, first):
            allowed = allowed_keys(place_ref, count, b, place_q, start_q)
            d_queries = []
            for h, (query, query_rows, d_out, d_out_rows, delta, lse) in enumerate(parts):
                scores = mm(kn_ref[h, b], query)
                d_prob = mm(vn_ref[h, b], d_out)
                probs = jnp.exp2(jnp.where(allowed, scores * SCORE_SCALE_2, masked_score) - lse)
                d_score = (probs * (d_prob - delta)).astype(bf16)
                d_value = mm(probs.astype(bf16), d_out_rows)
                d_key = mm(d_score, query_rows)
                if first:
                    dv_ref[h, b] = d_value
                    dk_ref[h, b] = d_key
                else:
                    dv_ref[h, b] += d_value
                    dk_ref[h, b] += d_key
                d_queries.append(mm(kt_ref[h, b], d_score))
            return d_queries

        def step(b, carry):
            return tuple(a + t for a, t in zip(carry, terms(b, None, False)))

        d_queries = tuple(terms(i, place_q, True))
        if i:
            d_queries = lax.fori_loop(starts_ref[i], i, step, d_queries)
        for h in range(heads):
            for g in range(QUERY_PER_KV):
                dq_ref[h, g, :, columns] = d_queries[h][:, g * BLOCK : (g + 1) * BLOCK] * SCORE_SCALE
    for h in range(heads):
        for s in range(count):
            places = slice(s * BLOCK, (s + 1) * BLOCK)
            for b in range(blocks):
                columns = slice(b * BLOCK, (b + 1) * BLOCK)
                dkv_refs[s][h, 0, :, columns] = (dk_ref[h, b, places, :] * SCORE_SCALE).T.astype(bf16)
                dkv_refs[s][h, 1, :, columns] = dv_ref[h, b, places, :].T.astype(bf16)


def head_spec(heads, *dims):
    return pl.BlockSpec((heads, *dims), lambda n, *_: (0,) * (1 + len(dims)))


def row_spec(tokens):
    return pl.BlockSpec((1, tokens), lambda n, *_: (0, 0))


def attention_forward(queries, pieces, starts, stripes, place, start):
    heads, _, _, tokens = queries.shape
    count, blocks = len(pieces), tokens // BLOCK
    keys = count * BLOCK
    per_query = head_spec(heads, QUERY_PER_KV, HEAD_SIZE, tokens)
    per_kv = head_spec(heads, 2, HEAD_SIZE, tokens)
    return pl.pallas_call(
        functools.partial(forward_kernel, heads, count, blocks),
        grid_spec=pltpu.PrefetchScalarGridSpec(
            num_scalar_prefetch=2,
            grid=(1,),
            in_specs=[row_spec(tokens)] * 2 + [per_query] + [per_kv] * count,
            out_specs=[per_query, head_spec(heads, QUERY_PER_KV, tokens)],
            scratch_shapes=[
                pltpu.VMEM((heads, blocks, keys, HEAD_SIZE), bf16),
                pltpu.VMEM((heads, blocks, HEAD_SIZE, keys), bf16),
                pltpu.VMEM((keys, QUERY_PER_KV * BLOCK), jnp.int32),
            ],
        ),
        out_shape=[
            jax.ShapeDtypeStruct(queries.shape, bf16),
            jax.ShapeDtypeStruct((heads, QUERY_PER_KV, tokens), f32),
        ],
        compiler_params=pltpu.CompilerParams(vmem_limit_bytes=40 << 20),
        cost_estimate=SMALL_COST,
        name="attention_forward",
    )(starts, stripes, place, start, queries, *pieces)


def attention_backward(queries, d_att, attended, lse, pieces, starts, stripes, place, start):
    heads, _, _, tokens = queries.shape
    count, blocks = len(pieces), tokens // BLOCK
    keys = count * BLOCK
    per_query = head_spec(heads, QUERY_PER_KV, HEAD_SIZE, tokens)
    per_kv = head_spec(heads, 2, HEAD_SIZE, tokens)
    return pl.pallas_call(
        functools.partial(backward_kernel, heads, count, blocks),
        grid_spec=pltpu.PrefetchScalarGridSpec(
            num_scalar_prefetch=2,
            grid=(1,),
            in_specs=[row_spec(tokens)] * 2
            + [per_query] * 3
            + [head_spec(heads, QUERY_PER_KV, tokens)]
            + [per_kv] * count,
            out_specs=[per_query] + [per_kv] * count,
            scratch_shapes=[
                pltpu.VMEM((heads, blocks, keys, HEAD_SIZE), bf16),
                pltpu.VMEM((heads, blocks, HEAD_SIZE, keys), bf16),
                pltpu.VMEM((heads, blocks, keys, HEAD_SIZE), bf16),
                pltpu.VMEM((keys, QUERY_PER_KV * BLOCK), jnp.int32),
                pltpu.VMEM((heads, blocks, keys, HEAD_SIZE), f32),
                pltpu.VMEM((heads, blocks, keys, HEAD_SIZE), f32),
            ],
        ),
        out_shape=[jax.ShapeDtypeStruct(queries.shape, f32)]
        + [jax.ShapeDtypeStruct(pieces[0].shape, bf16)] * count,
        compiler_params=pltpu.CompilerParams(vmem_limit_bytes=48 << 20),
        cost_estimate=SMALL_COST,
        name="attention_backward",
    )(starts, stripes, place, start, queries, d_att, attended, lse, *pieces)


def pack_kernel(_, ffn_ref, out_ref, other_ref, packed_ref):
    units, columns = ffn_ref.shape[2], out_ref.shape[1]
    for i in range(3):
        packed_ref[:, i * units : (i + 1) * units] = ffn_ref[i]
    packed_ref[:, 3 * units : 3 * units + columns] = out_ref[...]
    packed_ref[:, 3 * units + columns :] = other_ref[...]


def packed_share(feedforward_weight, out_share, out_other, index, share_of):
    rows, columns = out_share.shape
    units = feedforward_weight.shape[2]
    if rows % 16:
        parts = [share_of(feedforward_weight[i]) for i in range(3)]
        return jnp.concatenate([*parts, out_share, out_other], axis=1)
    whole = pl.BlockSpec((rows, columns), lambda n, _: (0, 0))
    width = 3 * units + 2 * columns
    return pl.pallas_call(
        pack_kernel,
        grid_spec=pltpu.PrefetchScalarGridSpec(
            num_scalar_prefetch=1,
            grid=(1,),
            in_specs=[
                pl.BlockSpec((3, rows, units), lambda n, place: (0, place[0], 0)),
                whole,
                whole,
            ],
            out_specs=pl.BlockSpec((rows, width), lambda n, _: (0, 0)),
        ),
        out_shape=jax.ShapeDtypeStruct((rows, width), bf16),
        compiler_params=pltpu.CompilerParams(vmem_limit_bytes=60 << 20),
        cost_estimate=SMALL_COST,
        name="pack",
    )(index[None], feedforward_weight, out_share, out_other)


def input_gradient_kernel(mine_ref, other_ref, x_ref, d_mid_ref, gain_ref, out_ref):
    x = x_ref[...].astype(f32)
    scale = lax.rsqrt(jnp.mean(x * x, axis=-1, keepdims=True) + norm_eps)
    unit = x * scale
    weighted = (mine_ref[...].astype(f32) + other_ref[...].astype(f32)) * gain_ref[...]
    out_ref[...] = (
        d_mid_ref[...].astype(f32)
        + scale * (weighted - unit * jnp.mean(weighted * unit, axis=-1, keepdims=True))
    ).astype(bf16)


def input_gradient(sent, x, d_mid, gain):
    tokens, width = x.shape
    block = 256
    here = pl.BlockSpec((block, width), lambda n: (n, 0))
    return pl.pallas_call(
        input_gradient_kernel,
        grid=(tokens // block,),
        in_specs=[here] * 4 + [pl.BlockSpec((1, width), lambda n: (0, 0))],
        out_specs=here,
        out_shape=jax.ShapeDtypeStruct((tokens, width), bf16),
        compiler_params=pltpu.CompilerParams(vmem_limit_bytes=32 << 20),
        cost_estimate=SMALL_COST,
        name="input_gradient",
    )(*sent, x, d_mid, gain)


def project_kernel(x_ref, w_ref, cos_ref, sin_ref, q_ref, kv_ref):
    projected = mm(x_ref[...], w_ref[...]).T
    cos_table, sin_table = cos_ref[...], sin_ref[...]
    for j in range(QUERY_PER_KV + 1):
        first = j * HEAD_SIZE
        front = projected[first : first + HALF]
        back = projected[first + HALF : first + HEAD_SIZE]
        target = q_ref.at[0, j] if j < QUERY_PER_KV else kv_ref.at[0, 0]
        target[:HALF, :] = (front * cos_table - back * sin_table).astype(bf16)
        target[HALF:, :] = (back * cos_table + front * sin_table).astype(bf16)
    kv_ref[0, 1] = projected[(QUERY_PER_KV + 1) * HEAD_SIZE :].astype(bf16)


def project(normed, weight, cos_table, sin_table, first, heads):
    tokens, width = normed.shape
    columns = (QUERY_PER_KV + 2) * HEAD_SIZE
    whole = lambda shape: pl.BlockSpec(shape, lambda h: (0, 0))
    return pl.pallas_call(
        project_kernel,
        grid=(heads,),
        in_specs=[
            whole((tokens, width)),
            pl.BlockSpec((width, columns), lambda h: (0, first + h)),
            whole((HALF, tokens)),
            whole((HALF, tokens)),
        ],
        out_specs=[
            pl.BlockSpec((1, QUERY_PER_KV, HEAD_SIZE, tokens), lambda h: (h, 0, 0, 0)),
            pl.BlockSpec((1, 2, HEAD_SIZE, tokens), lambda h: (h, 0, 0, 0)),
        ],
        out_shape=[
            jax.ShapeDtypeStruct((heads, QUERY_PER_KV, HEAD_SIZE, tokens), bf16),
            jax.ShapeDtypeStruct((heads, 2, HEAD_SIZE, tokens), bf16),
        ],
        compiler_params=pltpu.CompilerParams(vmem_limit_bytes=40 << 20),
        cost_estimate=SMALL_COST,
        name="project",
    )(normed, weight, cos_table, sin_table)


def middle_kernel(count, tp_ref, x_ref, gain_ref, *refs):
    mine, others = refs[:count], refs[count : 2 * count]
    w_first, w_second, middle_ref, normed_ref, first_ref, second_ref = refs[2 * count :]

    def fill(first, second):
        first_ref[...] = jnp.concatenate([r[...] for r in first], axis=0).T
        second_ref[...] = jnp.concatenate([r[...] for r in second], axis=0).T

    @pl.when(tp_ref[0] == 0)
    def _():
        fill(mine, others)

    @pl.when(tp_ref[0] == 1)
    def _():
        fill(others, mine)

    branch = mm(first_ref[...], w_first[...], ((1,), (1,))) + mm(
        second_ref[...], w_second[...], ((1,), (1,))
    )
    middle = x_ref[...].astype(f32) + branch
    middle_ref[...] = middle
    scale = lax.rsqrt(jnp.mean(middle * middle, axis=-1, keepdims=True) + norm_eps)
    normed_ref[...] = (middle * scale * gain_ref[...]).astype(bf16)


def middle_of(mine, others, tp_index, x, gain, weight, first):
    tokens, width = x.shape
    features = sum(p.shape[0] for p in mine)
    block = 256
    half = first // features
    token_spec = pl.BlockSpec((block, width), lambda n, _: (n, 0))
    return pl.pallas_call(
        functools.partial(middle_kernel, len(mine)),
        grid_spec=pltpu.PrefetchScalarGridSpec(
            num_scalar_prefetch=1,
            grid=(tokens // block,),
            in_specs=[token_spec, pl.BlockSpec((1, width), lambda n, _: (0, 0))]
            + [pl.BlockSpec((p.shape[0], block), lambda n, _: (0, n)) for p in (*mine, *others)]
            + [
                pl.BlockSpec((width, features), lambda n, tp: (0, half + tp[0])),
                pl.BlockSpec((width, features), lambda n, tp: (0, half + 1 - tp[0])),
            ],
            out_specs=[token_spec] * 2,
            scratch_shapes=[pltpu.VMEM((block, features), bf16)] * 2,
        ),
        out_shape=[
            jax.ShapeDtypeStruct((tokens, width), f32),
            jax.ShapeDtypeStruct((tokens, width), bf16),
        ],
        compiler_params=pltpu.CompilerParams(vmem_limit_bytes=40 << 20),
        cost_estimate=SMALL_COST,
        name="middle",
    )(tp_index[None], x, gain, *mine, *others, weight, weight)


def down_kernel(a_ref, w_ref, out_ref):
    out_ref[...] = mm(a_ref[...], w_ref[...], ((1,), (1,))).astype(bf16)


def down_project(activated, weight, first):
    tokens, units = activated.shape
    width, block = weight.shape[0], 512
    return pl.pallas_call(
        down_kernel,
        grid=(width // block,),
        in_specs=[
            pl.BlockSpec((tokens, units), lambda n: (0, 0)),
            pl.BlockSpec((block, units), lambda n: (n, first // units)),
        ],
        out_specs=pl.BlockSpec((tokens, block), lambda n: (0, n)),
        out_shape=jax.ShapeDtypeStruct((tokens, width), bf16),
        compiler_params=pltpu.CompilerParams(vmem_limit_bytes=40 << 20),
        cost_estimate=SMALL_COST,
        name="down_project",
    )(activated, weight)


def d_middle_kernel(
    mine_ref, other_ref, middle_ref, dy_ref, gain_ref, w_ref, branch_ref, *d_att_refs
):
    middle = middle_ref[...]
    scale = lax.rsqrt(jnp.mean(middle * middle, axis=-1, keepdims=True) + norm_eps)
    unit = middle * scale
    weighted = (mine_ref[...].astype(f32) + other_ref[...].astype(f32)) * gain_ref[...]
    d_mid = dy_ref[...].astype(f32) + scale * (
        weighted - unit * jnp.mean(weighted * unit, axis=-1, keepdims=True)
    )
    branch = d_mid.astype(bf16)
    branch_ref[...] = branch
    d_att = mm(branch, w_ref[...]).astype(bf16).T
    first = 0
    for ref in d_att_refs:
        ref[...] = d_att[first : first + ref.shape[0]]
        first += ref.shape[0]


def d_middle_of(sent, middle, d_out, gain, weight, first, parts):
    mine, other = sent
    tokens, width = middle.shape
    features = sum(parts)
    block = 256
    here = pl.BlockSpec((block, width), lambda n: (n, 0))
    row = pl.BlockSpec((1, width), lambda n: (0, 0))
    branch, *d_att = pl.pallas_call(
        d_middle_kernel,
        grid=(tokens // block,),
        in_specs=[here, here, here, here, row]
        + [pl.BlockSpec((width, features), lambda n: (0, first // features))],
        out_specs=[here] + [pl.BlockSpec((p, block), lambda n: (0, n)) for p in parts],
        out_shape=[jax.ShapeDtypeStruct((tokens, width), bf16)]
        + [jax.ShapeDtypeStruct((p, tokens), bf16) for p in parts],
        compiler_params=pltpu.CompilerParams(vmem_limit_bytes=48 << 20),
        cost_estimate=SMALL_COST,
        name="d_middle",
    )(mine, other, middle, d_out, gain, weight)
    return branch, d_att


def turn_back_kernel(cos_ref, sin_ref, dq_ref, *refs):
    kv_refs, out_ref = refs[:-1], refs[-1]
    cos_table, sin_table = cos_ref[...], sin_ref[...]
    total = kv_refs[0][0].astype(f32)
    for ref in kv_refs[1:]:
        total = total + ref[0].astype(f32)
    for j in range(QUERY_PER_KV + 1):
        vector = dq_ref[0, j] if j < QUERY_PER_KV else total[0]
        front, back = vector[:HALF], vector[HALF:]
        first = j * HEAD_SIZE
        out_ref[first : first + HALF, :] = (front * cos_table + back * sin_table).astype(bf16)
        out_ref[first + HALF : first + HEAD_SIZE, :] = (
            back * cos_table - front * sin_table
        ).astype(bf16)
    out_ref[(QUERY_PER_KV + 1) * HEAD_SIZE :, :] = total[1].astype(bf16)


def turned_back(d_query, d_kv_terms, cos_table, sin_table):
    heads, _, _, tokens = d_query.shape
    columns = (QUERY_PER_KV + 2) * HEAD_SIZE
    whole = pl.BlockSpec((HALF, tokens), lambda h: (0, 0))
    head = lambda n: pl.BlockSpec((1, n, HEAD_SIZE, tokens), lambda h: (h, 0, 0, 0))
    return pl.pallas_call(
        turn_back_kernel,
        grid=(heads,),
        in_specs=[whole, whole, head(QUERY_PER_KV)] + [head(2)] * len(d_kv_terms),
        out_specs=pl.BlockSpec((columns, tokens), lambda h: (h, 0)),
        out_shape=jax.ShapeDtypeStruct((heads * columns, tokens), bf16),
        compiler_params=pltpu.CompilerParams(vmem_limit_bytes=32 << 20),
        cost_estimate=SMALL_COST,
        name="turn_back",
    )(cos_table, sin_table, d_query, *d_kv_terms)


def d_one_kernel(count, *refs):
    parts, w_ref, out_ref, rows_ref = refs[:count], refs[count], refs[count + 1], refs[count + 2]

    @pl.when(pl.program_id(0) == 0)
    def _():
        first = 0
        for part in parts:
            columns = part.shape[0]
            rows_ref[:, first : first + columns] = part[...].T
            first += columns

    out_ref[...] = mm(rows_ref[...], w_ref[...], ((1,), (1,))).astype(bf16)


def d_one_of(parts, weight):
    width, columns = weight.shape
    tokens, block = parts[0].shape[1], 512
    return pl.pallas_call(
        functools.partial(d_one_kernel, len(parts)),
        grid=(width // block,),
        in_specs=[pl.BlockSpec(p.shape, lambda n: (0, 0)) for p in parts]
        + [pl.BlockSpec((block, columns), lambda n: (n, 0))],
        out_specs=pl.BlockSpec((tokens, block), lambda n: (0, n)),
        out_shape=jax.ShapeDtypeStruct((tokens, width), bf16),
        scratch_shapes=[pltpu.VMEM((tokens, columns), bf16)],
        compiler_params=pltpu.CompilerParams(vmem_limit_bytes=40 << 20),
        cost_estimate=SMALL_COST,
        name="d_one",
    )(*parts, weight)


def ffn_kernel(
    h_ref, dy_ref, wg_ref, wu_ref, wd_ref, act_ref, dg_ref, du_ref, out_ref, acc_ref
):
    step = pl.program_id(0)
    w_gate, w_up = wg_ref[...], wu_ref[...]
    gate = mm(h_ref[...], w_gate)
    up = mm(h_ref[...], w_up)
    d_act = mm(dy_ref[...], wd_ref[...])
    sigmoid_gate = jax.nn.sigmoid(gate)
    silu_gate = gate * sigmoid_gate
    act_ref[...] = (silu_gate * up).astype(bf16)
    d_gate = (d_act * up * sigmoid_gate * (1.0 + gate * (1.0 - sigmoid_gate))).astype(bf16)
    d_up = (d_act * silu_gate).astype(bf16)
    dg_ref[...] = d_gate
    du_ref[...] = d_up
    term = mm(d_gate, w_gate, ((1,), (1,))) + mm(d_up, w_up, ((1,), (1,)))

    @pl.when(step == 0)
    def _():
        acc_ref[...] = term

    @pl.when(step > 0)
    def _():
        acc_ref[...] += term

    @pl.when(step == pl.num_programs(0) - 1)
    def _():
        out_ref[...] = acc_ref[...].astype(bf16)


FFN_BLOCK = 512


def feed_forward(normed, d_out, weights, units):
    tokens, width = normed.shape
    weight_spec = lambda i: pl.BlockSpec(
        (width, FFN_BLOCK), lambda n: (0, i * units // FFN_BLOCK + n)
    )
    column_spec = pl.BlockSpec((tokens, FFN_BLOCK), lambda n: (0, n))
    whole = pl.BlockSpec((tokens, width), lambda n: (0, 0))
    return pl.pallas_call(
        ffn_kernel,
        grid=(units // FFN_BLOCK,),
        in_specs=[whole, whole] + [weight_spec(i) for i in range(3)],
        out_specs=[column_spec] * 3 + [whole],
        out_shape=[jax.ShapeDtypeStruct((tokens, units), bf16)] * 3
        + [jax.ShapeDtypeStruct((tokens, width), bf16)],
        scratch_shapes=[pltpu.VMEM((tokens, width), f32)],
        compiler_params=pltpu.CompilerParams(vmem_limit_bytes=56 << 20),
        cost_estimate=SMALL_COST,
        name="feed_forward",
    )(normed, d_out, weights, weights, weights)


def turn_kernel(chips, rows, core_ref, x_ref, mine_ref, other_ref, turned_ref):
    turned_ref[...] = x_ref[...].T
    core = core_ref[0]
    for chip in range(chips):
        for ref, which in ((mine_ref, core), (other_ref, 1 - core)):
            first = pl.multiple_of((chip * 2 + which) * rows, 16)
            ref[0, chip] = turned_ref[pl.ds(first, rows), :]


def rows_for_cores(activation, core):
    tokens, width = activation.shape
    groups, chips = lax.axis_size("fsdp"), lax.axis_size("ctx") // 2
    rows = width // (groups * chips * 2)
    shape = (groups, chips, rows, tokens)
    if rows % 16 or (width // groups) % 128:
        turned = activation.T.reshape(groups, chips, 2, rows, tokens)
        return tuple(
            lax.dynamic_index_in_dim(turned, c, 2, keepdims=False) for c in (core, 1 - core)
        )
    spec = pl.BlockSpec((1, chips, rows, tokens), lambda g, _: (g, 0, 0, 0))
    return pl.pallas_call(
        functools.partial(turn_kernel, chips, rows),
        grid_spec=pltpu.PrefetchScalarGridSpec(
            num_scalar_prefetch=1,
            grid=(groups,),
            in_specs=[pl.BlockSpec((tokens, width // groups), lambda g, _: (0, g))],
            out_specs=[spec, spec],
            scratch_shapes=[pltpu.VMEM((width // groups, tokens), bf16)],
        ),
        out_shape=[jax.ShapeDtypeStruct(shape, bf16)] * 2,
        compiler_params=pltpu.CompilerParams(vmem_limit_bytes=32 << 20),
        cost_estimate=SMALL_COST,
        name="turn_rows",
    )(core[None], activation)


class Order:
    def __init__(self, always=None):
        self.last = ()
        self.always = always

    def __call__(self, function, *args):
        leaves, tree = jax.tree.flatten(args)
        held = lax.optimization_barrier((*leaves, *self.last))
        result = function(*jax.tree.unflatten(tree, held[: len(leaves)]))
        self.last = (jax.tree.leaves(result)[0],)
        return result

    def apart(self, function, *args):
        def guarded(*args):
            shapes = jax.eval_shape(function, *args)
            nothing = lambda *_: jax.tree.map(lambda s: jnp.zeros(s.shape, s.dtype), shapes)
            return lax.cond(self.always, function, nothing, *args)

        return self(guarded, *args)


def swapped_of(*values):
    return [core_swap(v) for v in values]


def core_swap(value):
    size = lax.axis_size("ctx")
    return lax.ppermute(value, "ctx", [(i, i ^ 1) for i in range(size)])


def chip_shift(value, by):
    size = lax.axis_size("ctx")
    return lax.ppermute(value, "ctx", [(i, (i + 2 * by) % size) for i in range(size)])


def group_shift(value, by):
    size = lax.axis_size("fsdp")
    return lax.ppermute(value, "fsdp", [(i, (i + by) % size) for i in range(size)])


def tp_swap(value):
    return lax.ppermute(value, "tp", [(0, 1), (1, 0)])


def tp_send(part):
    part = lax.optimization_barrier(part)
    return part, tp_swap(part)


def tp_add(sent):
    mine, other = sent
    return mine.astype(f32) + other.astype(f32)


def both_cores(value):
    return value, core_swap(value)


def gathered_rows(weight, gains, hold):
    groups, count = lax.axis_size("fsdp"), lax.axis_size("ctx")
    group, index = lax.axis_index("fsdp"), lax.axis_index("ctx")
    rows, columns = weight.shape
    share = rows // count
    mine = lax.dynamic_slice_in_dim(weight, index * share, share, 0)
    extra = jnp.pad(gains, ((0, 16 - gains.shape[0]), (0, columns - gains.shape[1])))
    mine = jnp.concatenate([mine, extra], axis=0)
    fetched = [group_shift(mine, by) for by in range(1, groups)]
    stack = jnp.stack([gains] + [p[share : share + 2, : gains.shape[1]] for p in fetched], axis=0)
    all_gains = jnp.concatenate(
        [
            lax.dynamic_index_in_dim(stack, (group - i) % groups, 0, keepdims=False)
            for i in range(groups)
        ],
        axis=1,
    ).astype(f32)
    weight, _ = lax.optimization_barrier((weight, hold))
    whole = jnp.zeros((groups * rows, columns), weight.dtype)
    whole = lax.dynamic_update_slice_in_dim(whole, weight, group * rows, 0)
    pieces = jnp.stack([p[:share] for p in fetched], axis=0)

    def placed(whole, pieces, source):
        for by in range(1, groups):
            first = (group - by) % groups * rows + source * share
            whole = lax.dynamic_update_slice_in_dim(whole, pieces[by - 1], first, 0)
        return whole

    passed = [pieces] + [chip_shift(pieces, by) for by in range(1, count // 2)]
    for by, moved in enumerate(passed):
        source = (index - 2 * by) % count
        whole = placed(whole, moved, source)
        whole = placed(whole, core_swap(moved), source ^ 1)
    return whole, all_gains, fetched


def gradient_kernel(pairs, count, turned, pieces, place_ref, *refs):
    total = None
    for i in range(pairs):
        left, right = refs[2 * i], refs[2 * i + 1]
        groups, _, rows, tokens = left.shape
        term = mm(
            left[...].reshape(groups * rows, tokens), right[...], ((1,), (1 if turned else 0,))
        )
        total = term if total is None else total + term
    total = total.reshape(groups, rows, total.shape[-1])
    refs = refs[2 * pairs :]
    arrived = refs[:count]
    for piece in arrived:
        total = total + piece[...].astype(f32)
    if not pieces:
        refs[-1][...] = total.astype(bf16)
        return
    outs, sum_ref = refs[-1 - groups : -1], refs[-1]
    sum_ref[...] = total
    group = place_ref[1]
    for by, out in enumerate(outs):
        out[...] = sum_ref[lax.rem(group + by, groups)].astype(out.dtype)


def gradient_call(left, right, which, turned, arrived, pieces, inside=None):
    groups, chips, rows, tokens = left[0].shape
    group = lax.axis_index("fsdp")
    columns = right[0].shape[0 if turned else 1]
    block = next((b for b in (768, 512, 384) if columns % b == 0), columns)
    if rows % 16 or columns % block:
        total = None
        for a, b in zip(left, right):
            picked = lax.dynamic_index_in_dim(a, which, 1, keepdims=False)
            term = mm(picked.reshape(groups * rows, -1), b, ((1,), (1 if turned else 0,)))
            total = term if total is None else total + term
        total = sum((piece.astype(f32) for piece in arrived), total.reshape(groups, rows, -1))
        if not pieces:
            return total.astype(bf16)
        parts = [
            lax.dynamic_index_in_dim(total, (group + by) % groups, 0, keepdims=False)
            for by in range(groups)
        ]
        return [parts[0]] + [p.astype(bf16) for p in parts[1:]]
    left_spec = pl.BlockSpec((groups, 1, rows, tokens), lambda n, place: (0, place[0], 0, 0))
    if turned:
        right_spec = pl.BlockSpec((block, tokens), lambda n, _: (n, 0))
    else:
        right_spec = pl.BlockSpec((tokens, block), lambda n, _: (0, n))
    sum_spec = pl.BlockSpec((groups, rows, block), lambda n, _: (0, 0, n))
    operands = [v for pair in zip(left, right) for v in pair] + list(arrived)
    if pieces:
        out_specs = [pl.BlockSpec((rows, block), lambda n, _: (0, n))] * groups
        out_shape = [
            jax.ShapeDtypeStruct((rows, columns), bf16 if by else f32) for by in range(groups)
        ]
        scratch = [pltpu.VMEM((groups, rows, block), f32)]
    else:
        first, total, whole = inside or (0, columns, ())
        out_specs, scratch = pl.BlockSpec((groups, rows, block), lambda n, _: (0, 0, first // block + n)), []
        out_shape = jax.ShapeDtypeStruct((groups, rows, total), bf16)
        operands += whole
    return pl.pallas_call(
        functools.partial(gradient_kernel, len(left), len(arrived), turned, pieces),
        grid_spec=pltpu.PrefetchScalarGridSpec(
            num_scalar_prefetch=1,
            grid=(columns // block,),
            in_specs=[left_spec, right_spec] * len(left)
            + [sum_spec] * len(arrived)
            + [pl.BlockSpec(memory_space=pl.ANY)] * (len(operands) - 2 * len(left) - len(arrived)),
            out_specs=out_specs,
            scratch_shapes=scratch,
        ),
        out_shape=out_shape,
        input_output_aliases={len(operands): 0} if inside and inside[2] else {},
        compiler_params=pltpu.CompilerParams(vmem_limit_bytes=40 << 20),
        cost_estimate=SMALL_COST,
        name="gradient_chip" if arrived else "gradient_send",
    )(jnp.stack([which, group]), *operands)


def gradient_products(left, right, turned=False):
    chips, chip = lax.axis_size("ctx") // 2, lax.axis_index("ctx") // 2
    return [
        gradient_call(left, right, (chip + by) % chips, turned, (), False)
        for by in range(1, chips)
    ]


def gradient_send(products):
    return [chip_shift(p, by) for by, p in enumerate(products, 1)]


def gradient_chip(left, right, arrived, turned=False, pieces=False):
    return gradient_call(left, right, lax.axis_index("ctx") // 2, turned, arrived, pieces)


def gradient_groups(pieces):
    return [group_shift(piece, by) if by else piece for by, piece in enumerate(pieces)]


def gradient_scatter(total):
    groups, rows, columns = total.shape
    return lax.psum_scatter(
        total.reshape(groups * rows, columns), "fsdp", scatter_dimension=0, tiled=True
    )


def gradient_sum(terms):
    total = terms[0].astype(f32)
    for term in terms[1:]:
        total = total + term.astype(f32)
    return total


def gain_gradient(weights, gradients, gain):
    total = 0.0
    for weight, gradient in zip(weights, gradients):
        total = total + jnp.sum(weight.astype(f32) * gradient.astype(f32), axis=1)
    return total / gain


def slot_meta(ctx_index, tokens, stripe_row, lengths):
    count = stripe_row.shape[0]
    ends = jnp.cumsum(lengths)
    residue = jnp.sum(jnp.where(jnp.arange(count) == ctx_index, stripe_row, 0))
    packed = jnp.arange(tokens, dtype=jnp.int32) * count + residue
    passed = (packed[:, None] >= ends[None, :]).astype(jnp.int32)
    start = jnp.sum(passed * lengths[None, :], axis=1)
    return packed, start


def rms_normed(values, gain):
    scale_row = lax.rsqrt(jnp.mean(values * values, axis=-1, keepdims=True) + norm_eps)
    return (values * scale_row * gain, scale_row)


def norm_back(grad_normed, values, scale_row, gain):
    unit_rows = values * scale_row
    weighted = grad_normed * gain
    return scale_row * (weighted - unit_rows * jnp.mean(weighted * unit_rows, axis=-1, keepdims=True))


def on_device(
    hidden_in,
    cotangent,
    doc_lengths,
    stripe,
    query_key_value_weight,
    output_weight,
    feedforward_weight,
    gains,
):
    ctx_count, ctx_index = lax.axis_size("ctx"), lax.axis_index("ctx")
    group_count, group = lax.axis_size("fsdp"), lax.axis_index("fsdp")
    core = ctx_index % 2
    tokens, width = hidden_in.shape[1:]
    qkv_columns = query_key_value_weight.shape[1]
    att_columns = output_weight.shape[1]
    units = feedforward_weight.shape[2]
    kv_heads = qkv_columns // ((QUERY_PER_KV + 2) * HEAD_SIZE)

    def share(weight):
        rows = weight.shape[0] // ctx_count
        return lax.dynamic_slice_in_dim(weight, ctx_index * rows, rows, 0)

    tp_index = lax.axis_index("tp")
    out_share = share(output_weight)
    out_other = tp_swap(out_share)
    payload = packed_share(feedforward_weight, out_share, out_other, ctx_index, share)
    wq, gain_rows, fetched = gathered_rows(query_key_value_weight, gains, payload)
    payload = lax.optimization_barrier((payload, fetched[0]))[0]
    others = lax.all_gather(payload, ("fsdp", "ctx"), axis=0, tiled=True)

    lengths, stripe_row = doc_lengths[0], stripe[0]
    packed, start = slot_meta(ctx_index, tokens, stripe_row, lengths)
    frequency = rope_base ** (-(2.0 * jnp.arange(HALF, dtype=f32)) / HEAD_SIZE)
    angles = frequency[:, None] * (packed - start).astype(f32)[None, :]
    cos_table, sin_table = jnp.cos(angles), jnp.sin(angles)
    block_starts = start[::BLOCK] // (ctx_count * BLOCK)
    sources = []
    for by in range(ctx_count // 2):
        source = (ctx_index - 2 * by) % ctx_count
        sources += [source, source ^ 1]
    stripes = jnp.stack(
        [lax.dynamic_index_in_dim(stripe_row, s, 0, keepdims=False) for s in sources]
    )
    meta = (block_starts, stripes, packed[None, :], start[None, :])

    order = Order(lengths[0] > 0)
    touch = lambda *v: v
    x, grad_low = hidden_in[0], cotangent[0]
    rows_dy = order(rows_for_cores, grad_low, core)

    def first_norm(x, gain):
        values = x.astype(f32)
        scale = lax.rsqrt(jnp.mean(values * values, axis=-1, keepdims=True) + norm_eps)
        return (values * scale * gain).astype(bf16), scale

    first_normed, scale_one = order(first_norm, x, gain_rows[0])
    rows_one = order(rows_for_cores, first_normed, core)
    first_normed, tables, *meta = lax.optimization_barrier(
        (first_normed, (cos_table, sin_table), *meta)
    )
    sizes = (kv_heads // 2, kv_heads - kv_heads // 2)
    chunks = range(len(sizes))
    queries, own, moving, pieces, attended, lse = [], [], [], [], [], []
    for c in chunks:
        query, kv_own = order(
            functools.partial(project, first=sum(sizes[:c]), heads=sizes[c]),
            first_normed,
            wq,
            *tables,
        )
        queries.append(query)
        own.append(kv_own)
        moving.append([chip_shift(kv_own, by) for by in range(1, ctx_count // 2)])
    own_swapped = order.apart(swapped_of, *own)
    other_dy, other_one = order.apart(swapped_of, rows_dy[1], rows_one[1])
    left_dy, left_one = (rows_dy[0], other_dy), (rows_one[0], other_one)

    def attend(query, mine, partners, arrived, *meta):
        pieces = [mine, partners]
        for piece in arrived:
            pieces += [piece, core_swap(piece)]
        return attention_forward(query, pieces, *meta), pieces[3::2]

    attended_others = []
    for c in chunks:
        (att, lse_c), swapped = order.apart(
            attend, queries[c], own[c], own_swapped[c], moving[c], *meta
        )
        both = [v for pair in zip(moving[c], swapped) for v in pair]
        pieces.append([own[c], own_swapped[c], *both])
        attended.append(att)
        lse.append(lse_c)
        attended_others.append(tp_swap(att.reshape(-1, tokens)))
    attended_rows = [a.reshape(-1, tokens) for a in attended]
    attended_others[0] = order(lambda v: v, attended_others[0])
    all_attended, other_attended = order.apart(
        lambda *parts: (jnp.concatenate(parts, axis=0), core_swap(jnp.concatenate(parts, axis=0))),
        *attended_rows,
    )
    right_att = (all_attended, other_attended)
    middle, second_normed = order(
        functools.partial(middle_of, first=3 * units),
        attended_rows,
        attended_others,
        tp_index,
        x,
        gain_rows[1:],
        others,
    )

    turned_products = functools.partial(gradient_products, turned=True)
    activated, d_gate, d_up, d_two_part = order(
        functools.partial(feed_forward, units=units), second_normed, grad_low, others
    )
    d_two_sent = tp_send(d_two_part)

    def down_part(activated, normed, left_dy, core):
        inner = Order()
        other = core_swap(activated)
        rows = inner(rows_for_cores, normed, core)
        rows_other = core_swap(rows[1])
        return inner(gradient_products, left_dy, (activated, other)), other, (rows[0], rows_other)

    down_products, other_act, left_two = order.apart(
        down_part, activated, second_normed, left_dy, core
    )
    right_act = (activated, other_act)
    down_arrived = gradient_send(down_products)

    def gate_part(activated, d_gate, d_up, left_two, others):
        inner = Order()
        other_gate = core_swap(d_gate)
        down_sum = inner(functools.partial(down_project, first=2 * units), activated, others)
        gate_products = inner(gradient_products, left_two, (d_gate, other_gate))
        other_up = core_swap(lax.optimization_barrier((d_up, down_sum))[0])
        up_products = inner(gradient_products, left_two, (d_up, other_up))
        early = units // 16 * 5
        up_products = [[p[:, :, :early] for p in up_products], [p[:, :, early:] for p in up_products]]
        return gate_products, up_products, down_sum, other_gate, other_up

    gate_products, up_products, down_sum, other_gate, other_up = order.apart(
        gate_part, activated, d_gate, d_up, left_two, others
    )
    right_gate, right_up = (d_gate, other_gate), (d_up, other_up)
    shares = order(
        lambda ffn, qkv: [share(ffn[0]), share(ffn[1]), share(qkv)],
        feedforward_weight,
        query_key_value_weight,
    )
    down_arrived, gate_products, up_products, down_sum, d_two_sent = order(
        touch, down_arrived, gate_products, up_products, down_sum, d_two_sent
    )
    gate_arrived, up_first = gradient_send(gate_products), gradient_send(up_products[0])
    down_scattered = gradient_scatter(order(gradient_chip, left_dy, right_act, down_arrived))
    down_sent = tp_send(down_sum)
    d_branch, d_att = order(
        functools.partial(
            d_middle_of, first=3 * units, parts=[s * QUERY_PER_KV * HEAD_SIZE for s in sizes]
        ),
        d_two_sent,
        middle,
        grad_low,
        gain_rows[1:],
        others,
    )
    d_att = [d.reshape(-1, QUERY_PER_KV, HEAD_SIZE, tokens) for d in d_att]

    def attend_back(query, d_att, attended, lse, pieces, *meta):
        d_query, *d_pieces = attention_backward(query, d_att, attended, lse, pieces, *meta)
        sums = [
            (mine.astype(f32) + core_swap(partners).astype(f32)).astype(bf16)
            for mine, partners in zip(d_pieces[::2], d_pieces[1::2])
        ]
        return d_query, sums

    def attention_step(c):
        d_query, sums = order.apart(
            attend_back, queries[c], d_att[c], attended[c], lse[c], pieces[c], *meta
        )
        return d_query, [chip_shift(s, -by) if by else s for by, s in enumerate(sums)]

    d_query_0, d_kv_0 = attention_step(0)
    gate_arrived, up_products = order(touch, gate_arrived, up_products)
    up_second = gradient_send(up_products[1])
    gate_chip = order(gradient_chip, left_two, right_gate, gate_arrived)
    gate_chip, up_first = order(touch, gate_chip, up_first)
    gate_scattered = gradient_scatter(gate_chip)
    d_query_1, d_kv_1 = attention_step(1)

    def branch_part(d_branch, core, right_att):
        inner = Order()
        rows = inner(rows_for_cores, d_branch, core)
        left = (rows[0], core_swap(rows[1]))
        return inner(turned_products, left, right_att), left

    out_products, left_branch = order.apart(branch_part, d_branch, core, right_att)
    up_first, up_second = order(touch, up_first, up_second)
    up_arrived = [jnp.concatenate(pair, axis=2) for pair in zip(up_first, up_second)]
    up_chip = order(gradient_chip, left_two, right_up, up_arrived)
    d_kv_0, d_kv_1, down_sent, up_chip = order(touch, d_kv_0, d_kv_1, down_sent, up_chip)
    up_scattered = gradient_scatter(up_chip)

    def project_back(out_products, d_query, d_kv, wq, *tables):
        inner = Order()
        out_arrived = gradient_send(out_products)
        parts = [inner(turned_back, q, kv, *tables) for q, kv in zip(d_query, d_kv)]
        return inner(d_one_of, parts, wq), parts, out_arrived

    d_one_part, d_proj, out_arrived = order.apart(
        project_back, out_products, [d_query_0, d_query_1], [d_kv_0, d_kv_1], wq, *tables
    )
    d_one_sent = tp_send(d_one_part)

    grad_down = order(lambda v: v.astype(f32), down_scattered)
    gate_scattered = order(touch, gate_scattered)[0]

    def tail(left_one, d_proj, left_branch, right_att, out_arrived, middle, down_sent):
        inner = Order()
        finish = functools.partial(gradient_chip, turned=True, pieces=True)
        other_proj = [core_swap(p) for p in d_proj]
        chip = inner(finish, left_branch, right_att, out_arrived)
        right_proj = list(zip(d_proj, inner(touch, *other_proj)))
        products = inner(turned_products, left_one, right_proj[0])
        arrived = gradient_send(products)
        terms = gradient_groups(lax.optimization_barrier((chip, products))[0])
        products = inner(turned_products, left_one, right_proj[1])
        hidden_out = inner(lambda m, s: (m + tp_add(s)).astype(bf16), middle, down_sent)
        grad_out = inner(gradient_sum, terms)
        arrived_1 = gradient_send(lax.optimization_barrier((products, grad_out))[0])
        terms = gradient_groups(inner(finish, left_one, right_proj[0], arrived))
        chip = inner(finish, left_one, right_proj[1], arrived_1)
        return grad_out, hidden_out, inner(gradient_sum, terms), chip

    grad_out, hidden_out, grad_qkv_0, chip = order.apart(
        tail, left_one, d_proj, left_branch, right_att, out_arrived, middle, down_sent
    )
    terms = gradient_groups(chip)
    own_gains = lax.dynamic_slice_in_dim(
        gains, ctx_index * out_share.shape[0], out_share.shape[0], 1
    ).astype(f32)

    def ffn_gradient(down, gate, up):
        gain = gain_gradient(shares[:2], [gate, up], own_gains[1])
        return jnp.stack([gate.astype(f32), up.astype(f32), down], axis=0), gain

    grad_ffn, gain_two = order(ffn_gradient, grad_down, gate_scattered, up_scattered)
    grad_in = order(input_gradient, d_one_sent, x, d_branch, gain_rows[:1])

    def qkv_gradient(first, terms, gain_two):
        whole = jnp.concatenate([first, gradient_sum(terms)], axis=1)
        gain_one = gain_gradient(shares[2:], [whole], own_gains[0])
        return jnp.stack([gain_one, gain_two], axis=0), whole

    grad_gains, grad_qkv = order(qkv_gradient, grad_qkv_0, terms, gain_two)
    grad_gains = grad_gains + tp_swap(grad_gains)
    return (hidden_out[None], grad_in[None], grad_qkv, grad_out, grad_ffn, grad_gains)


def solution(mesh):
    return jax.shard_map(
        on_device,
        mesh=mesh,
        in_specs=(
            P("fsdp", "ctx", None),
            P("fsdp", "ctx", None),
            P("fsdp", None),
            P("fsdp", None),
            P("fsdp", "tp"),
            P("fsdp", "tp"),
            P(None, "fsdp", "tp"),
            P(None, "fsdp"),
        ),
        out_specs=(
            P("fsdp", "ctx", None),
            P("fsdp", "ctx", None),
            P(("fsdp", "ctx"), "tp"),
            P(("fsdp", "ctx"), "tp"),
            P(None, ("fsdp", "ctx"), "tp"),
            P(None, ("fsdp", "ctx")),
        ),
        check_vma=False,
    )
```
